32 devices in a mesh: rows: 4 (over z), wide: 8 (over y, x, core).
Axes of the slice: x: 2, y: 2, z: 4, core: 2. Of those that a mesh axis runs over, the one named last changes fastest.
Arguments:
- tokens: bfloat16 [4, 1536, 2048], P('rows', 'wide'), may hold values from -6 to 6
- segments: int32 [4, 1536], P('rows', 'wide'), may hold values from 0 to 6, as said below
- w_qkv: bfloat16 [2048, 6144], P(('rows', 'wide')), may hold values from -0.125 to 0.125
- b_qkv: bfloat16 [6144], P(('rows', 'wide')), may hold values from -4 to 4
- w_out: bfloat16 [2048, 2048], P(('rows', 'wide')), may hold values from -0.75 to 0.75
- ln1_gain: bfloat16 [2048], P(('rows', 'wide')), may hold values from 0.5 to 1.5
- ln1_bias: bfloat16 [2048], P(('rows', 'wide')), may hold values from -4 to 4
- ln2_gain: bfloat16 [2048], P(('rows', 'wide')), may hold values from 0.5 to 1.5
- ln2_bias: bfloat16 [2048], P(('rows', 'wide')), may hold values from -4 to 4
- w_gate: bfloat16 [2048, 5632], P('rows', 'wide'), may hold values from -0.125 to 0.125
- w_up: bfloat16 [2048, 5632], P('rows', 'wide'), may hold values from -0.125 to 0.125
- w_down: bfloat16 [2048, 5632], P('rows', 'wide'), may hold values from -0.078125 to 0.078125
- out_grad: bfloat16 [4, 1536, 2048], P('rows', 'wide'), may hold values from -6 to 6
Outputs:
- mixed: bfloat16 [4, 1536, 2048], P('rows', 'wide')
- grad_tokens: float32 [4, 1536, 2048], P('rows', 'wide')
- grad_w_qkv: float32 [2048, 6144], P(('rows', 'wide'))
- grad_b_qkv: float32 [6144], P(('rows', 'wide'))
- grad_w_out: float32 [2048, 2048], P(('rows', 'wide'))
- grad_ln1_gain: float32 [2048], P(('rows', 'wide'))
- grad_ln1_bias: float32 [2048], P(('rows', 'wide'))
- grad_ln2_gain: float32 [2048], P(('rows', 'wide'))
- grad_ln2_bias: float32 [2048], P(('rows', 'wide'))
- grad_w_gate: float32 [2048, 5632], P('rows', 'wide')
- grad_w_up: float32 [2048, 5632], P('rows', 'wide')
- grad_w_down: float32 [2048, 5632], P('rows', 'wide')
The draws below stay inside these ranges and needn't reach their ends.
Inputs may be any that keep to these rules, and one draw needn't show every extreme that they name: `segments`: each row holds documents 0 to 6 in order, none empty; documents 0 to 2 end within the row's first 192 tokens and document 6 starts within its last 192, so document 3 runs from the first device of wide to the last.
All inputs are finite; a program needn't handle non-finite values.
Results may differ from the reference program's by a relative error of at most 0.015.
Values may be sent and summed in bfloat16 or wider, within the bound.
No kernel may reach another device: no remote copies, remote signals or barrier semaphores. Data moves between devices by JAX's collectives and lax.ppermute only.
A program may use at most 320 MiB of HBM per device.

```python
import math
import jax
import jax.numpy as jnp
from jax import lax

D = 2048
HEADS = 32
HEAD_DIM = 64
ROT = 16
FF = 5632
TOK_DEV = 192
LEN = 1536
ROWS = 4


def choose_cuts(one_key):
    return jnp.sort(jax.random.permutation(one_key, TOK_DEV - 1)[:3]) + 1


def draw_segments(key, part):
    key = jax.random.fold_in(key, 7)
    head_keys = jax.random.split(jax.random.fold_in(key, 1), ROWS)
    tail_keys = jax.random.split(jax.random.fold_in(key, 2), ROWS)
    head_cuts = jax.vmap(choose_cuts)(head_keys)
    tail_cuts = jax.vmap(choose_cuts)(tail_keys) + (LEN - TOK_DEV)
    bounds = jnp.concatenate([head_cuts, tail_cuts], axis=1).astype(jnp.int32)
    places = jnp.arange(LEN, dtype=jnp.int32)
    return jnp.sum((places[None, :, None] >= bounds[:, None, :]).astype(jnp.int32), axis=2)


def level_of(stream_key, dims, cuts, low, high):
    level, own = 1.0, jax.random.fold_in(stream_key, 6)
    for axis_at, parts in cuts:
        heights = jnp.exp(jax.random.uniform(jax.random.fold_in(own, axis_at), (parts,), jnp.float32, low / len(cuts), high / len(cuts)))
        level = level * jnp.repeat(heights, dims[axis_at] // parts).reshape([-1 if axis == axis_at else 1 for axis in range(len(dims))])
    return level


def bell_draw(stream_key, shape, scale, limit, shards=(), kind=jnp.bfloat16):
    entries = jax.random.normal(stream_key, shape, jnp.float32) * scale
    if len(shards) > 0:
        entries = level_of(stream_key, shape, shards, -0.22, 0.18) * entries
    return jnp.clip(entries, min=-limit, max=limit).astype(kind)


def setup_inputs(seed: int = 0) -> dict:
    arg_keys = jax.random.split(jax.random.key(seed), 14)
    return {
        "tokens": bell_draw(arg_keys[0], (ROWS, LEN, D), 1.0, 6.0, ((0, 4), (1, 8))),
        "segments": draw_segments(jax.random.fold_in(arg_keys[13], 71), 0),
        "w_qkv": bell_draw(arg_keys[2], (D, 3 * D), D ** -0.5, 0.125, ((0, 32),)),
        "b_qkv": bell_draw(arg_keys[3], (3 * D,), 0.3, 4.0, ((0, 32),)),
        "w_out": bell_draw(arg_keys[4], (D, D), (D // 32) ** -0.5, 0.75, ((0, 32),)),
        "ln1_gain": jnp.clip(1.0 + 0.1 * jax.random.normal(arg_keys[5], (D,), jnp.float32), 0.5, 1.5).astype(jnp.bfloat16),
        "ln1_bias": bell_draw(arg_keys[6], (D,), 0.3, 4.0, ((0, 32),)),
        "ln2_gain": jnp.clip(1.0 + 0.1 * jax.random.normal(arg_keys[7], (D,), jnp.float32), 0.5, 1.5).astype(jnp.bfloat16),
        "ln2_bias": bell_draw(arg_keys[8], (D,), 0.3, 4.0, ((0, 32),)),
        "w_gate": bell_draw(arg_keys[9], (D, FF), D ** -0.5, 0.125, ((0, 4), (1, 8))),
        "w_up": bell_draw(arg_keys[10], (D, FF), D ** -0.5, 0.125, ((0, 4), (1, 8))),
        "w_down": bell_draw(arg_keys[11], (D, FF), FF ** -0.5, 0.078125, ((0, 4), (1, 8))),
        "out_grad": bell_draw(arg_keys[12], (ROWS, LEN, D), 1.0, 6.0, ((0, 4), (1, 8))),
    }


epsilon = 1e-05
highest = lax.Precision.HIGHEST

@jax.custom_vjp
def low(v):
    return lax.optimization_barrier(v.astype(jnp.bfloat16)).astype(jnp.float32)

@jax.custom_vjp
def low_back(v):
    return v

def low_keep(v):
    return (low(v), None)

def low_pass(kept, grad):
    return (grad,)

def back_keep(v):
    return (v, None)

def back_low(kept, grad):
    return (low(grad),)
low.defvjp(low_keep, low_pass)
low_back.defvjp(back_keep, back_low)

def layer_norm(values, gain, shift):
    centre = lax.optimization_barrier(jnp.mean(values, axis=-1, keepdims=True))
    centred = values - centre
    spread = lax.optimization_barrier(jnp.mean(centred * centred, axis=-1, keepdims=True))
    return centred * lax.rsqrt(spread + epsilon) * gain + shift

def rotary(values, places):
    half_rot = ROT // 2
    freqs = 10000.0 ** (-2.0 * jnp.arange(half_rot, dtype=jnp.float32) / ROT)
    angles = places.astype(jnp.float32)[:, None] * freqs[None, :]
    cosine = jnp.cos(angles)[:, None, :]
    sine = jnp.sin(angles)[:, None, :]
    first_half = values[..., :half_rot]
    second_half = values[..., half_rot:ROT]
    remainder = values[..., ROT:]
    return jnp.concatenate([first_half * cosine - second_half * sine, second_half * cosine + first_half * sine, remainder], axis=-1)

def layer_row(inputs, segs, w_qkv, b_qkv, w_out, gain_one, shift_one, gain_two, shift_two, w_gate, w_up, w_down):
    row_len = inputs.shape[0]
    model_width = inputs.shape[1]
    places = jnp.arange(row_len, dtype=jnp.int32)
    doc_first = lax.optimization_barrier(jnp.sum((segs[None, :] < segs[:, None]).astype(jnp.int32), axis=1))
    positions = places - doc_first
    act_one = low(layer_norm(inputs, gain_one, shift_one))
    projected = low_back(jnp.dot(act_one, w_qkv, precision=highest) + b_qkv)
    queries = projected[:, :model_width].reshape(row_len, HEADS, HEAD_DIM)
    keys_raw = projected[:, model_width:2 * model_width].reshape(row_len, HEADS, HEAD_DIM)
    values_raw = projected[:, 2 * model_width:].reshape(row_len, HEADS, HEAD_DIM)
    query_low = low(rotary(queries, positions))
    key_low = low(rotary(keys_raw, positions))
    value_low = low(values_raw)
    block_rows = math.gcd(row_len, 512)
    blocks = row_len // block_rows
    score_scale = HEAD_DIM ** (-0.5)

    def attend(pieces):
        query_block, place_block, seg_block = pieces
        scores = low_back(jnp.einsum('qhd,khd->hqk', query_block, key_low, precision=highest) * score_scale)
        visible = (seg_block[:, None] == segs[None, :]) & (places[None, :] <= place_block[:, None])
        attn_probs = jax.nn.softmax(jnp.where(visible[None], scores, -1e+30), axis=-1)
        return jnp.einsum('hqk,khd->qhd', low(attn_probs), value_low, precision=highest)
    attended = lax.map(jax.checkpoint(attend), (query_low.reshape(blocks, block_rows, HEADS, HEAD_DIM), places.reshape(blocks, block_rows), segs.reshape(blocks, block_rows)))
    attn_low = low(low_back(attended.reshape(row_len, model_width)))
    middle = inputs + low_back(jnp.dot(attn_low, w_out, precision=highest))
    act_two = low(layer_norm(middle, gain_two, shift_two))
    gate = low_back(jnp.dot(act_two, w_gate, precision=highest))
    upper = low_back(jnp.dot(act_two, w_up, precision=highest))
    hidden = low(jax.nn.silu(gate) * upper)
    mixed = low_back(jnp.dot(hidden, w_down.T, precision=highest))
    return middle + mixed

def reference(tokens, segments, w_qkv, b_qkv, w_out, ln1_gain, ln1_bias, ln2_gain, ln2_bias, w_gate, w_up, w_down, out_grad):
    params = tuple((member.astype(jnp.float32) for member in (w_qkv, b_qkv, w_out, ln1_gain, ln1_bias, ln2_gain, ln2_bias, w_gate, w_up, w_down)))

    def one_row(totals, pieces):
        row_tokens, row_segs, row_grad = pieces

        def forward(row_in, *weights):
            return layer_row(row_in, row_segs, *weights)
        result, pullback = jax.vjp(forward, row_tokens, *params)
        grads = pullback(row_grad)
        totals = jax.tree.map(jnp.add, totals, tuple(grads[1:]))
        return (totals, (result.astype(jnp.bfloat16), grads[0]))
    zeros = jax.tree.map(jnp.zeros_like, params)
    totals, outputs = lax.scan(one_row, zeros, (tokens.astype(jnp.float32), segments, out_grad.astype(jnp.float32)))
    return (outputs[0], outputs[1], totals[0], totals[1], totals[2], totals[3], totals[4], totals[5], totals[6], totals[7], totals[8], totals[9])
```

```python
import functools
import math

import jax
import jax.numpy as jnp
from jax import lax
from jax.experimental import pallas as pl
from jax.experimental.pallas import tpu as pltpu
from jax.sharding import PartitionSpec as P

HEADS = 32
HEAD_DIM = 64
ROT = 16
PAIR = 2 * HEAD_DIM

epsilon = 1e-05
neg_large = -1e30
BF = jnp.bfloat16
F32 = jnp.float32
ALL = ("rows", "wide")
NT = (((1,), (1,)), ((), ()))
TN = (((0,), (0,)), ((), ()))


def dot(left, right, dims=(((1,), (0,)), ((), ()))):
    return lax.dot_general(left, right, dims, preferred_element_type=F32)


def swap(x, bit, axis="wide"):
    return lax.ppermute(x, axis, [(i, i ^ bit) for i in range(lax.axis_size(axis))])


def upper_bits():
    return [1 << k for k in range(1, lax.axis_size("wide").bit_length() - 1)]


def gather_plane(x):
    bits = upper_bits()
    if len(bits) == 2:
        half = x.shape[0] // 2
        one, two = bits
        top, low = x[:half], x[half:]
        top_two, low_one = swap(top, two), swap(low, one)
        low_two, top_one = swap(low, two), swap(top, one)
        top_both, low_both = swap(top_two, one), swap(low_one, two)
        own = jnp.concatenate(
            [top, low, top_one, low_one, top_two, low_two, top_both, low_both]
        )
    else:
        own = x
        for bit in bits:
            own = jnp.concatenate([own, swap(own, bit)])
    return own, swap(own, 1)


def add_low(left, right):
    return (left.astype(F32) + right.astype(F32)).astype(BF)


def scatter_plane(own, other):
    bits = upper_bits()
    got = swap(other, 1)
    total = add_low(own, got)
    if len(bits) == 2:
        one, two = bits
        half = total.shape[0] // 8

        def part(m, h):
            return total[(2 * m + h) * half : (2 * m + h + 1) * half]

        far_top, far_low = swap(part(3, 0), one), swap(part(3, 1), two)
        top_one, low_two = swap(part(1, 0), one), swap(part(2, 1), two)
        top_two = swap(add_low(part(2, 0), far_top), two)
        low_one = swap(add_low(part(1, 1), far_low), one)
        return jnp.concatenate(
            [
                part(0, 0).astype(F32) + top_one.astype(F32) + top_two.astype(F32),
                part(0, 1).astype(F32) + low_one.astype(F32) + low_two.astype(F32),
            ]
        )
    for bit in reversed(bits[1:]):
        half = total.shape[0] // 2
        total = add_low(total[:half], swap(total[half:], bit))
    half = total.shape[0] // 2
    return total[:half].astype(F32) + swap(total[half:], bits[0]).astype(F32)


def to_relative(x):
    count = lax.axis_size("wide")
    me = lax.axis_index("wide")
    blocks = x.reshape(count, x.shape[0] // count, x.shape[1])

    def pick(first):
        return jnp.concatenate(
            [
                lax.dynamic_index_in_dim(blocks, me ^ m, 0, keepdims=False)
                for m in range(first, count, 2)
            ]
        )

    return pick(0), pick(1)


def to_absolute(own, other):
    count = lax.axis_size("wide")
    me = lax.axis_index("wide")
    half = count // 2
    blocks = jnp.concatenate([own, other]).reshape(count, -1, own.shape[1])
    pieces = []
    for place in range(count):
        m = me ^ place
        pieces.append(
            lax.dynamic_index_in_dim(blocks, (m & 1) * half + (m >> 1), 0, keepdims=False)
        )
    return jnp.concatenate(pieces)


def scatter_small(x):
    count_rows, count_wide = lax.axis_size("rows"), lax.axis_size("wide")
    me_rows, me_wide = lax.axis_index("rows"), lax.axis_index("wide")
    width = x.shape[1]
    x = x.reshape(count_rows, count_wide * width)
    size = count_rows // 2
    while size >= 1:
        side = (me_rows // size) % 2
        halves = x.reshape(2, -1, x.shape[1])
        keep = lax.dynamic_index_in_dim(halves, side, 0, keepdims=False)
        give = lax.dynamic_index_in_dim(halves, 1 - side, 0, keepdims=False)
        x = keep + swap(give, size, "rows")
        size //= 2
    x = x.reshape(count_wide, width)
    size = count_wide // 2
    while size >= 1:
        side = (me_wide // size) % 2
        halves = x.reshape(2, -1, x.shape[1])
        keep = lax.dynamic_index_in_dim(halves, side, 0, keepdims=False)
        give = lax.dynamic_index_in_dim(halves, 1 - side, 0, keepdims=False)
        x = keep + swap(give, size, "wide")
        size //= 2
    return x.reshape(width)


def turn_lanes(x, cosine, ahead, behind):
    half_rot = ROT // 2
    lanes = x.shape[-1]
    return (
        x * cosine
        + pltpu.roll(x, lanes - half_rot, 1) * ahead
        + pltpu.roll(x, half_rot, 1) * behind
    )


def project_kernel(
    order, own_ref, other_ref, gain, shift, weight, bias, cosine, ahead, behind, act, q, k, v
):
    count = pl.num_programs(0)
    step = pl.program_id(0)
    width = q.shape[1]

    def work(x_ref):
        x = x_ref[...].astype(F32)
        centred = x - jnp.mean(x, axis=1, keepdims=True)
        spread = jnp.mean(centred * centred, axis=1, keepdims=True)
        normed = (centred * lax.rsqrt(spread + epsilon) * gain[...] + shift[...]).astype(BF)
        act[...] = normed
        projected = dot(normed, weight[...]) + bias[...]
        for at in range(0, width, PAIR):
            angles = (cosine[...], ahead[...], behind[...])
            q[:, at : at + PAIR] = turn_lanes(projected[:, at : at + PAIR], *angles).astype(BF)
            k[:, at : at + PAIR] = turn_lanes(
                projected[:, width + at : width + at + PAIR], *angles
            ).astype(BF)
        v[...] = projected[:, 2 * width :].astype(BF)

    @pl.when(step < count // 2)
    def _():
        work(own_ref)

    @pl.when(step >= count // 2)
    def _():
        work(other_ref)


def project(own, other, gain, shift, weight, bias, tables):
    count = lax.axis_size("wide")
    half = count // 2
    rows = own.shape[0] // half
    depth, columns = weight.shape
    width = columns // 3
    total = rows * count
    me = lax.axis_index("wide")
    order = jnp.stack([me ^ m for m in list(range(0, count, 2)) + list(range(1, count, 2))])

    def whole(i, order):
        return (0, 0)

    def placed(i, order):
        return (order[i], 0)

    vec = pl.BlockSpec((1, depth), whole)
    table = pl.BlockSpec((rows, PAIR), placed)
    out = pl.BlockSpec((rows, width), placed)
    return pl.pallas_call(
        project_kernel,
        grid_spec=pltpu.PrefetchScalarGridSpec(
            num_scalar_prefetch=1,
            grid=(count,),
            in_specs=[
                pl.BlockSpec((rows, depth), lambda i, order: (jnp.minimum(i, half - 1), 0)),
                pl.BlockSpec((rows, depth), lambda i, order: (jnp.maximum(i - half, 0), 0)),
                vec,
                vec,
                pl.BlockSpec((depth, columns), whole),
                pl.BlockSpec((1, columns), whole),
                table,
                table,
                table,
            ],
            out_specs=[pl.BlockSpec((rows, depth), placed), out, out, out],
        ),
        out_shape=[
            jax.ShapeDtypeStruct((total, depth), BF),
            jax.ShapeDtypeStruct((total, width), BF),
            jax.ShapeDtypeStruct((total, width), BF),
            jax.ShapeDtypeStruct((total, width), BF),
        ],
        cost_estimate=pl.CostEstimate(
            flops=2 * total * depth * columns,
            bytes_accessed=2 * (2 * total * depth + total * columns + depth * columns),
            transcendentals=0,
        ),
        compiler_params=pltpu.CompilerParams(
            dimension_semantics=("arbitrary",), vmem_limit_bytes=48 * 2**20
        ),
        name="project",
    )(order, own, other, gain, shift, weight, bias, *tables)


def head_mask(head, shape):
    lane = lax.broadcasted_iota(jnp.int32, shape, 1)
    return (lane // HEAD_DIM) == head


def attend_kernel(first, q_ref, k_ref, v_ref, o_ref, log_ref, v_turned):
    block = q_ref.shape[0]
    at = pl.program_id(1)
    scale = HEAD_DIM ** (-0.5)

    @pl.when(at == 0)
    def _():
        v_turned[...] = v_ref[...].astype(F32).T.astype(BF)

    q = q_ref[...] * jnp.asarray(scale, BF)
    queries = [jnp.where(head_mask(h, q.shape), q, jnp.zeros_like(q)) for h in range(2)]
    own_first = first[...]
    own_place = at * block + lax.broadcasted_iota(jnp.int32, (1, block), 1)

    def step(number, state):
        keys = k_ref[pl.ds(number * block, block), :]
        values = v_turned[:, pl.ds(number * block, block)]
        place = number * block + lax.broadcasted_iota(jnp.int32, (block, block), 0)
        visible = (place >= own_first) & (place <= own_place)
        out = []
        for h in range(2):
            peak, total, mix = state[h]
            scores = jnp.where(visible, dot(keys, queries[h], NT), neg_large)
            new_peak = jnp.maximum(peak, jnp.max(scores, axis=0, keepdims=True))
            terms = jnp.where(visible, jnp.exp(scores - new_peak), 0.0)
            decay = jnp.exp(peak - new_peak)
            out.append(
                (
                    new_peak,
                    total * decay + jnp.sum(terms, axis=0, keepdims=True),
                    mix * decay
                    + dot(values[h * HEAD_DIM : (h + 1) * HEAD_DIM], terms.astype(BF)),
                )
            )
        return tuple(out)

    start = (
        jnp.full((1, block), neg_large, F32),
        jnp.zeros((1, block), F32),
        jnp.zeros((HEAD_DIM, block), F32),
    )
    state = lax.fori_loop(0, at + 1, step, (start, start))
    mixes = []
    for h in range(2):
        peak, total, mix = state[h]
        mixes.append(mix / total)
        log_ref[0, h : h + 1, :] = peak + jnp.log(total)
    o_ref[...] = jnp.concatenate(mixes, axis=0).T.astype(BF)


def attend(first, q, k, v):
    total, width = q.shape
    pairs = width // PAIR
    block = math.gcd(total, 256)
    return pl.pallas_call(
        attend_kernel,
        grid=(pairs, total // block),
        in_specs=[
            pl.BlockSpec((1, block), lambda p, i: (0, i)),
            pl.BlockSpec((block, PAIR), lambda p, i: (i, p)),
            pl.BlockSpec((total, PAIR), lambda p, i: (0, p)),
            pl.BlockSpec((total, PAIR), lambda p, i: (0, p)),
        ],
        out_specs=[
            pl.BlockSpec((block, PAIR), lambda p, i: (i, p)),
            pl.BlockSpec((1, 2, block), lambda p, i: (p, 0, i)),
        ],
        out_shape=[
            jax.ShapeDtypeStruct((total, width), BF),
            jax.ShapeDtypeStruct((pairs, 2, total), F32),
        ],
        scratch_shapes=[pltpu.VMEM((PAIR, total), BF)],
        cost_estimate=pl.CostEstimate(
            flops=8 * total * total * width,
            bytes_accessed=8 * total * width,
            transcendentals=total * total * width // PAIR,
        ),
        compiler_params=pltpu.CompilerParams(
            dimension_semantics=("arbitrary", "arbitrary"), vmem_limit_bytes=32 * 2**20
        ),
        name="attend",
    )(first, q, k, v)


def attend_back_kernel(
    first, q_ref, k_ref, v_ref, o_ref, g_ref, log_ref, cosine, ahead, behind,
    gq_ref, gk_ref, gv_ref, k_turned, delta, sum_q,
):
    total = q_ref.shape[0]
    block = k_ref.shape[0]
    at = pl.program_id(1)
    last = pl.num_programs(1)
    scale = HEAD_DIM ** (-0.5)
    k = k_ref[...]
    k_turned[...] = k.astype(F32).T.astype(BF)

    @pl.when(at == 0)
    def _():
        sum_q[...] = jnp.zeros_like(sum_q)

        def fill(number, carry):
            spot = pl.ds(number * block, block)
            both = (g_ref[spot, :].astype(F32) * o_ref[spot, :].astype(F32)).T
            for h in range(2):
                delta[h : h + 1, spot] = jnp.sum(
                    both[h * HEAD_DIM : (h + 1) * HEAD_DIM], axis=0, keepdims=True
                )
            return carry

        lax.fori_loop(0, last, fill, 0)

    v = v_ref[...]
    place = at * block + lax.broadcasted_iota(jnp.int32, (block, block), 0)

    def step(number, state):
        sum_k, sum_v = state
        spot = pl.ds(number * block, block)
        q = q_ref[spot, :] * jnp.asarray(scale, BF)
        g = g_ref[spot, :]
        own_place = number * block + lax.broadcasted_iota(jnp.int32, (1, block), 1)
        visible = (place >= first[:, spot]) & (place <= own_place)
        for h in range(2):
            mask = head_mask(h, q.shape)
            q_head = jnp.where(mask, q, jnp.zeros_like(q))
            g_head = jnp.where(mask, g, jnp.zeros_like(g))
            scores = dot(k, q_head, NT)
            probs = jnp.where(
                visible,
                jnp.exp(jnp.where(visible, scores - log_ref[0, h : h + 1, spot], neg_large)),
                0.0,
            )
            slopes = dot(v, g_head, NT)
            low = (probs * (slopes - delta[h : h + 1, spot])).astype(BF)
            sum_v = sum_v + dot(probs.astype(BF), g_head)
            sum_k = sum_k + dot(low, q_head)
            span = slice(h * HEAD_DIM, (h + 1) * HEAD_DIM)
            sum_q[span, spot] += dot(k_turned[span, :], low)
        return (sum_k, sum_v)

    zeros = jnp.zeros((block, PAIR), F32)
    sum_k, sum_v = lax.fori_loop(at, last, step, (zeros, zeros))
    gv_ref[...] = sum_v.astype(BF)
    mine = pl.ds(at * block, block)
    gk_ref[...] = turn_lanes(sum_k, cosine[mine, :], -ahead[mine, :], -behind[mine, :]).astype(BF)

    @pl.when(at == last - 1)
    def _():
        def finish(number, carry):
            spot = pl.ds(number * block, block)
            gq_ref[spot, :] = turn_lanes(
                sum_q[:, spot].T * scale, cosine[spot, :], -ahead[spot, :], -behind[spot, :]
            ).astype(BF)
            return carry

        lax.fori_loop(0, last, finish, 0)


def attend_back(first, q, k, v, o, g, logs, tables):
    total, width = q.shape
    pairs = width // PAIR
    block = math.gcd(total, 256)
    whole = pl.BlockSpec((total, PAIR), lambda p, i: (0, p))
    part = pl.BlockSpec((block, PAIR), lambda p, i: (i, p))
    table = pl.BlockSpec((total, PAIR), lambda p, i: (0, 0))
    shape = jax.ShapeDtypeStruct((total, width), BF)
    return pl.pallas_call(
        attend_back_kernel,
        grid=(pairs, total // block),
        in_specs=[
            pl.BlockSpec((1, total), lambda p, i: (0, 0)),
            whole,
            part,
            part,
            whole,
            whole,
            pl.BlockSpec((1, 2, total), lambda p, i: (p, 0, 0)),
            table,
            table,
            table,
        ],
        out_specs=[whole, part, part],
        out_shape=[shape, shape, shape],
        scratch_shapes=[
            pltpu.VMEM((PAIR, block), BF),
            pltpu.VMEM((2, total), F32),
            pltpu.VMEM((PAIR, total), F32),
        ],
        cost_estimate=pl.CostEstimate(
            flops=20 * total * total * width,
            bytes_accessed=16 * total * width,
            transcendentals=total * total * width // PAIR,
        ),
        compiler_params=pltpu.CompilerParams(
            dimension_semantics=("arbitrary", "arbitrary"), vmem_limit_bytes=48 * 2**20
        ),
        name="attend_back",
    )(first, q, k, v, o, g, logs, *tables)


def norm_parts(values):
    centred = values - jnp.mean(values, axis=-1, keepdims=True)
    spread = jnp.mean(centred * centred, axis=-1, keepdims=True)
    rate = lax.rsqrt(spread + epsilon)
    return centred * rate, rate


def norm_back(incoming, unit, rate, gain):
    scaled = incoming * gain
    return (
        rate
        * (
            scaled
            - jnp.mean(scaled, axis=-1, keepdims=True)
            - unit * jnp.mean(scaled * unit, axis=-1, keepdims=True)
        ),
        jnp.sum(incoming * unit, axis=0),
        jnp.sum(incoming, axis=0),
    )


def shards(
    tokens,
    segments,
    w_qkv,
    b_qkv,
    w_out,
    ln1_gain,
    ln1_bias,
    ln2_gain,
    ln2_bias,
    w_gate,
    w_up,
    w_down,
    out_grad,
):
    rows_n, wide_n = lax.axis_size("rows"), lax.axis_size("wide")
    me_row, me = lax.axis_index("rows"), lax.axis_index("wide")
    devices = rows_n * wide_n
    local = tokens.shape[1]
    width = tokens.shape[2]
    row_len = local * wide_n
    per = HEADS // wide_n
    span = per * HEAD_DIM
    slab = width // devices
    bias_slab = 3 * width // devices

    packed = jnp.concatenate(
        [b_qkv, ln1_gain, ln1_bias, ln2_gain, ln2_bias, segments[0].astype(BF)]
    )
    small = lax.all_gather(lax.all_gather(packed, "rows"), "wide")
    flat = small.transpose(1, 0, 2)

    def vector(start, size):
        return flat[:, :, start : start + size].reshape(1, devices * size).astype(F32)

    bias = vector(0, bias_slab)
    gain_one = vector(bias_slab, slab)
    shift_one = vector(bias_slab + slab, slab)
    gain_two = vector(bias_slab + 2 * slab, slab)
    shift_two = vector(bias_slab + 3 * slab, slab)
    row_segs = lax.dynamic_index_in_dim(small, me_row, 1, keepdims=False)[
        :, bias_slab + 4 * slab :
    ].reshape(row_len)
    own_bias = lax.dynamic_index_in_dim(
        bias.reshape(3, per, wide_n, HEAD_DIM), me, 2, keepdims=False
    ).reshape(1, 3 * span)

    doc_first = jnp.sum((row_segs[:, None] < row_segs[None, :]).astype(jnp.int32), axis=0)
    positions = jnp.arange(row_len, dtype=jnp.int32) - doc_first
    freqs = 10000.0 ** (-2.0 * jnp.arange(ROT // 2, dtype=F32) / ROT)
    lane = jnp.arange(PAIR) % HEAD_DIM
    lane_freqs = jnp.where(lane < ROT, jnp.tile(freqs, PAIR // (ROT // 2)), 0.0)
    angles = positions.astype(F32)[:, None] * lane_freqs[None, :]
    sine = jnp.sin(angles)
    half_rot = ROT // 2
    tables = (
        jnp.cos(angles),
        jnp.where(lane < half_rot, -sine, 0.0),
        jnp.where((lane >= half_rot) & (lane < ROT), sine, 0.0),
    )
    first = doc_first.reshape(1, row_len)

    fast_out = slab == HEAD_DIM and per == rows_n
    if fast_out:
        w_out_own = lax.all_gather(w_out, "rows", axis=0, tiled=True)
    else:
        w_out_own = lax.dynamic_index_in_dim(
            lax.all_gather(w_out, ALL, axis=0, tiled=True).reshape(
                per, wide_n, HEAD_DIM, width
            ),
            me,
            1,
            keepdims=False,
        ).reshape(span, width)
    by_head = w_qkv.reshape(slab, 3 * per, wide_n, HEAD_DIM).transpose(2, 0, 1, 3)
    w_qkv_part = lax.all_to_all(
        by_head.reshape(wide_n * slab, 3 * span), "wide", 0, 0, tiled=True
    )
    w_qkv_own = lax.all_gather(w_qkv_part, "rows", axis=0, tiled=True)
    gate_slab, up_slab, down_slab = (
        lax.all_gather(w_gate, "rows", axis=0, tiled=True),
        lax.all_gather(w_up, "rows", axis=0, tiled=True),
        lax.all_gather(w_down, "rows", axis=0, tiled=True),
    )

    own, other = gather_plane(tokens[0])
    act_one, q, k, v = project(
        own, other, gain_one, shift_one, w_qkv_own, own_bias, tables
    )
    attn_low, logs = attend(first, q, k, v)
    attn_own, attn_other = to_relative(attn_low)
    inputs = tokens[0].astype(F32)
    middle = inputs + scatter_plane(
        dot(attn_own, w_out_own).astype(BF), dot(attn_other, w_out_own).astype(BF)
    )
    unit_two, rate_two = norm_parts(middle)
    act_two = (unit_two * gain_two + shift_two).astype(BF)
    row_act = jnp.concatenate(gather_plane(act_two))
    grad_low = out_grad[0]
    row_grad = jnp.concatenate(gather_plane(grad_low))
    middle_row = row_act.shape[0] // 2

    gate = dot(row_act, gate_slab)
    upper = dot(row_act, up_slab)
    sig = jax.nn.sigmoid(gate)
    silu = gate * sig
    hidden = (silu * upper).astype(BF)
    mixed_part = dot(hidden, down_slab, NT).astype(BF)
    mixed = scatter_plane(mixed_part[:middle_row], mixed_part[middle_row:])
    result = (middle + mixed).astype(BF)[None]

    grad_down = dot(row_grad, hidden, TN)
    grad_hidden = dot(row_grad, down_slab)
    grad_gate_low = (grad_hidden * upper * sig * (1.0 + gate * (1.0 - sig))).astype(BF)
    grad_up_low = (grad_hidden * silu).astype(BF)
    grad_gate = dot(row_act, grad_gate_low, TN)
    grad_up = dot(row_act, grad_up_low, TN)
    act_part = (
        dot(grad_gate_low, gate_slab, NT) + dot(grad_up_low, up_slab, NT)
    ).astype(BF)
    grad_act_two = scatter_plane(act_part[:middle_row], act_part[middle_row:])
    grad_norm, grad_gain_two, grad_shift_two = norm_back(
        grad_act_two, unit_two, rate_two, gain_two
    )
    grad_middle = grad_low.astype(F32) + grad_norm
    branch_own, branch_other = gather_plane(grad_middle.astype(BF))
    branch = jnp.concatenate([branch_own, branch_other])
    grad_w_out = dot(jnp.concatenate([attn_own, attn_other]), branch, TN)
    grad_attn = to_absolute(
        dot(branch_own, w_out_own, NT).astype(BF), dot(branch_other, w_out_own, NT).astype(BF)
    )
    grad_q, grad_k, grad_v = attend_back(first, q, k, v, attn_low, grad_attn, logs, tables)
    grad_proj = jnp.concatenate([grad_q, grad_k, grad_v], axis=1)
    grad_w_qkv = dot(act_one, grad_proj, TN)
    grad_bias = jnp.sum(grad_proj, axis=0, dtype=F32)
    proj_own, proj_other = to_relative(grad_proj)
    grad_act_one = scatter_plane(
        dot(proj_own, w_qkv_own, NT).astype(BF), dot(proj_other, w_qkv_own, NT).astype(BF)
    )
    unit_one, rate_one = norm_parts(inputs)
    grad_input, grad_gain_one, grad_shift_one = norm_back(
        grad_act_one, unit_one, rate_one, gain_one
    )
    grad_tokens = (grad_middle + grad_input)[None]

    def sum_rows(x):
        return lax.psum_scatter(x.astype(BF), "rows", scatter_dimension=0, tiled=True)

    out_down = sum_rows(grad_down).astype(F32)
    out_gate = sum_rows(grad_gate).astype(F32)
    out_up = sum_rows(grad_up).astype(F32)
    if fast_out:
        out_w_out = sum_rows(grad_w_out).astype(F32)
    else:
        spread_out = lax.dynamic_update_index_in_dim(
            jnp.zeros((per, wide_n, HEAD_DIM, width), BF),
            grad_w_out.astype(BF).reshape(per, HEAD_DIM, width),
            me,
            1,
        )
        out_w_out = lax.psum_scatter(
            spread_out.reshape(width, width), ALL, scatter_dimension=0, tiled=True
        ).astype(F32)
    part_qkv = lax.all_to_all(sum_rows(grad_w_qkv), "wide", 0, 0, tiled=True)
    out_qkv = (
        part_qkv.reshape(wide_n, slab, 3 * per, HEAD_DIM)
        .transpose(1, 2, 0, 3)
        .reshape(slab, 3 * width)
        .astype(F32)
    )
    full_bias = lax.dynamic_update_index_in_dim(
        jnp.zeros((3, per, wide_n, HEAD_DIM), F32),
        grad_bias.reshape(3, per, HEAD_DIM),
        me,
        2,
    )
    sums = scatter_small(
        jnp.concatenate(
            [
                full_bias.reshape(devices, bias_slab),
                grad_gain_one.reshape(devices, slab),
                grad_shift_one.reshape(devices, slab),
                grad_gain_two.reshape(devices, slab),
                grad_shift_two.reshape(devices, slab),
            ],
            axis=1,
        )
    )
    out_bias = sums[:bias_slab]
    small_outs = [
        sums[bias_slab + i * slab : bias_slab + (i + 1) * slab] for i in range(4)
    ]
    return (
        result,
        grad_tokens,
        out_qkv,
        out_bias,
        out_w_out,
        *small_outs,
        out_gate,
        out_up,
        out_down,
    )


def solution(mesh):
    by_token = P("rows", "wide", None)
    by_both = P(("rows", "wide"), None)
    vector = P(("rows", "wide"))
    by_slab = P("rows", "wide")
    in_specs = (
        by_token, P("rows", "wide"), by_both, vector, by_both, vector, vector, vector, vector,
        by_slab, by_slab, by_slab, by_token,
    )
    out_specs = (
        by_token, by_token, by_both, vector, by_both, vector, vector, vector, vector,
        by_slab, by_slab, by_slab,
    )
    return jax.shard_map(shards, mesh=mesh, in_specs=in_specs, out_specs=out_specs, check_vma=False)
```

```python
import functools
import math

import jax
import jax.numpy as jnp
from jax import lax
from jax.experimental import pallas as pl
from jax.experimental.pallas import tpu as pltpu
from jax.sharding import PartitionSpec as P

HEADS = 32
HEAD_DIM = 64
ROT = 16
PAIR = 2 * HEAD_DIM

epsilon = 1e-05
neg_large = -1e30
BF = jnp.bfloat16
F32 = jnp.float32
ALL = ("rows", "wide")
NT = (((1,), (1,)), ((), ()))
TN = (((0,), (0,)), ((), ()))


def dot(left, right, dims=(((1,), (0,)), ((), ()))):
    return lax.dot_general(left, right, dims, preferred_element_type=F32)


def swap(x, bit, axis="wide"):
    return lax.ppermute(x, axis, [(i, i ^ bit) for i in range(lax.axis_size(axis))])


def upper_bits():
    return [1 << k for k in range(1, lax.axis_size("wide").bit_length() - 1)]


def gather_first(x):
    bits = upper_bits()
    if len(bits) != 2:
        return ()
    one, two = bits
    half = x.shape[0] // 2
    top, low = x[:half], x[half:]
    return swap(top, two), swap(low, one), swap(low, two), swap(top, one)


def gather_second(x, got):
    bits = upper_bits()
    if len(bits) != 2:
        return ()
    one, two = bits
    return swap(got[0], one), swap(got[1], two)


def gather_third(x, got, passed):
    if not got:
        own = x
        for bit in upper_bits():
            own = jnp.concatenate([own, swap(own, bit)])
        return own
    half = x.shape[0] // 2
    top_two, low_one, low_two, top_one = got
    return jnp.concatenate(
        [x[:half], x[half:], top_one, low_one, top_two, low_two, passed[0], passed[1]]
    )


def gather_last(x, got, passed):
    own = gather_third(x, got, passed)
    return own, swap(own, 1)


def gather_own(x):
    got = gather_first(x)
    return gather_third(x, got, gather_second(x, got))


def add_low(left, right):
    return (left.astype(F32) + right.astype(F32)).astype(BF)


def start_scatter(own, other):
    return add_low(lax.optimization_barrier(own), swap(other, 1))


def block_of(total, m, h):
    half = total.shape[0] // 8
    return total[(2 * m + h) * half : (2 * m + h + 1) * half]


def scatter_first(total):
    bits = upper_bits()
    if len(bits) != 2:
        return ()
    one, two = bits
    return (
        swap(block_of(total, 3, 0), one),
        swap(block_of(total, 3, 1), two),
        swap(block_of(total, 1, 0), one),
        swap(block_of(total, 2, 1), two),
    )


def scatter_second(total, got):
    bits = upper_bits()
    if len(bits) != 2:
        return ()
    one, two = bits
    return (
        swap(add_low(block_of(total, 2, 0), got[0]), two),
        swap(add_low(block_of(total, 1, 1), got[1]), one),
    )


def scatter_last(total, got, passed):
    if got:
        return jnp.concatenate(
            [
                block_of(total, 0, h).astype(F32) + got[2 + h].astype(F32) + passed[h].astype(F32)
                for h in range(2)
            ]
        )
    bits = upper_bits()
    for bit in reversed(bits[1:]):
        half = total.shape[0] // 2
        total = add_low(total[:half], swap(total[half:], bit))
    half = total.shape[0] // 2
    return total[:half].astype(F32) + swap(total[half:], bits[0]).astype(F32)


def scatter_plane(total):
    got = scatter_first(total)
    return scatter_last(total, got, scatter_second(total, got))


def after(x, *others):
    return lax.optimization_barrier((x, others))[0]


def to_relative(x):
    count = lax.axis_size("wide")
    me = lax.axis_index("wide")
    blocks = x.reshape(count, x.shape[0] // count, x.shape[1])

    def pick(first):
        return jnp.concatenate(
            [
                lax.dynamic_index_in_dim(blocks, me ^ m, 0, keepdims=False)
                for m in range(first, count, 2)
            ]
        )

    return pick(0), pick(1)


def to_absolute(own, other):
    count = lax.axis_size("wide")
    me = lax.axis_index("wide")
    half = count // 2
    blocks = jnp.concatenate([own, other]).reshape(count, -1, own.shape[1])
    pieces = []
    for place in range(count):
        m = me ^ place
        pieces.append(
            lax.dynamic_index_in_dim(blocks, (m & 1) * half + (m >> 1), 0, keepdims=False)
        )
    return jnp.concatenate(pieces)


def halve(x, axis):
    count, me = lax.axis_size(axis), lax.axis_index(axis)
    width = x.shape[1]
    size = count // 2
    while size >= 1:
        side = (me // size) % 2
        halves = x.reshape(2, -1, width)
        keep = lax.dynamic_index_in_dim(halves, side, 0, keepdims=False)
        give = lax.dynamic_index_in_dim(halves, 1 - side, 0, keepdims=False)
        x = keep + swap(give, size, axis)
        size //= 2
    return x.reshape(width)


def turn_lanes(x, cosine, ahead, behind):
    half_rot = ROT // 2
    lanes = x.shape[-1]
    return (
        x * cosine
        + pltpu.roll(x, lanes - half_rot, 1) * ahead
        + pltpu.roll(x, half_rot, 1) * behind
    )


def project_kernel(
    order, own_ref, other_ref, gain, shift, weight, bias, cosine, ahead, behind,
    act, q, k, v, stats,
):
    count = pl.num_programs(0)
    step = pl.program_id(0)
    width = q.shape[1]

    def work(x_ref):
        x = x_ref[...].astype(F32)
        centre = jnp.mean(x, axis=1, keepdims=True)
        centred = x - centre
        rate = lax.rsqrt(jnp.mean(centred * centred, axis=1, keepdims=True) + epsilon)
        lane = lax.broadcasted_iota(jnp.int32, stats.shape, 1)
        stats[...] = jnp.where(lane == 0, centre, rate)
        normed = (centred * rate * gain[...] + shift[...]).astype(BF)
        act[...] = normed
        projected = dot(normed, weight[...]) + bias[...]
        for at in range(0, width, PAIR):
            angles = (cosine[...], ahead[...], behind[...])
            q[:, at : at + PAIR] = turn_lanes(projected[:, at : at + PAIR], *angles).astype(BF)
            k[:, at : at + PAIR] = turn_lanes(
                projected[:, width + at : width + at + PAIR], *angles
            ).astype(BF)
        v[...] = projected[:, 2 * width :].astype(BF)

    @pl.when(step < count // 2)
    def _():
        work(own_ref)

    @pl.when(step >= count // 2)
    def _():
        work(other_ref)


def project(own, other, gain, shift, weight, bias, tables):
    count = lax.axis_size("wide")
    half = count // 2
    rows = own.shape[0] // half
    depth, columns = weight.shape
    width = columns // 3
    total = rows * count
    me = lax.axis_index("wide")
    order = jnp.stack([me ^ m for m in list(range(0, count, 2)) + list(range(1, count, 2))])

    def whole(i, order):
        return (0, 0)

    def placed(i, order):
        return (order[i], 0)

    vec = pl.BlockSpec((1, depth), whole)
    table = pl.BlockSpec((rows, PAIR), placed)
    out = pl.BlockSpec((rows, width), placed)
    return pl.pallas_call(
        project_kernel,
        grid_spec=pltpu.PrefetchScalarGridSpec(
            num_scalar_prefetch=1,
            grid=(count,),
            in_specs=[
                pl.BlockSpec((rows, depth), lambda i, order: (jnp.minimum(i, half - 1), 0)),
                pl.BlockSpec((rows, depth), lambda i, order: (jnp.maximum(i - half, 0), 0)),
                vec,
                vec,
                pl.BlockSpec((depth, columns), whole),
                pl.BlockSpec((1, columns), whole),
                table,
                table,
                table,
            ],
            out_specs=[
                pl.BlockSpec((rows, depth), placed),
                out,
                out,
                out,
                pl.BlockSpec((rows, PAIR), lambda i, order: (i, 0)),
            ],
        ),
        out_shape=[
            jax.ShapeDtypeStruct((total, depth), BF),
            jax.ShapeDtypeStruct((total, width), BF),
            jax.ShapeDtypeStruct((total, width), BF),
            jax.ShapeDtypeStruct((total, width), BF),
            jax.ShapeDtypeStruct((total, PAIR), F32),
        ],
        cost_estimate=pl.CostEstimate(flops=17 * 10**9, bytes_accessed=1, transcendentals=0),
        compiler_params=pltpu.CompilerParams(
            dimension_semantics=("arbitrary",), vmem_limit_bytes=48 * 2**20
        ),
        name="project",
    )(order, own, other, gain, shift, weight, bias, *tables)


def unproject_kernel(order, g_ref, x_ref, stats, weight, out, gain, shift, bias, held):
    half = order.shape[0]
    rows = held.shape[0] // half

    @pl.when(pl.program_id(0) == 0)
    def _():
        for i in range(half):
            start = pl.multiple_of(order[i] * rows, rows)
            held[i * rows : (i + 1) * rows, :] = g_ref[pl.ds(start, rows), :]
        bias[...] = jnp.sum(held[...].astype(F32), axis=0, keepdims=True)

    unit = (x_ref[...].astype(F32) - stats[:, 0:1]) * stats[:, 1:2]
    incoming = dot(held[...], weight[...], NT)
    out[...] = incoming.astype(BF)
    gain[...] = jnp.sum(incoming * unit, axis=0, keepdims=True)
    shift[...] = jnp.sum(incoming, axis=0, keepdims=True)


def unproject(grads, x, stats, weight, first):
    count = lax.axis_size("wide")
    total = x.shape[0]
    depth, columns = weight.shape
    block = math.gcd(depth, 1024)
    order = jnp.stack([lax.axis_index("wide") ^ m for m in range(first, count, 2)])
    vec = pl.BlockSpec((1, block), lambda j, order: (0, j))
    return pl.pallas_call(
        unproject_kernel,
        grid_spec=pltpu.PrefetchScalarGridSpec(
            num_scalar_prefetch=1,
            grid=(depth // block,),
            in_specs=[
                pl.BlockSpec(grads.shape, lambda j, order: (0, 0)),
                pl.BlockSpec((total, block), lambda j, order: (0, j)),
                pl.BlockSpec((total, PAIR), lambda j, order: (first, 0)),
                pl.BlockSpec((block, columns), lambda j, order: (j, 0)),
            ],
            out_specs=[
                pl.BlockSpec((total, block), lambda j, order: (0, j)),
                vec,
                vec,
                pl.BlockSpec((1, columns), lambda j, order: (0, 0)),
            ],
            scratch_shapes=[pltpu.VMEM((total, columns), BF)],
        ),
        out_shape=[
            jax.ShapeDtypeStruct((total, depth), BF),
            jax.ShapeDtypeStruct((1, depth), F32),
            jax.ShapeDtypeStruct((1, depth), F32),
            jax.ShapeDtypeStruct((1, columns), F32),
        ],
        cost_estimate=pl.CostEstimate(flops=7 * 10**9, bytes_accessed=1, transcendentals=0),
        compiler_params=pltpu.CompilerParams(
            dimension_semantics=("arbitrary",), vmem_limit_bytes=48 * 2**20
        ),
        name="unproject",
    )(order, grads, x, stats, weight)


def head_mask(head, shape):
    lane = lax.broadcasted_iota(jnp.int32, shape, 1)
    return (lane // HEAD_DIM) == head


def attend_kernel(first, q_ref, k_ref, v_ref, o_ref, log_ref, v_turned):
    block = q_ref.shape[0]
    at = pl.program_id(1)
    scale = HEAD_DIM ** (-0.5)

    @pl.when(at == 0)
    def _():
        v_turned[...] = v_ref[...].astype(F32).T.astype(BF)

    q = q_ref[...] * jnp.asarray(scale, BF)
    queries = [jnp.where(head_mask(h, q.shape), q, jnp.zeros_like(q)) for h in range(2)]
    own_first = first[...]
    own_place = at * block + lax.broadcasted_iota(jnp.int32, (1, block), 1)

    def step(number, state):
        keys = k_ref[pl.ds(number * block, block), :]
        values = v_turned[:, pl.ds(number * block, block)]
        place = number * block + lax.broadcasted_iota(jnp.int32, (block, block), 0)
        visible = (place >= own_first) & (place <= own_place)
        out = []
        for h in range(2):
            peak, total, mix = state[h]
            scores = jnp.where(visible, dot(keys, queries[h], NT), neg_large)
            new_peak = jnp.maximum(peak, jnp.max(scores, axis=0, keepdims=True))
            terms = jnp.where(visible, jnp.exp(scores - new_peak), 0.0)
            decay = jnp.exp(peak - new_peak)
            out.append(
                (
                    new_peak,
                    total * decay + jnp.sum(terms, axis=0, keepdims=True),
                    mix * decay
                    + dot(values[h * HEAD_DIM : (h + 1) * HEAD_DIM], terms.astype(BF)),
                )
            )
        return tuple(out)

    start = (
        jnp.full((1, block), neg_large, F32),
        jnp.zeros((1, block), F32),
        jnp.zeros((HEAD_DIM, block), F32),
    )
    state = lax.fori_loop(0, at + 1, step, (start, start))
    mixes = []
    for h in range(2):
        peak, total, mix = state[h]
        mixes.append(mix / total)
        log_ref[0, h : h + 1, :] = peak + jnp.log(total)
    o_ref[...] = jnp.concatenate(mixes, axis=0).T.astype(BF)


def attend(first, q, k, v):
    total, width = q.shape
    pairs = width // PAIR
    block = math.gcd(total, 256)
    return pl.pallas_call(
        attend_kernel,
        grid=(pairs, total // block),
        in_specs=[
            pl.BlockSpec((1, block), lambda p, i: (0, i)),
            pl.BlockSpec((block, PAIR), lambda p, i: (i, p)),
            pl.BlockSpec((total, PAIR), lambda p, i: (0, p)),
            pl.BlockSpec((total, PAIR), lambda p, i: (0, p)),
        ],
        out_specs=[
            pl.BlockSpec((block, PAIR), lambda p, i: (i, p)),
            pl.BlockSpec((1, 2, block), lambda p, i: (p, 0, i)),
        ],
        out_shape=[
            jax.ShapeDtypeStruct((total, width), BF),
            jax.ShapeDtypeStruct((pairs, 2, total), F32),
        ],
        scratch_shapes=[pltpu.VMEM((PAIR, total), BF)],
        cost_estimate=pl.CostEstimate(flops=39 * 10**9, bytes_accessed=1, transcendentals=0),
        compiler_params=pltpu.CompilerParams(
            dimension_semantics=("arbitrary", "arbitrary"), vmem_limit_bytes=32 * 2**20
        ),
        name="attend",
    )(first, q, k, v)


def attend_back_kernel(
    first, q_ref, k_ref, v_ref, o_ref, g_ref, log_ref, cosine, ahead, behind,
    gq_ref, gk_ref, gv_ref, k_turned, delta, sum_q,
):
    total = q_ref.shape[0]
    block = k_ref.shape[0]
    at = pl.program_id(1)
    last = pl.num_programs(1)
    scale = HEAD_DIM ** (-0.5)
    k = k_ref[...]
    k_turned[...] = k.astype(F32).T.astype(BF)

    @pl.when(at == 0)
    def _():
        sum_q[...] = jnp.zeros_like(sum_q)

        def fill(number, carry):
            spot = pl.ds(number * block, block)
            both = (g_ref[spot, :].astype(F32) * o_ref[spot, :].astype(F32)).T
            for h in range(2):
                delta[h : h + 1, spot] = jnp.sum(
                    both[h * HEAD_DIM : (h + 1) * HEAD_DIM], axis=0, keepdims=True
                )
            return carry

        lax.fori_loop(0, last, fill, 0)

    v = v_ref[...]
    place = at * block + lax.broadcasted_iota(jnp.int32, (block, block), 0)

    def step(number, state):
        sum_k, sum_v = state
        spot = pl.ds(number * block, block)
        q = q_ref[spot, :] * jnp.asarray(scale, BF)
        g = g_ref[spot, :]
        own_place = number * block + lax.broadcasted_iota(jnp.int32, (1, block), 1)
        visible = (place >= first[:, spot]) & (place <= own_place)
        for h in range(2):
            mask = head_mask(h, q.shape)
            q_head = jnp.where(mask, q, jnp.zeros_like(q))
            g_head = jnp.where(mask, g, jnp.zeros_like(g))
            scores = dot(k, q_head, NT)
            probs = jnp.where(
                visible,
                jnp.exp(jnp.where(visible, scores - log_ref[0, h : h + 1, spot], neg_large)),
                0.0,
            )
            slopes = dot(v, g_head, NT)
            low = (probs * (slopes - delta[h : h + 1, spot])).astype(BF)
            sum_v = sum_v + dot(probs.astype(BF), g_head)
            sum_k = sum_k + dot(low, q_head)
            span = slice(h * HEAD_DIM, (h + 1) * HEAD_DIM)
            sum_q[span, spot] += dot(k_turned[span, :], low)
        return (sum_k, sum_v)

    zeros = jnp.zeros((block, PAIR), F32)
    sum_k, sum_v = lax.fori_loop(at, last, step, (zeros, zeros))
    gv_ref[...] = sum_v.astype(BF)
    mine = pl.ds(at * block, block)
    gk_ref[...] = turn_lanes(sum_k, cosine[mine, :], -ahead[mine, :], -behind[mine, :]).astype(BF)

    @pl.when(at == last - 1)
    def _():
        def finish(number, carry):
            spot = pl.ds(number * block, block)
            gq_ref[spot, :] = turn_lanes(
                sum_q[:, spot].T * scale, cosine[spot, :], -ahead[spot, :], -behind[spot, :]
            ).astype(BF)
            return carry

        lax.fori_loop(0, last, finish, 0)


def attend_back(first, q, k, v, o, g, logs, tables):
    total, width = q.shape
    pairs = width // PAIR
    block = math.gcd(total, 256)
    whole = pl.BlockSpec((total, PAIR), lambda p, i: (0, p))
    part = pl.BlockSpec((block, PAIR), lambda p, i: (i, p))
    table = pl.BlockSpec((total, PAIR), lambda p, i: (0, 0))
    shape = jax.ShapeDtypeStruct((total, width), BF)
    return pl.pallas_call(
        attend_back_kernel,
        grid=(pairs, total // block),
        in_specs=[
            pl.BlockSpec((1, total), lambda p, i: (0, 0)),
            whole,
            part,
            part,
            whole,
            whole,
            pl.BlockSpec((1, 2, total), lambda p, i: (p, 0, 0)),
            table,
            table,
            table,
        ],
        out_specs=[whole, part, part],
        out_shape=[shape, shape, shape],
        scratch_shapes=[
            pltpu.VMEM((PAIR, block), BF),
            pltpu.VMEM((2, total), F32),
            pltpu.VMEM((PAIR, total), F32),
        ],
        cost_estimate=pl.CostEstimate(flops=44 * 10**9, bytes_accessed=1, transcendentals=0),
        compiler_params=pltpu.CompilerParams(
            dimension_semantics=("arbitrary", "arbitrary"), vmem_limit_bytes=48 * 2**20
        ),
        name="attend_back",
    )(first, q, k, v, o, g, logs, *tables)


def regroup_kernel(x_ref, o_ref):
    count, rows, width = o_ref.shape
    groups = width // HEAD_DIM
    for w in range(count):
        for g in range(0, groups, 2):
            pieces = []
            for j in (g, g + 1):
                at = (j * count + w) * HEAD_DIM
                base = at // PAIR * PAIR
                pair = x_ref[:, base : base + PAIR].astype(F32)
                pieces.append(pair[:, at - base : at - base + HEAD_DIM])
            o_ref[w, :, g * HEAD_DIM : g * HEAD_DIM + PAIR] = jnp.concatenate(
                pieces, axis=1
            ).astype(o_ref.dtype)


def regroup(x, count):
    rows, columns = x.shape
    return pl.pallas_call(
        regroup_kernel,
        out_shape=jax.ShapeDtypeStruct((count, rows, columns // count), x.dtype),
        compiler_params=pltpu.CompilerParams(vmem_limit_bytes=16 * 2**20),
        name="regroup",
    )(x)


def regroup_back_kernel(x_ref, o_ref):
    parts, count, rows, width = x_ref.shape
    for g in range(width // HEAD_DIM):
        base = g * HEAD_DIM // PAIR * PAIR
        shift = g * HEAD_DIM - base
        for w in range(0, count, 2):
            pieces = []
            for j in (w, w + 1):
                total = x_ref[0, j, :, base : base + PAIR].astype(F32)
                for part in range(1, parts):
                    total = total + x_ref[part, j, :, base : base + PAIR].astype(F32)
                pieces.append(total[:, shift : shift + HEAD_DIM])
            at = (g * count + w) * HEAD_DIM
            o_ref[:, at : at + PAIR] = jnp.concatenate(pieces, axis=1)


def regroup_back(x):
    parts, count, rows, width = x.shape
    return pl.pallas_call(
        regroup_back_kernel,
        out_shape=jax.ShapeDtypeStruct((rows, count * width), F32),
        compiler_params=pltpu.CompilerParams(vmem_limit_bytes=16 * 2**20),
        name="regroup_back",
    )(x)


def norm_parts(values):
    centred = values - jnp.mean(values, axis=-1, keepdims=True)
    spread = jnp.mean(centred * centred, axis=-1, keepdims=True)
    rate = lax.rsqrt(spread + epsilon)
    return centred * rate, rate


def norm_back(incoming, unit, rate, gain):
    scaled = incoming * gain
    return rate * (
        scaled
        - jnp.mean(scaled, axis=-1, keepdims=True)
        - unit * jnp.mean(scaled * unit, axis=-1, keepdims=True)
    )


def shards(
    tokens,
    segments,
    w_qkv,
    b_qkv,
    w_out,
    ln1_gain,
    ln1_bias,
    ln2_gain,
    ln2_bias,
    w_gate,
    w_up,
    w_down,
    out_grad,
):
    rows_n, wide_n = lax.axis_size("rows"), lax.axis_size("wide")
    me_row, me = lax.axis_index("rows"), lax.axis_index("wide")
    devices = rows_n * wide_n
    local = tokens.shape[1]
    width = tokens.shape[2]
    row_len = local * wide_n
    per = HEADS // wide_n
    span = per * HEAD_DIM
    slab = width // devices
    bias_slab = 3 * width // devices

    def stage(run, *args):
        shapes = jax.eval_shape(run, *args)

        def blank(*args):
            return jax.tree.map(lambda x: jnp.zeros(x.shape, x.dtype), shapes)

        return lax.cond(segments[0, 0] >= 0, run, blank, *args)

    def sum_rows(x, dim):
        return lax.psum_scatter(x, "rows", scatter_dimension=dim, tiled=True)

    fast_out = slab == HEAD_DIM and per == rows_n
    if fast_out:
        w_out_own = lax.all_gather(w_out, "rows", axis=0, tiled=True)
    else:
        w_out_own = lax.dynamic_index_in_dim(
            lax.all_gather(w_out, ALL, axis=0, tiled=True).reshape(
                per, wide_n, HEAD_DIM, width
            ),
            me,
            1,
            keepdims=False,
        ).reshape(span, width)
    w_qkv_part = lax.all_to_all(
        regroup(w_qkv, wide_n), "wide", 0, 0, tiled=True
    ).reshape(wide_n * slab, 3 * span)
    w_qkv_own = lax.all_gather(w_qkv_part, "rows", axis=0, tiled=True)
    units = w_gate.shape[1]
    enter_slab = lax.all_gather(
        jnp.concatenate([w_gate, w_up], axis=1), "rows", axis=0, tiled=True
    )
    down_slab = lax.all_gather(w_down, "rows", axis=0, tiled=True)

    grad_low = out_grad[0]

    def first_stage(b_qkv, ln1_gain, ln1_bias, ln2_gain, ln2_bias, segs, tokens):
        packed = jnp.concatenate([b_qkv, ln1_gain, ln1_bias, ln2_gain, ln2_bias, segs])
        small = lax.all_gather(lax.all_gather(packed, "rows"), "wide")
        got = gather_first(tokens)
        own, other = gather_last(
            tokens, got, gather_second(tokens, after(got, small) if got else got)
        )
        flat = small.transpose(1, 0, 2)

        def vector(start, size):
            return flat[:, :, start : start + size].reshape(1, devices * size).astype(F32)

        row_segs = lax.dynamic_index_in_dim(small, me_row, 1, keepdims=False)[
            :, bias_slab + 4 * slab :
        ].reshape(row_len)
        own_bias = lax.dynamic_index_in_dim(
            vector(0, bias_slab).reshape(3, per, wide_n, HEAD_DIM), me, 2, keepdims=False
        ).reshape(1, 3 * span)

        doc_first = jnp.sum((row_segs[:, None] < row_segs[None, :]).astype(jnp.int32), axis=0)
        positions = jnp.arange(row_len, dtype=jnp.int32) - doc_first
        freqs = 10000.0 ** (-2.0 * jnp.arange(ROT // 2, dtype=F32) / ROT)
        lane = jnp.arange(PAIR) % HEAD_DIM
        lane_freqs = jnp.where(lane < ROT, jnp.tile(freqs, PAIR // (ROT // 2)), 0.0)
        angles = positions.astype(F32)[:, None] * lane_freqs[None, :]
        sine = jnp.sin(angles)
        half_rot = ROT // 2
        tables = (
            jnp.cos(angles),
            jnp.where(lane < half_rot, -sine, 0.0),
            jnp.where((lane >= half_rot) & (lane < ROT), sine, 0.0),
        )
        gains = tuple(vector(bias_slab + i * slab, slab) for i in range(4))
        return own, other, own_bias, gains, doc_first.reshape(1, row_len), tables

    own, other, own_bias, gains, first, tables = stage(
        first_stage,
        after(b_qkv, w_qkv_part),
        ln1_gain,
        ln1_bias,
        ln2_gain,
        ln2_bias,
        segments[0].astype(BF),
        tokens[0],
    )
    gain_one, shift_one, gain_two, shift_two = gains
    grads_got = gather_first(after(grad_low, own))

    act_one, q, k, v, stats = project(
        after(own, w_out_own), other, gain_one, shift_one, w_qkv_own, own_bias, tables
    )
    grads_passed = gather_second(grad_low, grads_got)
    attn_low, logs = attend(first, after(q, *grads_got), k, v)
    attn_low = after(attn_low, *grads_passed)

    def middle_stage(attn_low, w_out_own, gain_two, shift_two, tokens, grads):
        row_grad = jnp.concatenate(gather_last(*grads))
        attn_halves = to_relative(attn_low)
        total = start_scatter(*[dot(a, w_out_own).astype(BF) for a in attn_halves])
        middle = tokens.astype(F32) + scatter_plane(total)
        unit, rate = norm_parts(middle)
        act_two = (unit * gain_two + shift_two).astype(BF)
        return attn_halves, middle, unit, rate, gather_own(act_two), row_grad

    attn_halves, middle, unit_two, rate_two, act_own, row_grad = stage(
        middle_stage,
        attn_low,
        w_out_own,
        gain_two,
        shift_two,
        tokens[0],
        (grad_low, grads_got, grads_passed),
    )

    over_first = (((0,), (1,)), ((), ()))
    over_second = (((1,), (0,)), ((), ()))

    def enter_stage(act_own, enter_slab, row_grad):
        act_halves = (act_own, swap(act_own, 1))
        entered = [dot(enter_slab, act, over_first) for act in act_halves]
        hidden = [(jax.nn.silu(e[:units]) * e[units:]).astype(BF) for e in entered]
        grad_down = dot(
            row_grad, jnp.concatenate(hidden, axis=1), (((0,), (1,)), ((), ()))
        ).astype(BF)
        return act_halves, entered, hidden, grad_down

    act_halves, entered, hidden, grad_down = stage(enter_stage, act_own, enter_slab, row_grad)
    sum_down = sum_rows(grad_down, 0)

    def hidden_stage(act_halves, entered, row_grad, enter_slab, down_slab):
        enter_grads, act_parts = [], []
        for e, grad in zip(entered, jnp.split(row_grad, 2)):
            gate, upper = e[:units], e[units:]
            sig = jax.nn.sigmoid(gate)
            grad_hidden = dot(down_slab, grad, over_first)
            enter_grads.append(
                jnp.concatenate(
                    [
                        (grad_hidden * upper * sig * (1.0 + gate * (1.0 - sig))).astype(BF),
                        (grad_hidden * (gate * sig)).astype(BF),
                    ]
                )
            )
            act_parts.append(dot(enter_grads[-1], enter_slab, over_first).astype(BF))
        grad_enter = dot(
            jnp.concatenate(enter_grads, axis=1), jnp.concatenate(act_halves), over_second
        ).astype(BF)
        return start_scatter(*act_parts), grad_enter

    act_sum, grad_enter = stage(
        hidden_stage, act_halves, entered, row_grad, enter_slab, down_slab
    )
    sum_enter = sum_rows(grad_enter, 1)

    def norm_stage(act_sum, unit, rate, gain, grad_low, hidden, down_slab):
        grad_act_two = scatter_plane(act_sum)
        grad_norm = norm_back(grad_act_two, unit, rate, gain)
        return (
            grad_low.astype(F32) + grad_norm,
            jnp.sum(grad_act_two * unit, axis=0),
            jnp.sum(grad_act_two, axis=0),
            start_scatter(*[dot(h, down_slab, over_first).astype(BF) for h in hidden]),
        )

    grad_middle, grad_gain_two, grad_shift_two, mixed_sum = stage(
        norm_stage, act_sum, unit_two, rate_two, gain_two, grad_low, hidden, down_slab
    )

    branch_own = stage(gather_own, after(grad_middle, sum_down).astype(BF))
    branch_halves = (branch_own, swap(branch_own, 1))
    grad_w_out = dot(
        jnp.concatenate(attn_halves), jnp.concatenate(branch_halves), TN
    ).astype(BF)
    if fast_out:
        sum_w_out = sum_rows(grad_w_out, 0)
    else:
        spread_out = lax.dynamic_update_index_in_dim(
            jnp.zeros((per, wide_n, HEAD_DIM, width), BF),
            grad_w_out.reshape(per, HEAD_DIM, width),
            me,
            1,
        )
        sum_w_out = lax.psum_scatter(
            spread_out.reshape(width, width), ALL, scatter_dimension=0, tiled=True
        )

    def back_stage(branch_halves, w_out_own, first, q, k, v, attn_low, logs, tables, act_one, mixed_sum):
        grad_attn = to_absolute(*[dot(b, w_out_own, NT).astype(BF) for b in branch_halves])
        grads = attend_back(first, q, k, v, attn_low, grad_attn, logs, tables)
        grad_proj = jnp.concatenate(grads, axis=1)
        return grad_proj, dot(act_one, grad_proj, TN).astype(BF), scatter_first(mixed_sum)

    grad_proj, grad_w_qkv, mixed_got = stage(
        back_stage,
        after(branch_halves, grad_w_out),
        w_out_own,
        first,
        q,
        k,
        v,
        attn_low,
        logs,
        tables,
        act_one,
        mixed_sum,
    )
    grad_proj, grad_w_qkv = after((grad_proj, grad_w_qkv), sum_enter)
    grad_w_qkv = after(grad_w_qkv, sum_w_out)
    sum_qkv = sum_rows(grad_w_qkv, 0)

    def last_stage(
        grad_proj, w_qkv_own, own, other, stats, gain, grad_middle, grad_gain_two, grad_shift_two,
        mixed_sum, mixed_got,
    ):
        mixed = scatter_last(mixed_sum, mixed_got, scatter_second(mixed_sum, mixed_got))
        part_other, *sums_other = unproject(grad_proj, other, stats, w_qkv_own, 1)
        part_own, *sums_own = unproject(grad_proj, own, stats, w_qkv_own, 0)
        total = start_scatter(part_own, part_other)
        grad_gain, grad_shift, grad_bias = (a + b for a, b in zip(sums_own, sums_other))
        full_bias = lax.dynamic_update_index_in_dim(
            jnp.zeros((3, per, wide_n, HEAD_DIM), F32),
            grad_bias.reshape(3, per, HEAD_DIM),
            me,
            2,
        )
        small = jnp.concatenate(
            [
                full_bias.reshape(devices, bias_slab),
                grad_gain.reshape(devices, slab),
                grad_shift.reshape(devices, slab),
                grad_gain_two.reshape(devices, slab),
                grad_shift_two.reshape(devices, slab),
            ],
            axis=1,
        )
        small = small.reshape(rows_n, wide_n, -1).transpose(1, 0, 2)
        sums = halve(small.reshape(wide_n, -1), "wide").reshape(rows_n, -1)
        rate = stats[:local, 1:2]
        unit = (own[:local].astype(F32) - stats[:local, 0:1]) * rate
        return grad_middle + norm_back(scatter_plane(total), unit, rate, gain), sums, mixed

    grad_tokens, sums, mixed = stage(
        last_stage,
        after(grad_proj, grad_w_qkv),
        w_qkv_own,
        own,
        other,
        stats,
        gain_one,
        grad_middle,
        grad_gain_two,
        grad_shift_two,
        mixed_sum,
        mixed_got,
    )
    grad_tokens = grad_tokens[None]
    mixed, sum_down, sum_enter = after((mixed, sum_down, sum_enter), sums)
    part_qkv = lax.all_to_all(
        after(sum_qkv, sums).reshape(wide_n, slab, 3 * span), "wide", 0, 0, tiled=True
    )
    sums = halve(after(sums, sum_qkv), "rows")
    result = (middle + mixed).astype(BF)[None]
    out_down = sum_down.astype(F32)
    out_gate, out_up = sum_enter[:units].T.astype(F32), sum_enter[units:].T.astype(F32)
    out_w_out = after(sum_w_out, sums).astype(F32)
    out_qkv = regroup_back(part_qkv[None])
    out_bias = sums[:bias_slab]
    small_outs = [
        sums[bias_slab + i * slab : bias_slab + (i + 1) * slab] for i in range(4)
    ]
    return (
        result,
        grad_tokens,
        out_qkv,
        out_bias,
        out_w_out,
        *small_outs,
        out_gate,
        out_up,
        out_down,
    )


def solution(mesh):
    by_token = P("rows", "wide", None)
    by_both = P(("rows", "wide"), None)
    vector = P(("rows", "wide"))
    by_slab = P("rows", "wide")
    in_specs = (
        by_token, P("rows", "wide"), by_both, vector, by_both, vector, vector, vector, vector,
        by_slab, by_slab, by_slab, by_token,
    )
    out_specs = (
        by_token, by_token, by_both, vector, by_both, vector, vector, vector, vector,
        by_slab, by_slab, by_slab,
    )
    return jax.shard_map(shards, mesh=mesh, in_specs=in_specs, out_specs=out_specs, check_vma=False)
```

```python
import functools
import math

import jax
import jax.numpy as jnp
from jax import lax
from jax.experimental import pallas as pl
from jax.experimental.pallas import tpu as pltpu
from jax.sharding import PartitionSpec as P

HEADS = 32
HEAD_DIM = 64
ROT = 16
PAIR = 2 * HEAD_DIM

epsilon = 1e-05
neg_large = -1e30
BF = jnp.bfloat16
F32 = jnp.float32
ALL = ("rows", "wide")
NT = (((1,), (1,)), ((), ()))
TN = (((0,), (0,)), ((), ()))


def dot(left, right, dims=(((1,), (0,)), ((), ()))):
    return lax.dot_general(left, right, dims, preferred_element_type=F32)


def swap(x, bit, axis="wide"):
    return lax.ppermute(x, axis, [(i, i ^ bit) for i in range(lax.axis_size(axis))])


def upper_bits():
    return [1 << k for k in range(1, lax.axis_size("wide").bit_length() - 1)]


def gather_first(x):
    bits = upper_bits()
    return tuple(swap(x, bit) for bit in bits) if len(bits) == 2 else ()


def gather_second(x, got):
    if not got:
        return ()
    one, two = upper_bits()
    half = x.shape[0] // 2
    return swap(got[1][:half], one), swap(got[0][half:], two)


def gather_third(x, got, passed):
    if got:
        return jnp.concatenate([x, *got, *passed])
    for bit in upper_bits():
        x = jnp.concatenate([x, swap(x, bit)])
    return x


def gather_last(x, got, passed):
    own = gather_third(x, got, passed)
    return own, swap(own, 1)


def gather_own(x):
    got = gather_first(x)
    return gather_third(x, got, gather_second(x, got))


def add_low(left, right):
    return (left.astype(F32) + right.astype(F32)).astype(BF)


def start_scatter(own, other):
    return add_low(lax.optimization_barrier(own), swap(other, 1))


def block_of(total, m, h):
    half = total.shape[0] // 8
    return total[(2 * m + h) * half : (2 * m + h + 1) * half]


def scatter_first(total):
    bits = upper_bits()
    if len(bits) != 2:
        return ()
    one, two = bits
    return (
        swap(block_of(total, 3, 0), one),
        swap(block_of(total, 3, 1), two),
        swap(block_of(total, 1, 0), one),
        swap(block_of(total, 2, 1), two),
    )


def scatter_between(total, got):
    if not got:
        return ()
    return add_low(block_of(total, 2, 0), got[0]), add_low(block_of(total, 1, 1), got[1])


def scatter_second(between):
    if not between:
        return ()
    one, two = upper_bits()
    return swap(between[0], two), swap(between[1], one)


def scatter_last(total, got, passed):
    if got:
        return jnp.concatenate(
            [
                block_of(total, 0, h).astype(F32) + got[2 + h].astype(F32) + passed[h].astype(F32)
                for h in range(2)
            ]
        )
    bits = upper_bits()
    for bit in reversed(bits[1:]):
        half = total.shape[0] // 2
        total = add_low(total[:half], swap(total[half:], bit))
    half = total.shape[0] // 2
    return total[:half].astype(F32) + swap(total[half:], bits[0]).astype(F32)


def scatter_plane(total):
    got = scatter_first(total)
    return scatter_last(total, got, scatter_second(scatter_between(total, got)))


def after(x, *others):
    return lax.optimization_barrier((x, others))[0]


def to_relative(x):
    count = lax.axis_size("wide")
    me = lax.axis_index("wide")
    blocks = x.reshape(count, x.shape[0] // count, x.shape[1])

    def pick(first):
        return jnp.concatenate(
            [
                lax.dynamic_index_in_dim(blocks, me ^ m, 0, keepdims=False)
                for m in range(first, count, 2)
            ]
        )

    return pick(0), pick(1)


def to_absolute(own, other):
    count = lax.axis_size("wide")
    me = lax.axis_index("wide")
    half = count // 2
    blocks = jnp.concatenate([own, other]).reshape(count, -1, own.shape[1])
    pieces = []
    for place in range(count):
        m = me ^ place
        pieces.append(
            lax.dynamic_index_in_dim(blocks, (m & 1) * half + (m >> 1), 0, keepdims=False)
        )
    return jnp.concatenate(pieces)


def halve(x, axis):
    count, me = lax.axis_size(axis), lax.axis_index(axis)
    width = x.shape[1]
    size = count // 2
    while size >= 1:
        side = (me // size) % 2
        halves = x.reshape(2, -1, width)
        keep = lax.dynamic_index_in_dim(halves, side, 0, keepdims=False)
        give = lax.dynamic_index_in_dim(halves, 1 - side, 0, keepdims=False)
        x = keep + swap(give, size, axis)
        size //= 2
    return x.reshape(width)


def turn_lanes(x, cosine, ahead, behind):
    half_rot = ROT // 2
    lanes = x.shape[-1]
    return (
        x * cosine
        + pltpu.roll(x, lanes - half_rot, 1) * ahead
        + pltpu.roll(x, half_rot, 1) * behind
    )


def project_kernel(
    order, own_ref, other_ref, gain, shift, weight, bias, cosine, ahead, behind,
    act, q, k, v, stats,
):
    count = pl.num_programs(0)
    step = pl.program_id(0)
    width = q.shape[1]

    def work(x_ref):
        x = x_ref[...].astype(F32)
        centre = jnp.mean(x, axis=1, keepdims=True)
        centred = x - centre
        rate = lax.rsqrt(jnp.mean(centred * centred, axis=1, keepdims=True) + epsilon)
        lane = lax.broadcasted_iota(jnp.int32, stats.shape, 1)
        stats[...] = jnp.where(lane == 0, centre, rate)
        normed = (centred * rate * gain[...] + shift[...]).astype(BF)
        act[...] = normed
        projected = dot(normed, weight[...]) + bias[...]
        for at in range(0, width, PAIR):
            angles = (cosine[...], ahead[...], behind[...])
            q[:, at : at + PAIR] = turn_lanes(projected[:, at : at + PAIR], *angles).astype(BF)
            k[:, at : at + PAIR] = turn_lanes(
                projected[:, width + at : width + at + PAIR], *angles
            ).astype(BF)
        v[...] = projected[:, 2 * width :].astype(BF)

    @pl.when(step < count // 2)
    def _():
        work(own_ref)

    @pl.when(step >= count // 2)
    def _():
        work(other_ref)


def project(own, other, gain, shift, weight, bias, tables):
    count = lax.axis_size("wide")
    half = count // 2
    rows = own.shape[0] // half
    depth, columns = weight.shape
    width = columns // 3
    total = rows * count
    me = lax.axis_index("wide")
    order = jnp.stack([me ^ m for m in list(range(0, count, 2)) + list(range(1, count, 2))])

    def whole(i, order):
        return (0, 0)

    def placed(i, order):
        return (order[i], 0)

    vec = pl.BlockSpec((1, depth), whole)
    table = pl.BlockSpec((rows, PAIR), placed)
    out = pl.BlockSpec((rows, width), placed)
    return pl.pallas_call(
        project_kernel,
        grid_spec=pltpu.PrefetchScalarGridSpec(
            num_scalar_prefetch=1,
            grid=(count,),
            in_specs=[
                pl.BlockSpec((rows, depth), lambda i, order: (jnp.minimum(i, half - 1), 0)),
                pl.BlockSpec((rows, depth), lambda i, order: (jnp.maximum(i - half, 0), 0)),
                vec,
                vec,
                pl.BlockSpec((depth, columns), whole),
                pl.BlockSpec((1, columns), whole),
                table,
                table,
                table,
            ],
            out_specs=[
                pl.BlockSpec((rows, depth), placed),
                out,
                out,
                out,
                pl.BlockSpec((rows, PAIR), lambda i, order: (i, 0)),
            ],
        ),
        out_shape=[
            jax.ShapeDtypeStruct((total, depth), BF),
            jax.ShapeDtypeStruct((total, width), BF),
            jax.ShapeDtypeStruct((total, width), BF),
            jax.ShapeDtypeStruct((total, width), BF),
            jax.ShapeDtypeStruct((total, PAIR), F32),
        ],
        cost_estimate=pl.CostEstimate(flops=17 * 10**9, bytes_accessed=1, transcendentals=0),
        compiler_params=pltpu.CompilerParams(
            dimension_semantics=("arbitrary",), vmem_limit_bytes=48 * 2**20
        ),
        name="project",
    )(order, own, other, gain, shift, weight, bias, *tables)


def unproject_kernel(order, g_ref, x_ref, stats, weight, out, gain, shift, bias, held):
    half = order.shape[0]
    rows = held.shape[0] // half

    @pl.when(pl.program_id(0) == 0)
    def _():
        for i in range(half):
            start = pl.multiple_of(order[i] * rows, rows)
            held[i * rows : (i + 1) * rows, :] = g_ref[pl.ds(start, rows), :]
        bias[...] = jnp.sum(held[...].astype(F32), axis=0, keepdims=True)

    unit = (x_ref[...].astype(F32) - stats[:, 0:1]) * stats[:, 1:2]
    incoming = dot(held[...], weight[...], NT)
    out[...] = incoming.astype(BF)
    gain[...] = jnp.sum(incoming * unit, axis=0, keepdims=True)
    shift[...] = jnp.sum(incoming, axis=0, keepdims=True)


def unproject(grads, x, stats, weight, first):
    count = lax.axis_size("wide")
    total = x.shape[0]
    depth, columns = weight.shape
    block = math.gcd(depth, 512)
    order = jnp.stack([lax.axis_index("wide") ^ m for m in range(first, count, 2)])
    vec = pl.BlockSpec((1, block), lambda j, order: (0, j))
    return pl.pallas_call(
        unproject_kernel,
        grid_spec=pltpu.PrefetchScalarGridSpec(
            num_scalar_prefetch=1,
            grid=(depth // block,),
            in_specs=[
                pl.BlockSpec(grads.shape, lambda j, order: (0, 0)),
                pl.BlockSpec((total, block), lambda j, order: (0, j)),
                pl.BlockSpec((total, PAIR), lambda j, order: (first, 0)),
                pl.BlockSpec((block, columns), lambda j, order: (j, 0)),
            ],
            out_specs=[
                pl.BlockSpec((total, block), lambda j, order: (0, j)),
                vec,
                vec,
                pl.BlockSpec((1, columns), lambda j, order: (0, 0)),
            ],
            scratch_shapes=[pltpu.VMEM((total, columns), BF)],
        ),
        out_shape=[
            jax.ShapeDtypeStruct((total, depth), BF),
            jax.ShapeDtypeStruct((1, depth), F32),
            jax.ShapeDtypeStruct((1, depth), F32),
            jax.ShapeDtypeStruct((1, columns), F32),
        ],
        cost_estimate=pl.CostEstimate(flops=7 * 10**9, bytes_accessed=1, transcendentals=0),
        compiler_params=pltpu.CompilerParams(
            dimension_semantics=("arbitrary",), vmem_limit_bytes=48 * 2**20
        ),
        name="unproject",
    )(order, grads, x, stats, weight)


def head_mask(head, shape):
    lane = lax.broadcasted_iota(jnp.int32, shape, 1)
    return (lane // HEAD_DIM) == head


def attend_kernel(first, q_ref, k_ref, v_ref, o_ref, log_ref, v_turned):
    block = q_ref.shape[0]
    at = pl.program_id(1)
    scale = HEAD_DIM ** (-0.5)

    @pl.when(at == 0)
    def _():
        v_turned[...] = v_ref[...].astype(F32).T.astype(BF)

    q = q_ref[...] * jnp.asarray(scale, BF)
    queries = [jnp.where(head_mask(h, q.shape), q, jnp.zeros_like(q)) for h in range(2)]
    own_first = first[...]
    own_place = at * block + lax.broadcasted_iota(jnp.int32, (1, block), 1)

    def step(number, state, diagonal=False):
        keys = k_ref[pl.ds(number * block, block), :]
        values = v_turned[:, pl.ds(number * block, block)]
        place = number * block + lax.broadcasted_iota(jnp.int32, (block, block), 0)
        visible = place >= own_first
        if diagonal:
            visible = visible & (place <= own_place)
        out = []
        for h in range(2):
            peak, total, mix = state[h]
            scores = jnp.where(visible, dot(keys, queries[h], NT), neg_large)
            new_peak = jnp.maximum(peak, jnp.max(scores, axis=0, keepdims=True))
            terms = jnp.exp(scores - new_peak)
            decay = jnp.exp(peak - new_peak)
            out.append(
                (
                    new_peak,
                    total * decay + jnp.sum(terms, axis=0, keepdims=True),
                    mix * decay
                    + dot(values[h * HEAD_DIM : (h + 1) * HEAD_DIM], terms.astype(BF)),
                )
            )
        return tuple(out)

    start = (
        jnp.full((1, block), neg_large, F32),
        jnp.zeros((1, block), F32),
        jnp.zeros((HEAD_DIM, block), F32),
    )
    state = step(at, lax.fori_loop(0, at, step, (start, start)), True)
    mixes = []
    for h in range(2):
        peak, total, mix = state[h]
        mixes.append(mix / total)
        log_ref[0, h : h + 1, :] = peak + jnp.log(total)
    o_ref[...] = jnp.concatenate(mixes, axis=0).T.astype(BF)


def attend(first, q, k, v):
    total, width = q.shape
    pairs = width // PAIR
    block = math.gcd(total, 256)
    return pl.pallas_call(
        attend_kernel,
        grid=(pairs, total // block),
        in_specs=[
            pl.BlockSpec((1, block), lambda p, i: (0, i)),
            pl.BlockSpec((block, PAIR), lambda p, i: (i, p)),
            pl.BlockSpec((total, PAIR), lambda p, i: (0, p)),
            pl.BlockSpec((total, PAIR), lambda p, i: (0, p)),
        ],
        out_specs=[
            pl.BlockSpec((block, PAIR), lambda p, i: (i, p)),
            pl.BlockSpec((1, 2, block), lambda p, i: (p, 0, i)),
        ],
        out_shape=[
            jax.ShapeDtypeStruct((total, width), BF),
            jax.ShapeDtypeStruct((pairs, 2, total), F32),
        ],
        scratch_shapes=[pltpu.VMEM((PAIR, total), BF)],
        cost_estimate=pl.CostEstimate(flops=39 * 10**9, bytes_accessed=1, transcendentals=0),
        compiler_params=pltpu.CompilerParams(
            dimension_semantics=("arbitrary", "arbitrary"), vmem_limit_bytes=32 * 2**20
        ),
        name="attend",
    )(first, q, k, v)


def attend_back_kernel(
    first, q_ref, k_ref, v_ref, o_ref, g_ref, log_ref, cosine, ahead, behind,
    out_ref, k_turned, delta, sum_q, sum_k, sum_v,
):
    block, width = k_ref.shape
    pairs = width // PAIR
    at = pl.program_id(0)
    last = pl.num_programs(0)
    scale = HEAD_DIM ** (-0.5)
    k_turned[...] = k_ref[...].astype(F32).T.astype(BF)

    @pl.when(at == 0)
    def _():
        sum_q[...] = jnp.zeros_like(sum_q)

        def fill(number, carry):
            spot = pl.ds(number * block, block)
            both = (g_ref[spot, :].astype(F32) * o_ref[spot, :].astype(F32)).T
            for h in range(2 * pairs):
                delta[h : h + 1, spot] = jnp.sum(
                    both[h * HEAD_DIM : (h + 1) * HEAD_DIM], axis=0, keepdims=True
                )
            return carry

        lax.fori_loop(0, last, fill, 0)

    place = at * block + lax.broadcasted_iota(jnp.int32, (block, block), 0)

    def step(number, diagonal=False):
        spot = pl.ds(number * block, block)
        visible = place >= first[:, spot]
        if diagonal:
            own_place = number * block + lax.broadcasted_iota(jnp.int32, (1, block), 1)
            visible = visible & (place <= own_place)
        for p in range(pairs):
            pair = slice(p * PAIR, (p + 1) * PAIR)
            q = q_ref[spot, pair] * jnp.asarray(scale, BF)
            g = g_ref[spot, pair]
            k, v = k_ref[:, pair], v_ref[:, pair]
            more_k = more_v = 0.0
            for h in range(2):
                mask = head_mask(h, q.shape)
                q_head = jnp.where(mask, q, jnp.zeros_like(q))
                g_head = jnp.where(mask, g, jnp.zeros_like(g))
                scores = dot(k, q_head, NT)
                probs = jnp.exp(
                    jnp.where(visible, scores - log_ref[p, h : h + 1, spot], neg_large)
                )
                slopes = dot(v, g_head, NT)
                head = 2 * p + h
                low = (probs * (slopes - delta[head : head + 1, spot])).astype(BF)
                more_v = more_v + dot(probs.astype(BF), g_head)
                more_k = more_k + dot(low, q_head)
                span = slice(head * HEAD_DIM, (head + 1) * HEAD_DIM)
                sum_q[span, spot] += dot(k_turned[span, :], low)
            if diagonal:
                sum_k[:, pair] = more_k
                sum_v[:, pair] = more_v
            else:
                sum_k[:, pair] += more_k
                sum_v[:, pair] += more_v

    step(at, True)

    def later(number, carry):
        step(number)
        return carry

    lax.fori_loop(at + 1, last, later, 0)
    mine = pl.ds(at * block, block)
    out_ref[mine, 2 * width :] = sum_v[...].astype(BF)
    for p in range(pairs):
        start = width + p * PAIR
        out_ref[mine, start : start + PAIR] = turn_lanes(
            sum_k[:, p * PAIR : (p + 1) * PAIR],
            cosine[mine, :],
            -ahead[mine, :],
            -behind[mine, :],
        ).astype(BF)

    @pl.when(at == last - 1)
    def _():
        def finish(number, carry):
            spot = pl.ds(number * block, block)
            for p in range(pairs):
                pair = slice(p * PAIR, (p + 1) * PAIR)
                out_ref[spot, pair] = turn_lanes(
                    sum_q[pair, spot].T * scale,
                    cosine[spot, :],
                    -ahead[spot, :],
                    -behind[spot, :],
                ).astype(BF)
            return carry

        lax.fori_loop(0, last, finish, 0)


def attend_back(first, q, k, v, o, g, logs, tables):
    total, width = q.shape
    block = math.gcd(total, 256)

    def whole(*shape):
        return pl.BlockSpec(shape, lambda i: (0,) * len(shape))

    part = pl.BlockSpec((block, width), lambda i: (i, 0))
    return pl.pallas_call(
        attend_back_kernel,
        grid=(total // block,),
        in_specs=[
            whole(1, total),
            whole(total, width),
            part,
            part,
            whole(total, width),
            whole(total, width),
            whole(*logs.shape),
            whole(total, PAIR),
            whole(total, PAIR),
            whole(total, PAIR),
        ],
        out_specs=whole(total, 3 * width),
        out_shape=jax.ShapeDtypeStruct((total, 3 * width), BF),
        scratch_shapes=[
            pltpu.VMEM((width, block), BF),
            pltpu.VMEM((width // HEAD_DIM, total), F32),
            pltpu.VMEM((width, total), F32),
            pltpu.VMEM((block, width), F32),
            pltpu.VMEM((block, width), F32),
        ],
        cost_estimate=pl.CostEstimate(flops=44 * 10**9, bytes_accessed=1, transcendentals=0),
        compiler_params=pltpu.CompilerParams(
            dimension_semantics=("arbitrary",), vmem_limit_bytes=48 * 2**20
        ),
        name="attend_back",
    )(first, q, k, v, o, g, logs, *tables)


def regroup_kernel(x_ref, o_ref):
    count, rows, width = o_ref.shape
    groups = width // HEAD_DIM
    for w in range(count):
        for g in range(0, groups, 2):
            pieces = []
            for j in (g, g + 1):
                at = (j * count + w) * HEAD_DIM
                base = at // PAIR * PAIR
                pair = x_ref[:, base : base + PAIR].astype(F32)
                pieces.append(pair[:, at - base : at - base + HEAD_DIM])
            o_ref[w, :, g * HEAD_DIM : g * HEAD_DIM + PAIR] = jnp.concatenate(
                pieces, axis=1
            ).astype(o_ref.dtype)


def regroup(x, count):
    rows, columns = x.shape
    return pl.pallas_call(
        regroup_kernel,
        out_shape=jax.ShapeDtypeStruct((count, rows, columns // count), x.dtype),
        compiler_params=pltpu.CompilerParams(vmem_limit_bytes=16 * 2**20),
        name="regroup",
    )(x)


def regroup_back_kernel(x_ref, o_ref):
    parts, count, rows, width = x_ref.shape
    for g in range(width // HEAD_DIM):
        base = g * HEAD_DIM // PAIR * PAIR
        shift = g * HEAD_DIM - base
        for w in range(0, count, 2):
            pieces = []
            for j in (w, w + 1):
                total = x_ref[0, j, :, base : base + PAIR].astype(F32)
                for part in range(1, parts):
                    total = total + x_ref[part, j, :, base : base + PAIR].astype(F32)
                pieces.append(total[:, shift : shift + HEAD_DIM])
            at = (g * count + w) * HEAD_DIM
            o_ref[:, at : at + PAIR] = jnp.concatenate(pieces, axis=1)


def regroup_back(x):
    parts, count, rows, width = x.shape
    return pl.pallas_call(
        regroup_back_kernel,
        out_shape=jax.ShapeDtypeStruct((rows, count * width), F32),
        compiler_params=pltpu.CompilerParams(vmem_limit_bytes=16 * 2**20),
        name="regroup_back",
    )(x)


def norm_parts(values):
    centred = values - jnp.mean(values, axis=-1, keepdims=True)
    spread = jnp.mean(centred * centred, axis=-1, keepdims=True)
    rate = lax.rsqrt(spread + epsilon)
    return centred * rate, rate


def norm_back(incoming, unit, rate, gain):
    scaled = incoming * gain
    return rate * (
        scaled
        - jnp.mean(scaled, axis=-1, keepdims=True)
        - unit * jnp.mean(scaled * unit, axis=-1, keepdims=True)
    )


def shards(
    tokens,
    segments,
    w_qkv,
    b_qkv,
    w_out,
    ln1_gain,
    ln1_bias,
    ln2_gain,
    ln2_bias,
    w_gate,
    w_up,
    w_down,
    out_grad,
):
    rows_n, wide_n = lax.axis_size("rows"), lax.axis_size("wide")
    me_row, me = lax.axis_index("rows"), lax.axis_index("wide")
    devices = rows_n * wide_n
    local = tokens.shape[1]
    width = tokens.shape[2]
    row_len = local * wide_n
    per = HEADS // wide_n
    span = per * HEAD_DIM
    slab = width // devices
    bias_slab = 3 * width // devices

    def stage(run, *args):
        shapes = jax.eval_shape(run, *args)

        def blank(*args):
            return jax.tree.map(lambda x: jnp.zeros(x.shape, x.dtype), shapes)

        return lax.cond(segments[0, 0] >= 0, run, blank, *args)

    def sum_rows(x, dim):
        return lax.psum_scatter(x, "rows", scatter_dimension=dim, tiled=True)

    fast_out = slab == HEAD_DIM and per == rows_n
    if fast_out:
        w_out_own = lax.all_gather(w_out, "rows", axis=0, tiled=True)
    else:
        w_out_own = lax.dynamic_index_in_dim(
            lax.all_gather(w_out, ALL, axis=0, tiled=True).reshape(
                per, wide_n, HEAD_DIM, width
            ),
            me,
            1,
            keepdims=False,
        ).reshape(span, width)
    w_qkv_part = lax.all_to_all(
        regroup(w_qkv, wide_n), "wide", 0, 0, tiled=True
    ).reshape(wide_n * slab, 3 * span)
    w_qkv_own = lax.all_gather(w_qkv_part, "rows", axis=0, tiled=True)
    units = w_gate.shape[1]
    enter_slab = lax.all_gather(
        jnp.concatenate([w_gate, w_up], axis=1), "rows", axis=0, tiled=True
    )
    down_slab = lax.all_gather(w_down, "rows", axis=0, tiled=True)

    grad_low = out_grad[0]

    def first_stage(b_qkv, ln1_gain, ln1_bias, ln2_gain, ln2_bias, segs, tokens):
        packed = jnp.concatenate([b_qkv, ln1_gain, ln1_bias, ln2_gain, ln2_bias, segs])
        small = lax.all_gather(lax.all_gather(packed, "rows"), "wide")
        got = gather_first(tokens)
        own, other = gather_last(
            tokens, got, gather_second(tokens, after(got, small) if got else got)
        )
        flat = small.transpose(1, 0, 2)

        def vector(start, size):
            return flat[:, :, start : start + size].reshape(1, devices * size).astype(F32)

        row_segs = lax.dynamic_index_in_dim(small, me_row, 1, keepdims=False)[
            :, bias_slab + 4 * slab :
        ].reshape(row_len)
        own_bias = lax.dynamic_index_in_dim(
            vector(0, bias_slab).reshape(3, per, wide_n, HEAD_DIM), me, 2, keepdims=False
        ).reshape(1, 3 * span)

        doc_first = jnp.sum((row_segs[:, None] < row_segs[None, :]).astype(jnp.int32), axis=0)
        positions = jnp.arange(row_len, dtype=jnp.int32) - doc_first
        freqs = 10000.0 ** (-2.0 * jnp.arange(ROT // 2, dtype=F32) / ROT)
        lane = jnp.arange(PAIR) % HEAD_DIM
        lane_freqs = jnp.where(lane < ROT, jnp.tile(freqs, PAIR // (ROT // 2)), 0.0)
        angles = positions.astype(F32)[:, None] * lane_freqs[None, :]
        sine = jnp.sin(angles)
        half_rot = ROT // 2
        tables = (
            jnp.cos(angles),
            jnp.where(lane < half_rot, -sine, 0.0),
            jnp.where((lane >= half_rot) & (lane < ROT), sine, 0.0),
        )
        gains = tuple(vector(bias_slab + i * slab, slab) for i in range(4))
        return own, other, own_bias, gains, doc_first.reshape(1, row_len), tables

    own, other, own_bias, gains, first, tables = stage(
        first_stage,
        after(b_qkv, w_qkv_part),
        ln1_gain,
        ln1_bias,
        ln2_gain,
        ln2_bias,
        segments[0].astype(BF),
        tokens[0],
    )
    gain_one, shift_one, gain_two, shift_two = gains
    grads_got = gather_first(after(grad_low, own))

    act_one, q, k, v, stats = project(
        after(own, w_out_own), other, gain_one, shift_one, w_qkv_own, own_bias, tables
    )
    grads_passed = gather_second(grad_low, grads_got)
    attn_low, logs = attend(first, after(q, *grads_got), k, v)
    attn_low = after(attn_low, *grads_passed)

    def middle_stage(attn_low, w_out_own, gain_two, shift_two, tokens, grads):
        row_grad = jnp.concatenate(gather_last(*grads))
        attn_halves = to_relative(attn_low)
        total = start_scatter(*[dot(a, w_out_own).astype(BF) for a in attn_halves])
        middle = tokens.astype(F32) + scatter_plane(total)
        unit, rate = norm_parts(middle)
        act_two = (unit * gain_two + shift_two).astype(BF)
        return attn_halves, middle, unit, rate, gather_own(act_two), row_grad

    attn_halves, middle, unit_two, rate_two, act_own, row_grad = stage(
        middle_stage,
        attn_low,
        w_out_own,
        gain_two,
        shift_two,
        tokens[0],
        (grad_low, grads_got, grads_passed),
    )

    over_first = (((0,), (1,)), ((), ()))
    over_second = (((1,), (0,)), ((), ()))

    def enter_stage(act_own, enter_slab, row_grad):
        act_other = swap(act_own, 1)
        entered = [dot(enter_slab, act, over_first) for act in (act_own, act_other)]
        hidden = [(jax.nn.silu(e[:units]) * e[units:]).astype(BF) for e in entered]
        grad_down = dot(
            row_grad, jnp.concatenate(hidden, axis=1), (((0,), (1,)), ((), ()))
        ).astype(BF)
        return act_other, entered, hidden, grad_down

    act_other, entered, hidden, grad_down = stage(enter_stage, act_own, enter_slab, row_grad)
    act_halves = (act_own, act_other)
    sum_down = sum_rows(grad_down, 0)

    def hidden_stage(act_halves, entered, row_grad, enter_slab, down_slab):
        enter_grads, act_parts = [], []
        for e, grad in zip(entered, jnp.split(row_grad, 2)):
            gate, upper = e[:units], e[units:]
            sig = jax.nn.sigmoid(gate)
            grad_hidden = dot(down_slab, grad, over_first)
            enter_grads.append(
                jnp.concatenate(
                    [
                        (grad_hidden * upper * sig * (1.0 + gate * (1.0 - sig))).astype(BF),
                        (grad_hidden * (gate * sig)).astype(BF),
                    ]
                )
            )
            act_parts.append(dot(enter_grads[-1], enter_slab, over_first).astype(BF))
        grad_enter = dot(
            jnp.concatenate(enter_grads, axis=1), jnp.concatenate(act_halves), over_second
        ).astype(BF)
        return start_scatter(*act_parts), grad_enter

    act_sum, grad_enter = stage(
        hidden_stage, act_halves, entered, row_grad, enter_slab, down_slab
    )
    sum_enter = sum_rows(grad_enter, 1)

    def norm_stage(act_sum, unit, rate, gain, grad_low, hidden, down_slab):
        got = scatter_first(act_sum)
        grad_act_two = scatter_last(act_sum, got, scatter_second(scatter_between(act_sum, got)))
        grad_norm = norm_back(grad_act_two, unit, rate, gain)
        return (
            grad_low.astype(F32) + grad_norm,
            jnp.sum(grad_act_two * unit, axis=0),
            jnp.sum(grad_act_two, axis=0),
            start_scatter(*[dot(h, down_slab, over_first).astype(BF) for h in hidden]),
        )

    grad_middle, grad_gain_two, grad_shift_two, mixed_sum = stage(
        norm_stage, act_sum, unit_two, rate_two, gain_two, grad_low, hidden, down_slab
    )


    def branch_stage(branch, sum_down):
        return gather_own(branch), sum_down.astype(F32)

    branch_own, out_down = stage(branch_stage, grad_middle.astype(BF), sum_down)
    branch_halves = (branch_own, swap(branch_own, 1))
    attn_own_grad = dot(branch_own, w_out_own, NT).astype(BF)

    def back_stage(
        branch_other, own_grad, w_out_own, first, q, k, v, attn_low, logs, tables, act_one, mixed_sum
    ):
        grad_attn = to_absolute(own_grad, dot(branch_other, w_out_own, NT).astype(BF))
        grad_proj = attend_back(first, q, k, v, attn_low, grad_attn, logs, tables)
        return grad_proj, dot(act_one, grad_proj, TN).astype(BF), scatter_first(mixed_sum)

    grad_proj, grad_w_qkv, mixed_got = stage(
        back_stage,
        branch_halves[1],
        attn_own_grad,
        w_out_own,
        first,
        q,
        k,
        v,
        attn_low,
        logs,
        tables,
        act_one,
        mixed_sum,
    )
    grad_proj, grad_w_qkv = after((grad_proj, grad_w_qkv), sum_enter)
    sum_qkv = sum_rows(grad_w_qkv, 0)

    attn_halves, branch_halves, mixed_got = after(
        (attn_halves, branch_halves, mixed_got), grad_w_qkv
    )
    grad_w_out = dot(attn_halves[0], branch_halves[0], TN)
    grad_w_out = (grad_w_out + dot(attn_halves[1], branch_halves[1], TN)).astype(BF)
    mixed_between = scatter_between(mixed_sum, mixed_got)
    if fast_out:
        sum_w_out = sum_rows(grad_w_out, 0)
    else:
        spread_out = lax.dynamic_update_index_in_dim(
            jnp.zeros((per, wide_n, HEAD_DIM, width), BF),
            grad_w_out.reshape(per, HEAD_DIM, width),
            me,
            1,
        )
        sum_w_out = lax.psum_scatter(
            spread_out.reshape(width, width), ALL, scatter_dimension=0, tiled=True
        )

    def last_stage(
        grad_proj, w_qkv_own, own, other, stats, gain, grad_middle, grad_gain_two, grad_shift_two,
        mixed_sum, mixed_got, mixed_between, middle,
    ):
        part_other, *sums_other = unproject(grad_proj, other, stats, w_qkv_own, 1)
        part_own, *sums_own = unproject(grad_proj, own, stats, w_qkv_own, 0)
        total = start_scatter(part_own, part_other)
        got = scatter_first(total)
        sums_own, sums_other, got = after((sums_own, sums_other, got))
        passed = scatter_second(scatter_between(total, got))
        total, got = after((total, got), *passed)
        grad_gain, grad_shift, grad_bias = (a + b for a, b in zip(sums_own, sums_other))
        full_bias = lax.dynamic_update_index_in_dim(
            jnp.zeros((3, per, wide_n, HEAD_DIM), F32),
            grad_bias.reshape(3, per, HEAD_DIM),
            me,
            2,
        )
        small = jnp.concatenate(
            [
                full_bias.reshape(devices, bias_slab),
                grad_gain.reshape(devices, slab),
                grad_shift.reshape(devices, slab),
                grad_gain_two.reshape(devices, slab),
                grad_shift_two.reshape(devices, slab),
            ],
            axis=1,
        )
        small = small.reshape(rows_n, wide_n, -1).transpose(1, 0, 2)
        sums = halve(small.reshape(wide_n, -1), "wide").reshape(rows_n, -1)
        rate = stats[:local, 1:2]
        unit = (own[:local].astype(F32) - stats[:local, 0:1]) * rate
        grad_act_one = scatter_last(total, got, passed)
        mixed_passed = scatter_second(mixed_between)
        if passed:
            mixed_passed = after(mixed_passed, *passed)
        mixed = scatter_last(mixed_sum, mixed_got, mixed_passed)
        return (
            (grad_middle + norm_back(grad_act_one, unit, rate, gain))[None],
            sums,
            (middle + mixed).astype(BF)[None],
        )

    grad_tokens, sums, result = stage(
        last_stage,
        after(grad_proj, grad_w_qkv, grad_w_out),
        w_qkv_own,
        own,
        other,
        stats,
        gain_one,
        grad_middle,
        grad_gain_two,
        grad_shift_two,
        mixed_sum,
        mixed_got,
        mixed_between,
        middle,
    )
    sum_enter = after(sum_enter, sums)
    out_gate, out_up = sum_enter[:units].T.astype(F32), sum_enter[units:].T.astype(F32)
    out_w_out = sum_w_out.astype(F32)
    part_qkv = lax.all_to_all(
        after(sum_qkv, sums).reshape(wide_n, slab, 3 * span), "wide", 0, 0, tiled=True
    )
    sums = halve(after(sums, sum_qkv), "rows")
    out_qkv = regroup_back(part_qkv[None])
    out_bias = sums[:bias_slab]
    small_outs = [
        sums[bias_slab + i * slab : bias_slab + (i + 1) * slab] for i in range(4)
    ]
    return (
        result,
        grad_tokens,
        out_qkv,
        out_bias,
        out_w_out,
        *small_outs,
        out_gate,
        out_up,
        out_down,
    )


def solution(mesh):
    by_token = P("rows", "wide", None)
    by_both = P(("rows", "wide"), None)
    vector = P(("rows", "wide"))
    by_slab = P("rows", "wide")
    in_specs = (
        by_token, P("rows", "wide"), by_both, vector, by_both, vector, vector, vector, vector,
        by_slab, by_slab, by_slab, by_token,
    )
    out_specs = (
        by_token, by_token, by_both, vector, by_both, vector, vector, vector, vector,
        by_slab, by_slab, by_slab,
    )
    return jax.shard_map(shards, mesh=mesh, in_specs=in_specs, out_specs=out_specs, check_vma=False)
```

```python
import functools
import math

import jax
import jax.numpy as jnp
from jax import lax
from jax.experimental import pallas as pl
from jax.experimental.pallas import tpu as pltpu
from jax.sharding import PartitionSpec as P

HEADS = 32
HEAD_DIM = 64
ROT = 16
PAIR = 2 * HEAD_DIM

epsilon = 1e-05
neg_large = -1e30
BF = jnp.bfloat16
F32 = jnp.float32
ALL = ("rows", "wide")
NT = (((1,), (1,)), ((), ()))
TN = (((0,), (0,)), ((), ()))


def dot(left, right, dims=(((1,), (0,)), ((), ()))):
    return lax.dot_general(left, right, dims, preferred_element_type=F32)


def swap(x, bit, axis="wide"):
    return lax.ppermute(x, axis, [(i, i ^ bit) for i in range(lax.axis_size(axis))])


def upper_bits():
    return [1 << k for k in range(1, lax.axis_size("wide").bit_length() - 1)]


def gather_first(x):
    bits = upper_bits()
    return tuple(swap(x, bit) for bit in bits) if len(bits) == 2 else ()


def gather_second(x, got):
    if not got:
        return ()
    one, two = upper_bits()
    half = x.shape[0] // 2
    return swap(got[1][:half], one), swap(got[0][half:], two)


def gather_third(x, got, passed):
    if got:
        return jnp.concatenate([x, *got, *passed])
    for bit in upper_bits():
        x = jnp.concatenate([x, swap(x, bit)])
    return x


def gather_last(x, got, passed):
    own = gather_third(x, got, passed)
    return own, swap(own, 1)


def gather_own(x):
    got = gather_first(x)
    return gather_third(x, got, gather_second(x, got))


def add_low(left, right):
    return (left.astype(F32) + right.astype(F32)).astype(BF)


def start_scatter(own, other):
    return add_low(lax.optimization_barrier(own), swap(other, 1))


def block_of(total, m, h):
    half = total.shape[0] // 8
    return total[(2 * m + h) * half : (2 * m + h + 1) * half]


def scatter_first(total):
    bits = upper_bits()
    if len(bits) != 2:
        return ()
    one, two = bits
    return (
        swap(block_of(total, 3, 0), one),
        swap(block_of(total, 3, 1), two),
        swap(block_of(total, 1, 0), one),
        swap(block_of(total, 2, 1), two),
    )


def scatter_between(total, got):
    if not got:
        return ()
    return add_low(block_of(total, 2, 0), got[0]), add_low(block_of(total, 1, 1), got[1])


def scatter_second(between):
    if not between:
        return ()
    one, two = upper_bits()
    return swap(between[0], two), swap(between[1], one)


def scatter_last(total, got, passed):
    if got:
        return jnp.concatenate(
            [
                block_of(total, 0, h).astype(F32) + got[2 + h].astype(F32) + passed[h].astype(F32)
                for h in range(2)
            ]
        )
    bits = upper_bits()
    for bit in reversed(bits[1:]):
        half = total.shape[0] // 2
        total = add_low(total[:half], swap(total[half:], bit))
    half = total.shape[0] // 2
    return total[:half].astype(F32) + swap(total[half:], bits[0]).astype(F32)


def scatter_plane(total):
    got = scatter_first(total)
    return scatter_last(total, got, scatter_second(scatter_between(total, got)))


def after(x, *others):
    return lax.optimization_barrier((x, others))[0]


def to_relative(x):
    count = lax.axis_size("wide")
    me = lax.axis_index("wide")
    blocks = x.reshape(count, x.shape[0] // count, x.shape[1])

    def pick(first):
        return jnp.concatenate(
            [
                lax.dynamic_index_in_dim(blocks, me ^ m, 0, keepdims=False)
                for m in range(first, count, 2)
            ]
        )

    return pick(0), pick(1)


def to_absolute(own, other):
    count = lax.axis_size("wide")
    me = lax.axis_index("wide")
    half = count // 2
    blocks = jnp.concatenate([own, other]).reshape(count, -1, own.shape[1])
    pieces = []
    for place in range(count):
        m = me ^ place
        pieces.append(
            lax.dynamic_index_in_dim(blocks, (m & 1) * half + (m >> 1), 0, keepdims=False)
        )
    return jnp.concatenate(pieces)


def halve(x, axis):
    count, me = lax.axis_size(axis), lax.axis_index(axis)
    width = x.shape[1]
    size = count // 2
    while size >= 1:
        side = (me // size) % 2
        halves = x.reshape(2, -1, width)
        keep = lax.dynamic_index_in_dim(halves, side, 0, keepdims=False)
        give = lax.dynamic_index_in_dim(halves, 1 - side, 0, keepdims=False)
        x = keep + swap(give, size, axis)
        size //= 2
    return x.reshape(width)


def turn_lanes(x, cosine, ahead, behind):
    half_rot = ROT // 2
    lanes = x.shape[-1]
    return (
        x * cosine
        + pltpu.roll(x, lanes - half_rot, 1) * ahead
        + pltpu.roll(x, half_rot, 1) * behind
    )


def project_kernel(
    order, own_ref, other_ref, gain, shift, weight, bias, cosine, ahead, behind,
    act, q, k, v, stats,
):
    half = pl.num_programs(0) // 2
    width = q.shape[1]
    x = jnp.where(pl.program_id(0) < half, own_ref[...], other_ref[...]).astype(F32)
    centre = jnp.mean(x, axis=1, keepdims=True)
    centred = x - centre
    rate = lax.rsqrt(jnp.mean(centred * centred, axis=1, keepdims=True) + epsilon)
    lane = lax.broadcasted_iota(jnp.int32, stats.shape, 1)
    stats[...] = jnp.where(lane == 0, centre, rate)
    normed = (centred * rate * gain[...] + shift[...]).astype(BF)
    act[...] = normed
    projected = dot(normed, weight[...]) + bias[...]
    for at in range(0, width, PAIR):
        angles = (cosine[...], ahead[...], behind[...])
        q[:, at : at + PAIR] = turn_lanes(projected[:, at : at + PAIR], *angles).astype(BF)
        k[:, at : at + PAIR] = turn_lanes(
            projected[:, width + at : width + at + PAIR], *angles
        ).astype(BF)
    v[...] = projected[:, 2 * width :].astype(BF)


def project(own, other, gain, shift, weight, bias, tables):
    count = lax.axis_size("wide")
    half = count // 2
    rows = own.shape[0] // half
    depth, columns = weight.shape
    width = columns // 3
    total = rows * count
    me = lax.axis_index("wide")
    order = jnp.stack([me ^ m for m in list(range(0, count, 2)) + list(range(1, count, 2))])

    def whole(i, order):
        return (0, 0)

    def placed(i, order):
        return (order[i], 0)

    vec = pl.BlockSpec((1, depth), whole)
    table = pl.BlockSpec((rows, PAIR), placed)
    out = pl.BlockSpec((rows, width), placed)
    return pl.pallas_call(
        project_kernel,
        grid_spec=pltpu.PrefetchScalarGridSpec(
            num_scalar_prefetch=1,
            grid=(count,),
            in_specs=[
                pl.BlockSpec((rows, depth), lambda i, order: (jnp.minimum(i, half - 1), 0)),
                pl.BlockSpec((rows, depth), lambda i, order: (jnp.maximum(i - half, 0), 0)),
                vec,
                vec,
                pl.BlockSpec((depth, columns), whole),
                pl.BlockSpec((1, columns), whole),
                table,
                table,
                table,
            ],
            out_specs=[
                pl.BlockSpec((rows, depth), placed),
                out,
                out,
                out,
                pl.BlockSpec((rows, PAIR), lambda i, order: (i, 0)),
            ],
        ),
        out_shape=[
            jax.ShapeDtypeStruct((total, depth), BF),
            jax.ShapeDtypeStruct((total, width), BF),
            jax.ShapeDtypeStruct((total, width), BF),
            jax.ShapeDtypeStruct((total, width), BF),
            jax.ShapeDtypeStruct((total, PAIR), F32),
        ],
        cost_estimate=pl.CostEstimate(flops=17 * 10**9, bytes_accessed=1, transcendentals=0),
        compiler_params=pltpu.CompilerParams(
            dimension_semantics=("arbitrary",), vmem_limit_bytes=48 * 2**20
        ),
        name="project",
    )(order, own, other, gain, shift, weight, bias, *tables)


def unproject_kernel(order, g_ref, x_ref, stats, weight, out, gain, shift, bias, held):
    half = order.shape[0]
    rows = held.shape[0] // half

    @pl.when(pl.program_id(0) == 0)
    def _():
        for i in range(half):
            start = pl.multiple_of(order[i] * rows, rows)
            held[i * rows : (i + 1) * rows, :] = g_ref[pl.ds(start, rows), :]
        bias[...] = jnp.sum(held[...].astype(F32), axis=0, keepdims=True)

    unit = (x_ref[...].astype(F32) - stats[:, 0:1]) * stats[:, 1:2]
    incoming = dot(held[...], weight[...], NT)
    out[...] = incoming.astype(BF)
    gain[...] = jnp.sum(incoming * unit, axis=0, keepdims=True)
    shift[...] = jnp.sum(incoming, axis=0, keepdims=True)


def unproject(grads, x, stats, weight, first):
    count = lax.axis_size("wide")
    total = x.shape[0]
    depth, columns = weight.shape
    block = math.gcd(depth, 512)
    order = jnp.stack([lax.axis_index("wide") ^ m for m in range(first, count, 2)])
    vec = pl.BlockSpec((1, block), lambda j, order: (0, j))
    return pl.pallas_call(
        unproject_kernel,
        grid_spec=pltpu.PrefetchScalarGridSpec(
            num_scalar_prefetch=1,
            grid=(depth // block,),
            in_specs=[
                pl.BlockSpec(grads.shape, lambda j, order: (0, 0)),
                pl.BlockSpec((total, block), lambda j, order: (0, j)),
                pl.BlockSpec((total, PAIR), lambda j, order: (first, 0)),
                pl.BlockSpec((block, columns), lambda j, order: (j, 0)),
            ],
            out_specs=[
                pl.BlockSpec((total, block), lambda j, order: (0, j)),
                vec,
                vec,
                pl.BlockSpec((1, columns), lambda j, order: (0, 0)),
            ],
            scratch_shapes=[pltpu.VMEM((total, columns), BF)],
        ),
        out_shape=[
            jax.ShapeDtypeStruct((total, depth), BF),
            jax.ShapeDtypeStruct((1, depth), F32),
            jax.ShapeDtypeStruct((1, depth), F32),
            jax.ShapeDtypeStruct((1, columns), F32),
        ],
        cost_estimate=pl.CostEstimate(flops=7 * 10**9, bytes_accessed=1, transcendentals=0),
        compiler_params=pltpu.CompilerParams(
            dimension_semantics=("arbitrary",), vmem_limit_bytes=48 * 2**20
        ),
        name="unproject",
    )(order, grads, x, stats, weight)


def head_mask(head, shape):
    lane = lax.broadcasted_iota(jnp.int32, shape, 1)
    return (lane // HEAD_DIM) == head


def attend_kernel(first, q_ref, k_ref, v_ref, o_ref, log_ref, v_turned):
    block = q_ref.shape[0]
    at = pl.program_id(1)
    scale = HEAD_DIM ** (-0.5)

    @pl.when(at == 0)
    def _():
        v_turned[...] = v_ref[...].astype(F32).T.astype(BF)

    q = q_ref[...] * jnp.asarray(scale, BF)
    queries = [jnp.where(head_mask(h, q.shape), q, jnp.zeros_like(q)) for h in range(2)]
    own_first = first[...]
    own_place = at * block + lax.broadcasted_iota(jnp.int32, (1, block), 1)

    def step(number, state):
        keys = k_ref[pl.ds(number * block, block), :]
        values = v_turned[:, pl.ds(number * block, block)]
        place = number * block + lax.broadcasted_iota(jnp.int32, (block, block), 0)
        visible = (place >= own_first) & (place <= own_place)
        out = []
        for h in range(2):
            peak, total, mix = state[h]
            scores = jnp.where(visible, dot(keys, queries[h], NT), neg_large)
            new_peak = jnp.maximum(peak, jnp.max(scores, axis=0, keepdims=True))
            terms = jnp.exp(scores - new_peak)
            decay = jnp.exp(peak - new_peak)
            out.append(
                (
                    new_peak,
                    total * decay + jnp.sum(terms, axis=0, keepdims=True),
                    mix * decay
                    + dot(values[h * HEAD_DIM : (h + 1) * HEAD_DIM], terms.astype(BF)),
                )
            )
        return tuple(out)

    start = (
        jnp.full((1, block), neg_large, F32),
        jnp.zeros((1, block), F32),
        jnp.zeros((HEAD_DIM, block), F32),
    )
    state = lax.fori_loop(0, at + 1, step, (start, start))
    mixes = []
    for h in range(2):
        peak, total, mix = state[h]
        mixes.append(mix / total)
        log_ref[0, h : h + 1, :] = peak + jnp.log(total)
    o_ref[...] = jnp.concatenate(mixes, axis=0).T.astype(BF)


def attend(first, q, k, v):
    total, width = q.shape
    pairs = width // PAIR
    block = math.gcd(total, 256)
    return pl.pallas_call(
        attend_kernel,
        grid=(pairs, total // block),
        in_specs=[
            pl.BlockSpec((1, block), lambda p, i: (0, i)),
            pl.BlockSpec((block, PAIR), lambda p, i: (i, p)),
            pl.BlockSpec((total, PAIR), lambda p, i: (0, p)),
            pl.BlockSpec((total, PAIR), lambda p, i: (0, p)),
        ],
        out_specs=[
            pl.BlockSpec((block, PAIR), lambda p, i: (i, p)),
            pl.BlockSpec((1, 2, block), lambda p, i: (p, 0, i)),
        ],
        out_shape=[
            jax.ShapeDtypeStruct((total, width), BF),
            jax.ShapeDtypeStruct((pairs, 2, total), F32),
        ],
        scratch_shapes=[pltpu.VMEM((PAIR, total), BF)],
        cost_estimate=pl.CostEstimate(flops=39 * 10**9, bytes_accessed=1, transcendentals=0),
        compiler_params=pltpu.CompilerParams(
            dimension_semantics=("arbitrary", "arbitrary"), vmem_limit_bytes=32 * 2**20
        ),
        name="attend",
    )(first, q, k, v)


def attend_back_kernel(
    first, q_ref, k_ref, v_ref, o_ref, g_ref, log_ref, cosine, ahead, behind,
    out_ref, k_turned, delta, sum_q, sum_k, sum_v,
):
    block, width = k_ref.shape
    pairs = width // PAIR
    at = pl.program_id(0)
    last = pl.num_programs(0)
    scale = HEAD_DIM ** (-0.5)
    k_turned[...] = k_ref[...].astype(F32).T.astype(BF)

    @pl.when(at == 0)
    def _():
        sum_q[...] = jnp.zeros_like(sum_q)

        def fill(number, carry):
            spot = pl.ds(number * block, block)
            both = (g_ref[spot, :].astype(F32) * o_ref[spot, :].astype(F32)).T
            for h in range(2 * pairs):
                delta[h : h + 1, spot] = jnp.sum(
                    both[h * HEAD_DIM : (h + 1) * HEAD_DIM], axis=0, keepdims=True
                )
            return carry

        lax.fori_loop(0, last, fill, 0)

    place = at * block + lax.broadcasted_iota(jnp.int32, (block, block), 0)

    def step(number, carry):
        spot = pl.ds(number * block, block)
        own_place = number * block + lax.broadcasted_iota(jnp.int32, (1, block), 1)
        visible = (place >= first[:, spot]) & (place <= own_place)
        for p in range(pairs):
            pair = slice(p * PAIR, (p + 1) * PAIR)
            q = q_ref[spot, pair] * jnp.asarray(scale, BF)
            g = g_ref[spot, pair]
            k, v = k_ref[:, pair], v_ref[:, pair]
            more_k = more_v = 0.0
            for h in range(2):
                mask = head_mask(h, q.shape)
                q_head = jnp.where(mask, q, jnp.zeros_like(q))
                g_head = jnp.where(mask, g, jnp.zeros_like(g))
                scores = dot(k, q_head, NT)
                probs = jnp.exp(
                    jnp.where(visible, scores - log_ref[p, h : h + 1, spot], neg_large)
                )
                slopes = dot(v, g_head, NT)
                head = 2 * p + h
                low = (probs * (slopes - delta[head : head + 1, spot])).astype(BF)
                more_v = more_v + dot(probs.astype(BF), g_head)
                more_k = more_k + dot(low, q_head)
                span = slice(head * HEAD_DIM, (head + 1) * HEAD_DIM)
                sum_q[span, spot] += dot(k_turned[span, :], low)
            sum_k[:, pair] += more_k
            sum_v[:, pair] += more_v
        return carry

    sum_k[...] = jnp.zeros_like(sum_k)
    sum_v[...] = jnp.zeros_like(sum_v)
    lax.fori_loop(at, last, step, 0)
    mine = pl.ds(at * block, block)
    out_ref[mine, 2 * width :] = sum_v[...].astype(BF)
    for p in range(pairs):
        start = width + p * PAIR
        out_ref[mine, start : start + PAIR] = turn_lanes(
            sum_k[:, p * PAIR : (p + 1) * PAIR],
            cosine[mine, :],
            -ahead[mine, :],
            -behind[mine, :],
        ).astype(BF)

    @pl.when(at == last - 1)
    def _():
        def finish(number, carry):
            spot = pl.ds(number * block, block)
            for p in range(pairs):
                pair = slice(p * PAIR, (p + 1) * PAIR)
                out_ref[spot, pair] = turn_lanes(
                    sum_q[pair, spot].T * scale,
                    cosine[spot, :],
                    -ahead[spot, :],
                    -behind[spot, :],
                ).astype(BF)
            return carry

        lax.fori_loop(0, last, finish, 0)


def attend_back(first, q, k, v, o, g, logs, tables):
    total, width = q.shape
    block = math.gcd(total, 256)

    def whole(*shape):
        return pl.BlockSpec(shape, lambda i: (0,) * len(shape))

    part = pl.BlockSpec((block, width), lambda i: (i, 0))
    return pl.pallas_call(
        attend_back_kernel,
        grid=(total // block,),
        in_specs=[
            whole(1, total),
            whole(total, width),
            part,
            part,
            whole(total, width),
            whole(total, width),
            whole(*logs.shape),
            whole(total, PAIR),
            whole(total, PAIR),
            whole(total, PAIR),
        ],
        out_specs=whole(total, 3 * width),
        out_shape=jax.ShapeDtypeStruct((total, 3 * width), BF),
        scratch_shapes=[
            pltpu.VMEM((width, block), BF),
            pltpu.VMEM((width // HEAD_DIM, total), F32),
            pltpu.VMEM((width, total), F32),
            pltpu.VMEM((block, width), F32),
            pltpu.VMEM((block, width), F32),
        ],
        cost_estimate=pl.CostEstimate(flops=44 * 10**9, bytes_accessed=1, transcendentals=0),
        compiler_params=pltpu.CompilerParams(
            dimension_semantics=("arbitrary",), vmem_limit_bytes=48 * 2**20
        ),
        name="attend_back",
    )(first, q, k, v, o, g, logs, *tables)


def regroup_kernel(x_ref, o_ref):
    count, rows, width = o_ref.shape
    groups = width // HEAD_DIM
    for w in range(count):
        for g in range(0, groups, 2):
            pieces = []
            for j in (g, g + 1):
                at = (j * count + w) * HEAD_DIM
                base = at // PAIR * PAIR
                pair = x_ref[:, base : base + PAIR].astype(F32)
                pieces.append(pair[:, at - base : at - base + HEAD_DIM])
            o_ref[w, :, g * HEAD_DIM : g * HEAD_DIM + PAIR] = jnp.concatenate(
                pieces, axis=1
            ).astype(o_ref.dtype)


def regroup(x, count):
    rows, columns = x.shape
    return pl.pallas_call(
        regroup_kernel,
        out_shape=jax.ShapeDtypeStruct((count, rows, columns // count), x.dtype),
        compiler_params=pltpu.CompilerParams(vmem_limit_bytes=16 * 2**20),
        name="regroup",
    )(x)


def regroup_back_kernel(x_ref, o_ref):
    parts, count, rows, width = x_ref.shape
    for g in range(width // HEAD_DIM):
        base = g * HEAD_DIM // PAIR * PAIR
        shift = g * HEAD_DIM - base
        for w in range(0, count, 2):
            pieces = []
            for j in (w, w + 1):
                total = x_ref[0, j, :, base : base + PAIR].astype(F32)
                for part in range(1, parts):
                    total = total + x_ref[part, j, :, base : base + PAIR].astype(F32)
                pieces.append(total[:, shift : shift + HEAD_DIM])
            at = (g * count + w) * HEAD_DIM
            o_ref[:, at : at + PAIR] = jnp.concatenate(pieces, axis=1)


def regroup_back(x):
    parts, count, rows, width = x.shape
    return pl.pallas_call(
        regroup_back_kernel,
        out_shape=jax.ShapeDtypeStruct((rows, count * width), F32),
        compiler_params=pltpu.CompilerParams(vmem_limit_bytes=16 * 2**20),
        name="regroup_back",
    )(x)


def norm_parts(values):
    centred = values - jnp.mean(values, axis=-1, keepdims=True)
    spread = jnp.mean(centred * centred, axis=-1, keepdims=True)
    rate = lax.rsqrt(spread + epsilon)
    return centred * rate, rate


def norm_back(incoming, unit, rate, gain):
    scaled = incoming * gain
    return rate * (
        scaled
        - jnp.mean(scaled, axis=-1, keepdims=True)
        - unit * jnp.mean(scaled * unit, axis=-1, keepdims=True)
    )


def shards(
    tokens,
    segments,
    w_qkv,
    b_qkv,
    w_out,
    ln1_gain,
    ln1_bias,
    ln2_gain,
    ln2_bias,
    w_gate,
    w_up,
    w_down,
    out_grad,
):
    rows_n, wide_n = lax.axis_size("rows"), lax.axis_size("wide")
    me_row, me = lax.axis_index("rows"), lax.axis_index("wide")
    devices = rows_n * wide_n
    local = tokens.shape[1]
    width = tokens.shape[2]
    row_len = local * wide_n
    per = HEADS // wide_n
    span = per * HEAD_DIM
    slab = width // devices
    bias_slab = 3 * width // devices

    def stage(run, *args):
        shapes = jax.eval_shape(run, *args)

        def blank(*args):
            return jax.tree.map(lambda x: jnp.zeros(x.shape, x.dtype), shapes)

        return lax.cond(segments[0, 0] >= 0, run, blank, *args)

    def sum_rows(x, dim):
        return lax.psum_scatter(x, "rows", scatter_dimension=dim, tiled=True)

    fast_out = slab == HEAD_DIM and per == rows_n
    if fast_out:
        w_out_own = lax.all_gather(w_out, "rows", axis=0, tiled=True)
    else:
        w_out_own = lax.dynamic_index_in_dim(
            lax.all_gather(w_out, ALL, axis=0, tiled=True).reshape(
                per, wide_n, HEAD_DIM, width
            ),
            me,
            1,
            keepdims=False,
        ).reshape(span, width)
    w_qkv_part = lax.all_to_all(
        regroup(w_qkv, wide_n), "wide", 0, 0, tiled=True
    ).reshape(wide_n * slab, 3 * span)
    w_qkv_own = lax.all_gather(w_qkv_part, "rows", axis=0, tiled=True)
    units = w_gate.shape[1]
    enter_slab = lax.all_gather(
        jnp.concatenate([w_gate, w_up], axis=1), "rows", axis=0, tiled=True
    )
    down_slab = lax.all_gather(w_down, "rows", axis=0, tiled=True)

    grad_low = out_grad[0]

    def first_stage(b_qkv, ln1_gain, ln1_bias, ln2_gain, ln2_bias, segs, tokens):
        packed = jnp.concatenate([b_qkv, ln1_gain, ln1_bias, ln2_gain, ln2_bias, segs])
        small = lax.all_gather(lax.all_gather(packed, "rows"), "wide")
        got = gather_first(tokens)
        own, other = gather_last(
            tokens, got, gather_second(tokens, after(got, small) if got else got)
        )
        flat = small.transpose(1, 0, 2)

        def vector(start, size):
            return flat[:, :, start : start + size].reshape(1, devices * size).astype(F32)

        row_segs = lax.dynamic_index_in_dim(small, me_row, 1, keepdims=False)[
            :, bias_slab + 4 * slab :
        ].reshape(row_len)
        own_bias = lax.dynamic_index_in_dim(
            vector(0, bias_slab).reshape(3, per, wide_n, HEAD_DIM), me, 2, keepdims=False
        ).reshape(1, 3 * span)

        doc_first = jnp.sum((row_segs[:, None] < row_segs[None, :]).astype(jnp.int32), axis=0)
        positions = jnp.arange(row_len, dtype=jnp.int32) - doc_first
        freqs = 10000.0 ** (-2.0 * jnp.arange(ROT // 2, dtype=F32) / ROT)
        lane = jnp.arange(PAIR) % HEAD_DIM
        lane_freqs = jnp.where(lane < ROT, jnp.tile(freqs, PAIR // (ROT // 2)), 0.0)
        angles = positions.astype(F32)[:, None] * lane_freqs[None, :]
        sine = jnp.sin(angles)
        half_rot = ROT // 2
        tables = (
            jnp.cos(angles),
            jnp.where(lane < half_rot, -sine, 0.0),
            jnp.where((lane >= half_rot) & (lane < ROT), sine, 0.0),
        )
        gains = tuple(vector(bias_slab + i * slab, slab) for i in range(4))
        return own, other, own_bias, gains, doc_first.reshape(1, row_len), tables

    own, other, own_bias, gains, first, tables = stage(
        first_stage,
        after(b_qkv, w_qkv_part),
        ln1_gain,
        ln1_bias,
        ln2_gain,
        ln2_bias,
        segments[0].astype(BF),
        tokens[0],
    )
    gain_one, shift_one, gain_two, shift_two = gains
    grads_got = gather_first(after(grad_low, own))

    act_one, q, k, v, stats = project(
        after(own, w_out_own), other, gain_one, shift_one, w_qkv_own, own_bias, tables
    )
    grads_passed = gather_second(grad_low, grads_got)
    attn_low, logs = attend(first, after(q, *grads_got), k, v)
    attn_low = after(attn_low, *grads_passed)

    def middle_stage(attn_low, w_out_own, gain_two, shift_two, tokens, grads):
        row_grad = jnp.concatenate(gather_last(*grads))
        attn_halves = to_relative(attn_low)
        total = start_scatter(*[dot(a, w_out_own).astype(BF) for a in attn_halves])
        middle = tokens.astype(F32) + scatter_plane(total)
        unit, rate = norm_parts(middle)
        act_two = (unit * gain_two + shift_two).astype(BF)
        return attn_halves, middle, unit, rate, gather_own(act_two), row_grad

    attn_halves, middle, unit_two, rate_two, act_own, row_grad = middle_stage(
        attn_low,
        w_out_own,
        gain_two,
        shift_two,
        tokens[0],
        (grad_low, grads_got, grads_passed),
    )

    over_first = (((0,), (1,)), ((), ()))
    over_second = (((1,), (0,)), ((), ()))

    def enter_stage(act_own, enter_slab, row_grad):
        act_other = swap(act_own, 1)
        entered = [dot(enter_slab, act, over_first) for act in (act_own, act_other)]
        hidden = [(jax.nn.silu(e[:units]) * e[units:]).astype(BF) for e in entered]
        grad_down = dot(
            row_grad, jnp.concatenate(hidden, axis=1), (((0,), (1,)), ((), ()))
        ).astype(BF)
        return act_other, entered, hidden, grad_down

    act_other, entered, hidden, grad_down = stage(enter_stage, act_own, enter_slab, row_grad)
    act_halves = (act_own, act_other)
    sum_down = sum_rows(grad_down, 0)

    def hidden_stage(act_halves, entered, row_grad, enter_slab, down_slab):
        enter_grads, act_parts = [], []
        for e, grad in zip(entered, jnp.split(row_grad, 2)):
            gate, upper = e[:units], e[units:]
            sig = jax.nn.sigmoid(gate)
            grad_hidden = dot(down_slab, grad, over_first)
            enter_grads.append(
                jnp.concatenate(
                    [
                        (grad_hidden * upper * sig * (1.0 + gate * (1.0 - sig))).astype(BF),
                        (grad_hidden * (gate * sig)).astype(BF),
                    ]
                )
            )
            act_parts.append(dot(enter_grads[-1], enter_slab, over_first).astype(BF))
        grad_enter = dot(
            jnp.concatenate(enter_grads, axis=1), jnp.concatenate(act_halves), over_second
        ).astype(BF)
        return start_scatter(*act_parts), grad_enter

    act_sum, grad_enter = stage(
        hidden_stage, act_halves, entered, row_grad, enter_slab, down_slab
    )
    sum_enter = sum_rows(grad_enter, 1)

    def norm_stage(act_sum, unit, rate, gain, grad_low, hidden, down_slab):
        got = scatter_first(act_sum)
        grad_act_two = scatter_last(act_sum, got, scatter_second(scatter_between(act_sum, got)))
        grad_norm = norm_back(grad_act_two, unit, rate, gain)
        return (
            grad_low.astype(F32) + grad_norm,
            jnp.sum(grad_act_two * unit, axis=0),
            jnp.sum(grad_act_two, axis=0),
            start_scatter(*[dot(h, down_slab, over_first).astype(BF) for h in hidden]),
        )

    grad_middle, grad_gain_two, grad_shift_two, mixed_sum = stage(
        norm_stage, act_sum, unit_two, rate_two, gain_two, grad_low, hidden, down_slab
    )


    def branch_stage(branch, sum_down):
        return gather_own(branch), sum_down.astype(F32)

    branch_own, out_down = stage(branch_stage, grad_middle.astype(BF), sum_down)
    branch_halves = (branch_own, swap(branch_own, 1))
    attn_own_grad = dot(branch_own, w_out_own, NT).astype(BF)

    def back_stage(
        branch_other, own_grad, w_out_own, first, q, k, v, attn_low, logs, tables, act_one, mixed_sum
    ):
        grad_attn = to_absolute(own_grad, dot(branch_other, w_out_own, NT).astype(BF))
        grad_proj = attend_back(first, q, k, v, attn_low, grad_attn, logs, tables)
        return grad_proj, dot(act_one, grad_proj, TN).astype(BF), scatter_first(mixed_sum)

    grad_proj, grad_w_qkv, mixed_got = stage(
        back_stage,
        branch_halves[1],
        attn_own_grad,
        w_out_own,
        first,
        q,
        k,
        v,
        attn_low,
        logs,
        tables,
        act_one,
        mixed_sum,
    )
    grad_proj, grad_w_qkv = after((grad_proj, grad_w_qkv), sum_enter)
    sum_qkv = sum_rows(grad_w_qkv, 0)

    attn_halves, branch_halves, mixed_got = after(
        (attn_halves, branch_halves, mixed_got), grad_w_qkv
    )
    grad_w_out = dot(attn_halves[0], branch_halves[0], TN)
    grad_w_out = (grad_w_out + dot(attn_halves[1], branch_halves[1], TN)).astype(BF)
    mixed_between = scatter_between(mixed_sum, mixed_got)
    if fast_out:
        sum_w_out = sum_rows(grad_w_out, 0)
    else:
        spread_out = lax.dynamic_update_index_in_dim(
            jnp.zeros((per, wide_n, HEAD_DIM, width), BF),
            grad_w_out.reshape(per, HEAD_DIM, width),
            me,
            1,
        )
        sum_w_out = lax.psum_scatter(
            spread_out.reshape(width, width), ALL, scatter_dimension=0, tiled=True
        )

    def last_stage(
        grad_proj, w_qkv_own, own, other, stats, gain, grad_middle, grad_gain_two, grad_shift_two,
        mixed_sum, mixed_got, mixed_between, middle,
    ):
        part_other, *sums_other = unproject(grad_proj, other, stats, w_qkv_own, 1)
        part_own, *sums_own = unproject(grad_proj, own, stats, w_qkv_own, 0)
        total = start_scatter(part_own, part_other)
        got = scatter_first(total)
        sums_own, sums_other, got = after((sums_own, sums_other, got))
        passed = scatter_second(scatter_between(total, got))
        total, got = after((total, got), *passed)
        grad_gain, grad_shift, grad_bias = (a + b for a, b in zip(sums_own, sums_other))
        full_bias = lax.dynamic_update_index_in_dim(
            jnp.zeros((3, per, wide_n, HEAD_DIM), F32),
            grad_bias.reshape(3, per, HEAD_DIM),
            me,
            2,
        )
        small = jnp.concatenate(
            [
                full_bias.reshape(devices, bias_slab),
                grad_gain.reshape(devices, slab),
                grad_shift.reshape(devices, slab),
                grad_gain_two.reshape(devices, slab),
                grad_shift_two.reshape(devices, slab),
            ],
            axis=1,
        )
        small = small.reshape(rows_n, wide_n, -1).transpose(1, 0, 2)
        sums = halve(small.reshape(wide_n, -1), "wide").reshape(rows_n, -1)
        rate = stats[:local, 1:2]
        unit = (own[:local].astype(F32) - stats[:local, 0:1]) * rate
        grad_act_one = scatter_last(total, got, passed)
        mixed_passed = scatter_second(mixed_between)
        if passed:
            mixed_passed = after(mixed_passed, *passed)
        mixed = scatter_last(mixed_sum, mixed_got, mixed_passed)
        return (
            (grad_middle + norm_back(grad_act_one, unit, rate, gain))[None],
            sums,
            (middle + mixed).astype(BF)[None],
        )

    grad_tokens, sums, result = stage(
        last_stage,
        after(grad_proj, grad_w_qkv, grad_w_out),
        w_qkv_own,
        own,
        other,
        stats,
        gain_one,
        grad_middle,
        grad_gain_two,
        grad_shift_two,
        mixed_sum,
        mixed_got,
        mixed_between,
        middle,
    )
    sum_enter = after(sum_enter, sums)
    out_gate, out_up = sum_enter[:units].T.astype(F32), sum_enter[units:].T.astype(F32)
    out_w_out = sum_w_out.astype(F32)
    part_qkv = lax.all_to_all(
        after(sum_qkv, sums).reshape(wide_n, slab, 3 * span), "wide", 0, 0, tiled=True
    )
    sums = halve(after(sums, sum_qkv), "rows")
    out_qkv = regroup_back(part_qkv[None])
    out_bias = sums[:bias_slab]
    small_outs = [
        sums[bias_slab + i * slab : bias_slab + (i + 1) * slab] for i in range(4)
    ]
    return (
        result,
        grad_tokens,
        out_qkv,
        out_bias,
        out_w_out,
        *small_outs,
        out_gate,
        out_up,
        out_down,
    )


def solution(mesh):
    by_token = P("rows", "wide", None)
    by_both = P(("rows", "wide"), None)
    vector = P(("rows", "wide"))
    by_slab = P("rows", "wide")
    in_specs = (
        by_token, P("rows", "wide"), by_both, vector, by_both, vector, vector, vector, vector,
        by_slab, by_slab, by_slab, by_token,
    )
    out_specs = (
        by_token, by_token, by_both, vector, by_both, vector, vector, vector, vector,
        by_slab, by_slab, by_slab,
    )
    return jax.shard_map(shards, mesh=mesh, in_specs=in_specs, out_specs=out_specs, check_vma=False)
```

```python
import functools
import math

import jax
import jax.numpy as jnp
from jax import lax
from jax.experimental import pallas as pl
from jax.experimental.pallas import tpu as pltpu
from jax.sharding import PartitionSpec as P

HEADS = 32
HEAD_DIM = 64
ROT = 16
PAIR = 2 * HEAD_DIM

epsilon = 1e-05
neg_large = -1e30
BF = jnp.bfloat16
F32 = jnp.float32
ALL = ("rows", "wide")
NT = (((1,), (1,)), ((), ()))
TN = (((0,), (0,)), ((), ()))


def dot(left, right, dims=(((1,), (0,)), ((), ()))):
    return lax.dot_general(left, right, dims, preferred_element_type=F32)


def swap(x, bit, axis="wide"):
    return lax.ppermute(x, axis, [(i, i ^ bit) for i in range(lax.axis_size(axis))])


def upper_bits():
    return [1 << k for k in range(1, lax.axis_size("wide").bit_length() - 1)]


def gather_first(x):
    bits = upper_bits()
    return tuple(swap(x, bit) for bit in bits) if len(bits) == 2 else ()


def gather_second(x, got):
    if not got:
        return ()
    one, two = upper_bits()
    half = x.shape[0] // 2
    return swap(got[1][:half], one), swap(got[0][half:], two)


def gather_third(x, got, passed):
    if got:
        return jnp.concatenate([x, *got, *passed])
    for bit in upper_bits():
        x = jnp.concatenate([x, swap(x, bit)])
    return x


def gather_last(x, got, passed):
    own = gather_third(x, got, passed)
    return own, swap(own, 1)


def gather_own(x):
    got = gather_first(x)
    return gather_third(x, got, gather_second(x, got))


def add_low(left, right):
    return (left.astype(F32) + right.astype(F32)).astype(BF)


def start_scatter(own, other):
    return add_low(lax.optimization_barrier(own), swap(other, 1))


def block_of(total, m, h):
    half = total.shape[0] // 8
    return total[(2 * m + h) * half : (2 * m + h + 1) * half]


def scatter_first(total):
    bits = upper_bits()
    if len(bits) != 2:
        return ()
    one, two = bits
    return (
        swap(block_of(total, 3, 0), one),
        swap(block_of(total, 3, 1), two),
        swap(block_of(total, 1, 0), one),
        swap(block_of(total, 2, 1), two),
    )


def scatter_between(total, got):
    if not got:
        return ()
    return add_low(block_of(total, 2, 0), got[0]), add_low(block_of(total, 1, 1), got[1])


def scatter_second(between):
    if not between:
        return ()
    one, two = upper_bits()
    return swap(between[0], two), swap(between[1], one)


def scatter_last(total, got, passed):
    if got:
        return jnp.concatenate(
            [
                block_of(total, 0, h).astype(F32) + got[2 + h].astype(F32) + passed[h].astype(F32)
                for h in range(2)
            ]
        )
    bits = upper_bits()
    for bit in reversed(bits[1:]):
        half = total.shape[0] // 2
        total = add_low(total[:half], swap(total[half:], bit))
    half = total.shape[0] // 2
    return total[:half].astype(F32) + swap(total[half:], bits[0]).astype(F32)


def scatter_plane(total):
    got = scatter_first(total)
    return scatter_last(total, got, scatter_second(scatter_between(total, got)))


def after(x, *others):
    return lax.optimization_barrier((x, others))[0]


def to_relative(x):
    count = lax.axis_size("wide")
    me = lax.axis_index("wide")
    blocks = x.reshape(count, x.shape[0] // count, x.shape[1])

    def pick(first):
        return jnp.concatenate(
            [
                lax.dynamic_index_in_dim(blocks, me ^ m, 0, keepdims=False)
                for m in range(first, count, 2)
            ]
        )

    return pick(0), pick(1)


def to_absolute(own, other):
    count = lax.axis_size("wide")
    me = lax.axis_index("wide")
    half = count // 2
    blocks = jnp.concatenate([own, other]).reshape(count, -1, own.shape[1])
    pieces = []
    for place in range(count):
        m = me ^ place
        pieces.append(
            lax.dynamic_index_in_dim(blocks, (m & 1) * half + (m >> 1), 0, keepdims=False)
        )
    return jnp.concatenate(pieces)


def halve(x, axis):
    count, me = lax.axis_size(axis), lax.axis_index(axis)
    width = x.shape[1]
    size = count // 2
    while size >= 1:
        side = (me // size) % 2
        halves = x.reshape(2, -1, width)
        keep = lax.dynamic_index_in_dim(halves, side, 0, keepdims=False)
        give = lax.dynamic_index_in_dim(halves, 1 - side, 0, keepdims=False)
        x = keep + swap(give, size, axis)
        size //= 2
    return x.reshape(width)


def turn_lanes(x, cosine, ahead, behind):
    half_rot = ROT // 2
    lanes = x.shape[-1]
    return (
        x * cosine
        + pltpu.roll(x, lanes - half_rot, 1) * ahead
        + pltpu.roll(x, half_rot, 1) * behind
    )


def project_kernel(
    order, own_ref, other_ref, gain, shift, weight, bias, cosine, ahead, behind,
    act, q, k, v, stats,
):
    half = pl.num_programs(0) // 2
    width = q.shape[1]
    x = jnp.where(pl.program_id(0) < half, own_ref[...], other_ref[...]).astype(F32)
    centre = jnp.mean(x, axis=1, keepdims=True)
    centred = x - centre
    rate = lax.rsqrt(jnp.mean(centred * centred, axis=1, keepdims=True) + epsilon)
    lane = lax.broadcasted_iota(jnp.int32, stats.shape, 1)
    stats[...] = jnp.where(lane == 0, centre, rate)
    normed = (centred * rate * gain[...] + shift[...]).astype(BF)
    act[...] = normed
    projected = dot(normed, weight[...]) + bias[...]
    for at in range(0, width, PAIR):
        angles = (cosine[...], ahead[...], behind[...])
        q[:, at : at + PAIR] = turn_lanes(projected[:, at : at + PAIR], *angles).astype(BF)
        k[:, at : at + PAIR] = turn_lanes(
            projected[:, width + at : width + at + PAIR], *angles
        ).astype(BF)
    v[...] = projected[:, 2 * width :].astype(BF)


def project(own, other, gain, shift, weight, bias, tables):
    count = lax.axis_size("wide")
    half = count // 2
    rows = own.shape[0] // half
    depth, columns = weight.shape
    width = columns // 3
    total = rows * count
    me = lax.axis_index("wide")
    order = jnp.stack([me ^ m for m in list(range(0, count, 2)) + list(range(1, count, 2))])

    def whole(i, order):
        return (0, 0)

    def placed(i, order):
        return (order[i], 0)

    vec = pl.BlockSpec((1, depth), whole)
    table = pl.BlockSpec((rows, PAIR), placed)
    out = pl.BlockSpec((rows, width), placed)
    return pl.pallas_call(
        project_kernel,
        grid_spec=pltpu.PrefetchScalarGridSpec(
            num_scalar_prefetch=1,
            grid=(count,),
            in_specs=[
                pl.BlockSpec((rows, depth), lambda i, order: (jnp.minimum(i, half - 1), 0)),
                pl.BlockSpec((rows, depth), lambda i, order: (jnp.maximum(i - half, 0), 0)),
                vec,
                vec,
                pl.BlockSpec((depth, columns), whole),
                pl.BlockSpec((1, columns), whole),
                table,
                table,
                table,
            ],
            out_specs=[
                pl.BlockSpec((rows, depth), placed),
                out,
                out,
                out,
                pl.BlockSpec((rows, PAIR), lambda i, order: (i, 0)),
            ],
        ),
        out_shape=[
            jax.ShapeDtypeStruct((total, depth), BF),
            jax.ShapeDtypeStruct((total, width), BF),
            jax.ShapeDtypeStruct((total, width), BF),
            jax.ShapeDtypeStruct((total, width), BF),
            jax.ShapeDtypeStruct((total, PAIR), F32),
        ],
        cost_estimate=pl.CostEstimate(flops=17 * 10**9, bytes_accessed=1, transcendentals=0),
        compiler_params=pltpu.CompilerParams(
            dimension_semantics=("arbitrary",), vmem_limit_bytes=48 * 2**20
        ),
        name="project",
    )(order, own, other, gain, shift, weight, bias, *tables)


def unproject_kernel(order, g_ref, x_ref, stats, weight, out, gain, shift, bias, held):
    half = order.shape[0]
    rows = held.shape[0] // half

    @pl.when(pl.program_id(0) == 0)
    def _():
        for i in range(half):
            start = pl.multiple_of(order[i] * rows, rows)
            held[i * rows : (i + 1) * rows, :] = g_ref[pl.ds(start, rows), :]
        bias[...] = jnp.sum(held[...].astype(F32), axis=0, keepdims=True)

    unit = (x_ref[...].astype(F32) - stats[:, 0:1]) * stats[:, 1:2]
    incoming = dot(held[...], weight[...], NT)
    out[...] = incoming.astype(BF)
    gain[...] = jnp.sum(incoming * unit, axis=0, keepdims=True)
    shift[...] = jnp.sum(incoming, axis=0, keepdims=True)


def unproject(grads, x, stats, weight, first):
    count = lax.axis_size("wide")
    total = x.shape[0]
    depth, columns = weight.shape
    block = math.gcd(depth, 512)
    order = jnp.stack([lax.axis_index("wide") ^ m for m in range(first, count, 2)])
    vec = pl.BlockSpec((1, block), lambda j, order: (0, j))
    return pl.pallas_call(
        unproject_kernel,
        grid_spec=pltpu.PrefetchScalarGridSpec(
            num_scalar_prefetch=1,
            grid=(depth // block,),
            in_specs=[
                pl.BlockSpec(grads.shape, lambda j, order: (0, 0)),
                pl.BlockSpec((total, block), lambda j, order: (0, j)),
                pl.BlockSpec((total, PAIR), lambda j, order: (first, 0)),
                pl.BlockSpec((block, columns), lambda j, order: (j, 0)),
            ],
            out_specs=[
                pl.BlockSpec((total, block), lambda j, order: (0, j)),
                vec,
                vec,
                pl.BlockSpec((1, columns), lambda j, order: (0, 0)),
            ],
            scratch_shapes=[pltpu.VMEM((total, columns), BF)],
        ),
        out_shape=[
            jax.ShapeDtypeStruct((total, depth), BF),
            jax.ShapeDtypeStruct((1, depth), F32),
            jax.ShapeDtypeStruct((1, depth), F32),
            jax.ShapeDtypeStruct((1, columns), F32),
        ],
        cost_estimate=pl.CostEstimate(flops=7 * 10**9, bytes_accessed=1, transcendentals=0),
        compiler_params=pltpu.CompilerParams(
            dimension_semantics=("arbitrary",), vmem_limit_bytes=48 * 2**20
        ),
        name="unproject",
    )(order, grads, x, stats, weight)


def head_mask(head, shape):
    lane = lax.broadcasted_iota(jnp.int32, shape, 1)
    return (lane // HEAD_DIM) == head


def attend_kernel(first, q_ref, k_ref, v_ref, o_ref, log_ref, v_turned):
    block = q_ref.shape[0]
    at = pl.program_id(1)
    scale = HEAD_DIM ** (-0.5)

    @pl.when(at == 0)
    def _():
        v_turned[...] = v_ref[...].astype(F32).T.astype(BF)

    q = q_ref[...] * jnp.asarray(scale, BF)
    queries = [jnp.where(head_mask(h, q.shape), q, jnp.zeros_like(q)) for h in range(2)]
    own_first = first[...]
    own_place = at * block + lax.broadcasted_iota(jnp.int32, (1, block), 1)

    def step(number, state):
        keys = k_ref[pl.ds(number * block, block), :]
        values = v_turned[:, pl.ds(number * block, block)]
        place = number * block + lax.broadcasted_iota(jnp.int32, (block, block), 0)
        visible = (place >= own_first) & (place <= own_place)
        out = []
        for h in range(2):
            peak, total, mix = state[h]
            scores = jnp.where(visible, dot(keys, queries[h], NT), neg_large)
            new_peak = jnp.maximum(peak, jnp.max(scores, axis=0, keepdims=True))
            terms = jnp.exp(scores - new_peak)
            decay = jnp.exp(peak - new_peak)
            out.append(
                (
                    new_peak,
                    total * decay + jnp.sum(terms, axis=0, keepdims=True),
                    mix * decay
                    + dot(values[h * HEAD_DIM : (h + 1) * HEAD_DIM], terms.astype(BF)),
                )
            )
        return tuple(out)

    start = (
        jnp.full((1, block), neg_large, F32),
        jnp.zeros((1, block), F32),
        jnp.zeros((HEAD_DIM, block), F32),
    )
    state = lax.fori_loop(0, at + 1, step, (start, start))
    mixes = []
    for h in range(2):
        peak, total, mix = state[h]
        mixes.append(mix / total)
        log_ref[0, h : h + 1, :] = peak + jnp.log(total)
    o_ref[...] = jnp.concatenate(mixes, axis=0).T.astype(BF)


def attend(first, q, k, v):
    total, width = q.shape
    pairs = width // PAIR
    block = math.gcd(total, 256)
    return pl.pallas_call(
        attend_kernel,
        grid=(pairs, total // block),
        in_specs=[
            pl.BlockSpec((1, block), lambda p, i: (0, i)),
            pl.BlockSpec((block, PAIR), lambda p, i: (i, p)),
            pl.BlockSpec((total, PAIR), lambda p, i: (0, p)),
            pl.BlockSpec((total, PAIR), lambda p, i: (0, p)),
        ],
        out_specs=[
            pl.BlockSpec((block, PAIR), lambda p, i: (i, p)),
            pl.BlockSpec((1, 2, block), lambda p, i: (p, 0, i)),
        ],
        out_shape=[
            jax.ShapeDtypeStruct((total, width), BF),
            jax.ShapeDtypeStruct((pairs, 2, total), F32),
        ],
        scratch_shapes=[pltpu.VMEM((PAIR, total), BF)],
        cost_estimate=pl.CostEstimate(flops=39 * 10**9, bytes_accessed=1, transcendentals=0),
        compiler_params=pltpu.CompilerParams(
            dimension_semantics=("arbitrary", "arbitrary"), vmem_limit_bytes=32 * 2**20
        ),
        name="attend",
    )(first, q, k, v)


def attend_back_kernel(
    first, q_ref, k_ref, v_ref, o_ref, g_ref, log_ref, cosine, ahead, behind,
    out_ref, k_turned, delta, sum_q, sum_k, sum_v,
):
    block, width = k_ref.shape
    pairs = width // PAIR
    at = pl.program_id(0)
    last = pl.num_programs(0)
    scale = HEAD_DIM ** (-0.5)
    k_turned[...] = k_ref[...].astype(F32).T.astype(BF)

    @pl.when(at == 0)
    def _():
        sum_q[...] = jnp.zeros_like(sum_q)

        def fill(number, carry):
            spot = pl.ds(number * block, block)
            both = (g_ref[spot, :].astype(F32) * o_ref[spot, :].astype(F32)).T
            for h in range(2 * pairs):
                delta[h : h + 1, spot] = jnp.sum(
                    both[h * HEAD_DIM : (h + 1) * HEAD_DIM], axis=0, keepdims=True
                )
            return carry

        lax.fori_loop(0, last, fill, 0)

    place = at * block + lax.broadcasted_iota(jnp.int32, (block, block), 0)

    def step(number, carry):
        spot = pl.ds(number * block, block)
        own_place = number * block + lax.broadcasted_iota(jnp.int32, (1, block), 1)
        visible = (place >= first[:, spot]) & (place <= own_place)
        for p in range(pairs):
            pair = slice(p * PAIR, (p + 1) * PAIR)
            q = q_ref[spot, pair] * jnp.asarray(scale, BF)
            g = g_ref[spot, pair]
            k, v = k_ref[:, pair], v_ref[:, pair]
            more_k = more_v = 0.0
            for h in range(2):
                mask = head_mask(h, q.shape)
                q_head = jnp.where(mask, q, jnp.zeros_like(q))
                g_head = jnp.where(mask, g, jnp.zeros_like(g))
                scores = dot(k, q_head, NT)
                probs = jnp.exp(
                    jnp.where(visible, scores - log_ref[p, h : h + 1, spot], neg_large)
                )
                slopes = dot(v, g_head, NT)
                head = 2 * p + h
                low = (probs * (slopes - delta[head : head + 1, spot])).astype(BF)
                more_v = more_v + dot(probs.astype(BF), g_head)
                more_k = more_k + dot(low, q_head)
                span = slice(head * HEAD_DIM, (head + 1) * HEAD_DIM)
                sum_q[span, spot] += dot(k_turned[span, :], low)
            sum_k[:, pair] += more_k
            sum_v[:, pair] += more_v
        return carry

    sum_k[...] = jnp.zeros_like(sum_k)
    sum_v[...] = jnp.zeros_like(sum_v)
    lax.fori_loop(at, last, step, 0)
    mine = pl.ds(at * block, block)
    out_ref[mine, 2 * width :] = sum_v[...].astype(BF)
    for p in range(pairs):
        start = width + p * PAIR
        out_ref[mine, start : start + PAIR] = turn_lanes(
            sum_k[:, p * PAIR : (p + 1) * PAIR],
            cosine[mine, :],
            -ahead[mine, :],
            -behind[mine, :],
        ).astype(BF)

    @pl.when(at == last - 1)
    def _():
        def finish(number, carry):
            spot = pl.ds(number * block, block)
            for p in range(pairs):
                pair = slice(p * PAIR, (p + 1) * PAIR)
                out_ref[spot, pair] = turn_lanes(
                    sum_q[pair, spot].T * scale,
                    cosine[spot, :],
                    -ahead[spot, :],
                    -behind[spot, :],
                ).astype(BF)
            return carry

        lax.fori_loop(0, last, finish, 0)


def attend_back(first, q, k, v, o, g, logs, tables):
    total, width = q.shape
    block = math.gcd(total, 256)

    def whole(*shape):
        return pl.BlockSpec(shape, lambda i: (0,) * len(shape))

    part = pl.BlockSpec((block, width), lambda i: (i, 0))
    return pl.pallas_call(
        attend_back_kernel,
        grid=(total // block,),
        in_specs=[
            whole(1, total),
            whole(total, width),
            part,
            part,
            whole(total, width),
            whole(total, width),
            whole(*logs.shape),
            whole(total, PAIR),
            whole(total, PAIR),
            whole(total, PAIR),
        ],
        out_specs=whole(total, 3 * width),
        out_shape=jax.ShapeDtypeStruct((total, 3 * width), BF),
        scratch_shapes=[
            pltpu.VMEM((width, block), BF),
            pltpu.VMEM((width // HEAD_DIM, total), F32),
            pltpu.VMEM((width, total), F32),
            pltpu.VMEM((block, width), F32),
            pltpu.VMEM((block, width), F32),
        ],
        cost_estimate=pl.CostEstimate(flops=44 * 10**9, bytes_accessed=1, transcendentals=0),
        compiler_params=pltpu.CompilerParams(
            dimension_semantics=("arbitrary",), vmem_limit_bytes=48 * 2**20
        ),
        name="attend_back",
    )(first, q, k, v, o, g, logs, *tables)


def regroup_kernel(x_ref, o_ref):
    count, rows, width = o_ref.shape
    groups = width // HEAD_DIM
    for w in range(count):
        for g in range(0, groups, 2):
            pieces = []
            for j in (g, g + 1):
                at = (j * count + w) * HEAD_DIM
                base = at // PAIR * PAIR
                pair = x_ref[:, base : base + PAIR].astype(F32)
                pieces.append(pair[:, at - base : at - base + HEAD_DIM])
            o_ref[w, :, g * HEAD_DIM : g * HEAD_DIM + PAIR] = jnp.concatenate(
                pieces, axis=1
            ).astype(o_ref.dtype)


def regroup(x, count):
    rows, columns = x.shape
    return pl.pallas_call(
        regroup_kernel,
        out_shape=jax.ShapeDtypeStruct((count, rows, columns // count), x.dtype),
        compiler_params=pltpu.CompilerParams(vmem_limit_bytes=16 * 2**20),
        name="regroup",
    )(x)


def regroup_back_kernel(x_ref, o_ref):
    parts, count, rows, width = x_ref.shape
    for g in range(width // HEAD_DIM):
        base = g * HEAD_DIM // PAIR * PAIR
        shift = g * HEAD_DIM - base
        for w in range(0, count, 2):
            pieces = []
            for j in (w, w + 1):
                total = x_ref[0, j, :, base : base + PAIR].astype(F32)
                for part in range(1, parts):
                    total = total + x_ref[part, j, :, base : base + PAIR].astype(F32)
                pieces.append(total[:, shift : shift + HEAD_DIM])
            at = (g * count + w) * HEAD_DIM
            o_ref[:, at : at + PAIR] = jnp.concatenate(pieces, axis=1)


def regroup_back(x):
    parts, count, rows, width = x.shape
    return pl.pallas_call(
        regroup_back_kernel,
        out_shape=jax.ShapeDtypeStruct((rows, count * width), F32),
        compiler_params=pltpu.CompilerParams(vmem_limit_bytes=16 * 2**20),
        name="regroup_back",
    )(x)


def norm_parts(values):
    centred = values - jnp.mean(values, axis=-1, keepdims=True)
    spread = jnp.mean(centred * centred, axis=-1, keepdims=True)
    rate = lax.rsqrt(spread + epsilon)
    return centred * rate, rate


def norm_back(incoming, unit, rate, gain):
    scaled = incoming * gain
    return rate * (
        scaled
        - jnp.mean(scaled, axis=-1, keepdims=True)
        - unit * jnp.mean(scaled * unit, axis=-1, keepdims=True)
    )


def shards(
    tokens,
    segments,
    w_qkv,
    b_qkv,
    w_out,
    ln1_gain,
    ln1_bias,
    ln2_gain,
    ln2_bias,
    w_gate,
    w_up,
    w_down,
    out_grad,
):
    rows_n, wide_n = lax.axis_size("rows"), lax.axis_size("wide")
    me_row, me = lax.axis_index("rows"), lax.axis_index("wide")
    devices = rows_n * wide_n
    local = tokens.shape[1]
    width = tokens.shape[2]
    row_len = local * wide_n
    per = HEADS // wide_n
    span = per * HEAD_DIM
    slab = width // devices
    bias_slab = 3 * width // devices

    def stage(run, *args):
        shapes = jax.eval_shape(run, *args)

        def blank(*args):
            return jax.tree.map(lambda x: jnp.zeros(x.shape, x.dtype), shapes)

        return lax.cond(segments[0, 0] >= 0, run, blank, *args)

    def sum_rows(x, dim):
        return lax.psum_scatter(x, "rows", scatter_dimension=dim, tiled=True)

    fast_out = slab == HEAD_DIM and per == rows_n
    if fast_out:
        w_out_own = lax.all_gather(w_out, "rows", axis=0, tiled=True)
    else:
        w_out_own = lax.dynamic_index_in_dim(
            lax.all_gather(w_out, ALL, axis=0, tiled=True).reshape(
                per, wide_n, HEAD_DIM, width
            ),
            me,
            1,
            keepdims=False,
        ).reshape(span, width)
    w_qkv_part = lax.all_to_all(
        regroup(w_qkv, wide_n), "wide", 0, 0, tiled=True
    ).reshape(wide_n * slab, 3 * span)
    w_qkv_own = lax.all_gather(w_qkv_part, "rows", axis=0, tiled=True)
    units = w_gate.shape[1]
    enter_slab = lax.all_gather(
        jnp.concatenate([w_gate, w_up], axis=1), "rows", axis=0, tiled=True
    )
    down_slab = lax.all_gather(w_down, "rows", axis=0, tiled=True)

    grad_low = out_grad[0]

    def first_stage(b_qkv, ln1_gain, ln1_bias, ln2_gain, ln2_bias, segs, tokens):
        packed = jnp.concatenate([b_qkv, ln1_gain, ln1_bias, ln2_gain, ln2_bias, segs])
        small = lax.all_gather(lax.all_gather(packed, "rows"), "wide")
        got = gather_first(tokens)
        own, other = gather_last(
            tokens, got, gather_second(tokens, after(got, small) if got else got)
        )
        flat = small.transpose(1, 0, 2)

        def vector(start, size):
            return flat[:, :, start : start + size].reshape(1, devices * size).astype(F32)

        row_segs = lax.dynamic_index_in_dim(small, me_row, 1, keepdims=False)[
            :, bias_slab + 4 * slab :
        ].reshape(row_len)
        own_bias = lax.dynamic_index_in_dim(
            vector(0, bias_slab).reshape(3, per, wide_n, HEAD_DIM), me, 2, keepdims=False
        ).reshape(1, 3 * span)

        doc_first = jnp.sum((row_segs[:, None] < row_segs[None, :]).astype(jnp.int32), axis=0)
        positions = jnp.arange(row_len, dtype=jnp.int32) - doc_first
        freqs = 10000.0 ** (-2.0 * jnp.arange(ROT // 2, dtype=F32) / ROT)
        lane = jnp.arange(PAIR) % HEAD_DIM
        lane_freqs = jnp.where(lane < ROT, jnp.tile(freqs, PAIR // (ROT // 2)), 0.0)
        angles = positions.astype(F32)[:, None] * lane_freqs[None, :]
        sine = jnp.sin(angles)
        half_rot = ROT // 2
        tables = (
            jnp.cos(angles),
            jnp.where(lane < half_rot, -sine, 0.0),
            jnp.where((lane >= half_rot) & (lane < ROT), sine, 0.0),
        )
        gains = tuple(vector(bias_slab + i * slab, slab) for i in range(4))
        return own, other, own_bias, gains, doc_first.reshape(1, row_len), tables

    own, other, own_bias, gains, first, tables = stage(
        first_stage,
        after(b_qkv, w_qkv_part),
        ln1_gain,
        ln1_bias,
        ln2_gain,
        ln2_bias,
        segments[0].astype(BF),
        tokens[0],
    )
    gain_one, shift_one, gain_two, shift_two = gains
    grads_got = gather_first(after(grad_low, own))

    act_one, q, k, v, stats = project(
        after(own, w_out_own), other, gain_one, shift_one, w_qkv_own, own_bias, tables
    )
    grads_passed = gather_second(grad_low, grads_got)
    attn_low, logs = attend(first, after(q, *grads_got), k, v)
    attn_low = after(attn_low, *grads_passed)

    def middle_stage(attn_low, w_out_own, gain_two, shift_two, tokens, grads):
        row_grad = jnp.concatenate(gather_last(*grads))
        attn_halves = to_relative(attn_low)
        total = start_scatter(*[dot(a, w_out_own).astype(BF) for a in attn_halves])
        middle = tokens.astype(F32) + scatter_plane(total)
        unit, rate = norm_parts(middle)
        act_two = (unit * gain_two + shift_two).astype(BF)
        return attn_halves, middle, unit, rate, gather_own(act_two), row_grad

    attn_halves, middle, unit_two, rate_two, act_own, row_grad = middle_stage(
        attn_low,
        w_out_own,
        gain_two,
        shift_two,
        tokens[0],
        (grad_low, grads_got, grads_passed),
    )

    over_first = (((0,), (1,)), ((), ()))
    over_second = (((1,), (0,)), ((), ()))

    def enter_stage(act_own, enter_slab, row_grad):
        act_other = swap(act_own, 1)
        entered = [dot(enter_slab, act, over_first) for act in (act_own, act_other)]
        hidden = [(jax.nn.silu(e[:units]) * e[units:]).astype(BF) for e in entered]
        grad_down = dot(
            row_grad, jnp.concatenate(hidden, axis=1), (((0,), (1,)), ((), ()))
        ).astype(BF)
        return act_other, entered, hidden, grad_down

    act_other, entered, hidden, grad_down = stage(enter_stage, act_own, enter_slab, row_grad)
    act_halves = (act_own, act_other)
    sum_down = sum_rows(grad_down, 0)

    def hidden_stage(act_halves, entered, row_grad, enter_slab, down_slab):
        enter_grads, act_parts = [], []
        for e, grad in zip(entered, jnp.split(row_grad, 2)):
            gate, upper = e[:units], e[units:]
            sig = jax.nn.sigmoid(gate)
            grad_hidden = dot(down_slab, grad, over_first)
            enter_grads.append(
                jnp.concatenate(
                    [
                        (grad_hidden * upper * sig * (1.0 + gate * (1.0 - sig))).astype(BF),
                        (grad_hidden * (gate * sig)).astype(BF),
                    ]
                )
            )
            act_parts.append(dot(enter_grads[-1], enter_slab, over_first).astype(BF))
        grad_enter = dot(
            jnp.concatenate(enter_grads, axis=1), jnp.concatenate(act_halves), over_second
        ).astype(BF)
        return start_scatter(*act_parts), grad_enter

    act_sum, grad_enter = stage(
        hidden_stage, act_halves, entered, row_grad, enter_slab, down_slab
    )
    sum_enter = sum_rows(grad_enter, 1)

    def norm_stage(act_sum, unit, rate, gain, grad_low, hidden, down_slab):
        got = scatter_first(act_sum)
        grad_act_two = scatter_last(act_sum, got, scatter_second(scatter_between(act_sum, got)))
        grad_norm = norm_back(grad_act_two, unit, rate, gain)
        return (
            grad_low.astype(F32) + grad_norm,
            jnp.sum(grad_act_two * unit, axis=0),
            jnp.sum(grad_act_two, axis=0),
            start_scatter(*[dot(h, down_slab, over_first).astype(BF) for h in hidden]),
        )

    grad_middle, grad_gain_two, grad_shift_two, mixed_sum = stage(
        norm_stage, act_sum, unit_two, rate_two, gain_two, grad_low, hidden, down_slab
    )


    def branch_stage(branch, sum_down):
        return gather_own(branch), sum_down.astype(F32)

    branch_own, out_down = stage(branch_stage, grad_middle.astype(BF), sum_down)
    branch_halves = (branch_own, swap(branch_own, 1))
    attn_own_grad = dot(branch_own, w_out_own, NT).astype(BF)
    grad_w_out_own = dot(attn_halves[0], branch_own, TN)

    def back_stage(
        branch_other, own_grad, w_out_own, first, q, k, v, attn_low, logs, tables, act_one, mixed_sum
    ):
        grad_attn = to_absolute(own_grad, dot(branch_other, w_out_own, NT).astype(BF))
        grad_proj = attend_back(first, q, k, v, attn_low, grad_attn, logs, tables)
        return grad_proj, dot(act_one, grad_proj, TN).astype(BF), scatter_first(mixed_sum)

    grad_proj, grad_w_qkv, mixed_got = stage(
        back_stage,
        after(branch_halves[1], grad_w_out_own),
        attn_own_grad,
        w_out_own,
        first,
        q,
        k,
        v,
        attn_low,
        logs,
        tables,
        act_one,
        mixed_sum,
    )
    grad_proj, grad_w_qkv = after((grad_proj, grad_w_qkv), sum_enter)
    sum_qkv = sum_rows(grad_w_qkv, 0)

    branch_other = after(branch_halves[1], grad_w_qkv)
    grad_w_out = (grad_w_out_own + dot(attn_halves[1], branch_other, TN)).astype(BF)
    if fast_out:
        sum_w_out = sum_rows(grad_w_out, 0)
    else:
        spread_out = lax.dynamic_update_index_in_dim(
            jnp.zeros((per, wide_n, HEAD_DIM, width), BF),
            grad_w_out.reshape(per, HEAD_DIM, width),
            me,
            1,
        )
        sum_w_out = lax.psum_scatter(
            spread_out.reshape(width, width), ALL, scatter_dimension=0, tiled=True
        )

    def last_stage(
        grad_proj, w_qkv_own, own, other, stats, gain, grad_middle, grad_gain_two, grad_shift_two,
        mixed_sum, mixed_got, middle,
    ):
        part_other, *sums_other = unproject(grad_proj, other, stats, w_qkv_own, 1)
        part_own, *sums_own = unproject(grad_proj, own, stats, w_qkv_own, 0)
        total = start_scatter(part_own, part_other)
        got = scatter_first(total)
        sums_own, sums_other, got, mixed_got = after((sums_own, sums_other, got, mixed_got))
        passed = scatter_second(scatter_between(total, got))
        total, got = after((total, got), *passed)
        grad_gain, grad_shift, grad_bias = (a + b for a, b in zip(sums_own, sums_other))
        full_bias = lax.dynamic_update_index_in_dim(
            jnp.zeros((3, per, wide_n, HEAD_DIM), F32),
            grad_bias.reshape(3, per, HEAD_DIM),
            me,
            2,
        )
        small = jnp.concatenate(
            [
                full_bias.reshape(devices, bias_slab),
                grad_gain.reshape(devices, slab),
                grad_shift.reshape(devices, slab),
                grad_gain_two.reshape(devices, slab),
                grad_shift_two.reshape(devices, slab),
            ],
            axis=1,
        )
        small = small.reshape(rows_n, wide_n, -1).transpose(1, 0, 2)
        sums = halve(small.reshape(wide_n, -1), "wide").reshape(rows_n, -1)
        rate = stats[:local, 1:2]
        unit = (own[:local].astype(F32) - stats[:local, 0:1]) * rate
        grad_act_one = scatter_last(total, got, passed)
        mixed_passed = scatter_second(scatter_between(mixed_sum, mixed_got))
        if passed:
            mixed_passed = after(mixed_passed, *passed)
        mixed = scatter_last(mixed_sum, mixed_got, mixed_passed)
        return (
            (grad_middle + norm_back(grad_act_one, unit, rate, gain))[None],
            sums,
            (middle + mixed).astype(BF)[None],
        )

    grad_tokens, sums, result = stage(
        last_stage,
        after(grad_proj, grad_w_qkv, grad_w_out),
        w_qkv_own,
        own,
        other,
        stats,
        gain_one,
        grad_middle,
        grad_gain_two,
        grad_shift_two,
        mixed_sum,
        mixed_got,
        middle,
    )
    sum_enter = after(sum_enter, sums)
    out_gate, out_up = sum_enter[:units].T.astype(F32), sum_enter[units:].T.astype(F32)
    out_w_out = sum_w_out.astype(F32)
    part_qkv = lax.all_to_all(
        after(sum_qkv, sums).reshape(wide_n, slab, 3 * span), "wide", 0, 0, tiled=True
    )
    sums = halve(after(sums, sum_qkv), "rows")
    out_qkv = regroup_back(part_qkv[None])
    out_bias = sums[:bias_slab]
    small_outs = [
        sums[bias_slab + i * slab : bias_slab + (i + 1) * slab] for i in range(4)
    ]
    return (
        result,
        grad_tokens,
        out_qkv,
        out_bias,
        out_w_out,
        *small_outs,
        out_gate,
        out_up,
        out_down,
    )


def solution(mesh):
    by_token = P("rows", "wide", None)
    by_both = P(("rows", "wide"), None)
    vector = P(("rows", "wide"))
    by_slab = P("rows", "wide")
    in_specs = (
        by_token, P("rows", "wide"), by_both, vector, by_both, vector, vector, vector, vector,
        by_slab, by_slab, by_slab, by_token,
    )
    out_specs = (
        by_token, by_token, by_both, vector, by_both, vector, vector, vector, vector,
        by_slab, by_slab, by_slab,
    )
    return jax.shard_map(shards, mesh=mesh, in_specs=in_specs, out_specs=out_specs, check_vma=False)
```

```python
import functools
import math

import jax
import jax.numpy as jnp
from jax import lax
from jax.experimental import pallas as pl
from jax.experimental.pallas import tpu as pltpu
from jax.sharding import PartitionSpec as P

HEADS = 32
HEAD_DIM = 64
ROT = 16
PAIR = 2 * HEAD_DIM

epsilon = 1e-05
neg_large = -1e30
BF = jnp.bfloat16
F32 = jnp.float32
ALL = ("rows", "wide")
NT = (((1,), (1,)), ((), ()))
TN = (((0,), (0,)), ((), ()))


def dot(left, right, dims=(((1,), (0,)), ((), ()))):
    return lax.dot_general(left, right, dims, preferred_element_type=F32)


def swap(x, bit, axis="wide"):
    return lax.ppermute(x, axis, [(i, i ^ bit) for i in range(lax.axis_size(axis))])


def upper_bits():
    return [1 << k for k in range(1, lax.axis_size("wide").bit_length() - 1)]


def gather_first(x):
    bits = upper_bits()
    return tuple(swap(x, bit) for bit in bits) if len(bits) == 2 else ()


def gather_second(x, got):
    if not got:
        return ()
    one, two = upper_bits()
    half = x.shape[0] // 2
    return swap(got[1][:half], one), swap(got[0][half:], two)


def gather_third(x, got, passed):
    if got:
        return jnp.concatenate([x, *got, *passed])
    for bit in upper_bits():
        x = jnp.concatenate([x, swap(x, bit)])
    return x


def gather_last(x, got, passed):
    own = gather_third(x, got, passed)
    return own, swap(own, 1)


def gather_own(x):
    got = gather_first(x)
    return gather_third(x, got, gather_second(x, got))


def add_low(left, right):
    return (left.astype(F32) + right.astype(F32)).astype(BF)


def start_scatter(own, other):
    return add_low(lax.optimization_barrier(own), swap(other, 1))


def block_of(total, m, h):
    half = total.shape[0] // 8
    return total[(2 * m + h) * half : (2 * m + h + 1) * half]


def scatter_first(total):
    bits = upper_bits()
    if len(bits) != 2:
        return ()
    one, two = bits
    return (
        swap(block_of(total, 3, 0), one),
        swap(block_of(total, 3, 1), two),
        swap(block_of(total, 1, 0), one),
        swap(block_of(total, 2, 1), two),
    )


def scatter_between(total, got):
    if not got:
        return ()
    return add_low(block_of(total, 2, 0), got[0]), add_low(block_of(total, 1, 1), got[1])


def scatter_second(between):
    if not between:
        return ()
    one, two = upper_bits()
    return swap(between[0], two), swap(between[1], one)


def scatter_last(total, got, passed):
    if got:
        return jnp.concatenate(
            [
                block_of(total, 0, h).astype(F32) + got[2 + h].astype(F32) + passed[h].astype(F32)
                for h in range(2)
            ]
        )
    bits = upper_bits()
    for bit in reversed(bits[1:]):
        half = total.shape[0] // 2
        total = add_low(total[:half], swap(total[half:], bit))
    half = total.shape[0] // 2
    return total[:half].astype(F32) + swap(total[half:], bits[0]).astype(F32)


def scatter_plane(total):
    got = scatter_first(total)
    return scatter_last(total, got, scatter_second(scatter_between(total, got)))


def after(x, *others):
    return lax.optimization_barrier((x, others))[0]


def to_relative(x):
    count = lax.axis_size("wide")
    me = lax.axis_index("wide")
    blocks = x.reshape(count, x.shape[0] // count, x.shape[1])

    def pick(first):
        return jnp.concatenate(
            [
                lax.dynamic_index_in_dim(blocks, me ^ m, 0, keepdims=False)
                for m in range(first, count, 2)
            ]
        )

    return pick(0), pick(1)


def to_absolute(own, other):
    count = lax.axis_size("wide")
    me = lax.axis_index("wide")
    half = count // 2
    blocks = jnp.concatenate([own, other]).reshape(count, -1, own.shape[1])
    pieces = []
    for place in range(count):
        m = me ^ place
        pieces.append(
            lax.dynamic_index_in_dim(blocks, (m & 1) * half + (m >> 1), 0, keepdims=False)
        )
    return jnp.concatenate(pieces)


def halve(x, axis):
    count, me = lax.axis_size(axis), lax.axis_index(axis)
    width = x.shape[1]
    size = count // 2
    while size >= 1:
        side = (me // size) % 2
        halves = x.reshape(2, -1, width)
        keep = lax.dynamic_index_in_dim(halves, side, 0, keepdims=False)
        give = lax.dynamic_index_in_dim(halves, 1 - side, 0, keepdims=False)
        x = keep + swap(give, size, axis)
        size //= 2
    return x.reshape(width)


def turn_lanes(x, cosine, ahead, behind):
    half_rot = ROT // 2
    lanes = x.shape[-1]
    return (
        x * cosine
        + pltpu.roll(x, lanes - half_rot, 1) * ahead
        + pltpu.roll(x, half_rot, 1) * behind
    )


def project_kernel(
    order, own_ref, other_ref, gain, shift, weight, bias, cosine, ahead, behind,
    act, q, k, v, stats,
):
    half = pl.num_programs(0) // 2
    width = q.shape[1]
    x = jnp.where(pl.program_id(0) < half, own_ref[...], other_ref[...]).astype(F32)
    centre = jnp.mean(x, axis=1, keepdims=True)
    centred = x - centre
    rate = lax.rsqrt(jnp.mean(centred * centred, axis=1, keepdims=True) + epsilon)
    lane = lax.broadcasted_iota(jnp.int32, stats.shape, 1)
    stats[...] = jnp.where(lane == 0, centre, rate)
    normed = (centred * rate * gain[...] + shift[...]).astype(BF)
    act[...] = normed
    projected = dot(normed, weight[...]) + bias[...]
    for at in range(0, width, PAIR):
        angles = (cosine[...], ahead[...], behind[...])
        q[:, at : at + PAIR] = turn_lanes(projected[:, at : at + PAIR], *angles).astype(BF)
        k[:, at : at + PAIR] = turn_lanes(
            projected[:, width + at : width + at + PAIR], *angles
        ).astype(BF)
    v[...] = projected[:, 2 * width :].astype(BF)


def project(own, other, gain, shift, weight, bias, tables):
    count = lax.axis_size("wide")
    half = count // 2
    rows = own.shape[0] // half
    depth, columns = weight.shape
    width = columns // 3
    total = rows * count
    me = lax.axis_index("wide")
    order = jnp.stack([me ^ m for m in list(range(0, count, 2)) + list(range(1, count, 2))])

    def whole(i, order):
        return (0, 0)

    def placed(i, order):
        return (order[i], 0)

    vec = pl.BlockSpec((1, depth), whole)
    table = pl.BlockSpec((rows, PAIR), placed)
    out = pl.BlockSpec((rows, width), placed)
    return pl.pallas_call(
        project_kernel,
        grid_spec=pltpu.PrefetchScalarGridSpec(
            num_scalar_prefetch=1,
            grid=(count,),
            in_specs=[
                pl.BlockSpec((rows, depth), lambda i, order: (jnp.minimum(i, half - 1), 0)),
                pl.BlockSpec((rows, depth), lambda i, order: (jnp.maximum(i - half, 0), 0)),
                vec,
                vec,
                pl.BlockSpec((depth, columns), whole),
                pl.BlockSpec((1, columns), whole),
                table,
                table,
                table,
            ],
            out_specs=[
                pl.BlockSpec((rows, depth), placed),
                out,
                out,
                out,
                pl.BlockSpec((rows, PAIR), lambda i, order: (i, 0)),
            ],
        ),
        out_shape=[
            jax.ShapeDtypeStruct((total, depth), BF),
            jax.ShapeDtypeStruct((total, width), BF),
            jax.ShapeDtypeStruct((total, width), BF),
            jax.ShapeDtypeStruct((total, width), BF),
            jax.ShapeDtypeStruct((total, PAIR), F32),
        ],
        cost_estimate=pl.CostEstimate(flops=17 * 10**9, bytes_accessed=1, transcendentals=0),
        compiler_params=pltpu.CompilerParams(
            dimension_semantics=("arbitrary",), vmem_limit_bytes=48 * 2**20
        ),
        name="project",
    )(order, own, other, gain, shift, weight, bias, *tables)


def unproject_kernel(order, g_ref, x_ref, stats, weight, out, gain, shift, bias, held):
    half = order.shape[0]
    rows = held.shape[0] // half

    @pl.when(pl.program_id(0) == 0)
    def _():
        for i in range(half):
            start = pl.multiple_of(order[i] * rows, rows)
            held[i * rows : (i + 1) * rows, :] = g_ref[pl.ds(start, rows), :]
        bias[...] = jnp.sum(held[...].astype(F32), axis=0, keepdims=True)

    unit = (x_ref[...].astype(F32) - stats[:, 0:1]) * stats[:, 1:2]
    incoming = dot(held[...], weight[...], NT)
    out[...] = incoming.astype(BF)
    gain[...] = jnp.sum(incoming * unit, axis=0, keepdims=True)
    shift[...] = jnp.sum(incoming, axis=0, keepdims=True)


def unproject(grads, x, stats, weight, first):
    count = lax.axis_size("wide")
    total = x.shape[0]
    depth, columns = weight.shape
    block = math.gcd(depth, 1024)
    order = jnp.stack([lax.axis_index("wide") ^ m for m in range(first, count, 2)])
    vec = pl.BlockSpec((1, block), lambda j, order: (0, j))
    return pl.pallas_call(
        unproject_kernel,
        grid_spec=pltpu.PrefetchScalarGridSpec(
            num_scalar_prefetch=1,
            grid=(depth // block,),
            in_specs=[
                pl.BlockSpec(grads.shape, lambda j, order: (0, 0)),
                pl.BlockSpec((total, block), lambda j, order: (0, j)),
                pl.BlockSpec((total, PAIR), lambda j, order: (first, 0)),
                pl.BlockSpec((block, columns), lambda j, order: (j, 0)),
            ],
            out_specs=[
                pl.BlockSpec((total, block), lambda j, order: (0, j)),
                vec,
                vec,
                pl.BlockSpec((1, columns), lambda j, order: (0, 0)),
            ],
            scratch_shapes=[pltpu.VMEM((total, columns), BF)],
        ),
        out_shape=[
            jax.ShapeDtypeStruct((total, depth), BF),
            jax.ShapeDtypeStruct((1, depth), F32),
            jax.ShapeDtypeStruct((1, depth), F32),
            jax.ShapeDtypeStruct((1, columns), F32),
        ],
        cost_estimate=pl.CostEstimate(flops=7 * 10**9, bytes_accessed=1, transcendentals=0),
        compiler_params=pltpu.CompilerParams(
            dimension_semantics=("arbitrary",), vmem_limit_bytes=48 * 2**20
        ),
        name="unproject",
    )(order, grads, x, stats, weight)


def head_mask(head, shape):
    lane = lax.broadcasted_iota(jnp.int32, shape, 1)
    return (lane // HEAD_DIM) == head


def attend_kernel(first, q_ref, k_ref, v_ref, o_ref, log_ref, v_turned):
    block = q_ref.shape[0]
    at = pl.program_id(1)
    scale = HEAD_DIM ** (-0.5)

    @pl.when(at == 0)
    def _():
        v_turned[...] = v_ref[...].astype(F32).T.astype(BF)

    q = q_ref[...] * jnp.asarray(scale, BF)
    queries = [jnp.where(head_mask(h, q.shape), q, jnp.zeros_like(q)) for h in range(2)]
    own_first = first[...]
    own_place = at * block + lax.broadcasted_iota(jnp.int32, (1, block), 1)

    def step(number, state):
        keys = k_ref[pl.ds(number * block, block), :]
        values = v_turned[:, pl.ds(number * block, block)]
        place = number * block + lax.broadcasted_iota(jnp.int32, (block, block), 0)
        visible = (place >= own_first) & (place <= own_place)
        out = []
        for h in range(2):
            peak, total, mix = state[h]
            scores = jnp.where(visible, dot(keys, queries[h], NT), neg_large)
            new_peak = jnp.maximum(peak, jnp.max(scores, axis=0, keepdims=True))
            terms = jnp.exp(scores - new_peak)
            decay = jnp.exp(peak - new_peak)
            out.append(
                (
                    new_peak,
                    total * decay + jnp.sum(terms, axis=0, keepdims=True),
                    mix * decay
                    + dot(values[h * HEAD_DIM : (h + 1) * HEAD_DIM], terms.astype(BF)),
                )
            )
        return tuple(out)

    start = (
        jnp.full((1, block), neg_large, F32),
        jnp.zeros((1, block), F32),
        jnp.zeros((HEAD_DIM, block), F32),
    )
    state = lax.fori_loop(0, at + 1, step, (start, start))
    mixes = []
    for h in range(2):
        peak, total, mix = state[h]
        mixes.append(mix / total)
        log_ref[0, h : h + 1, :] = peak + jnp.log(total)
    o_ref[...] = jnp.concatenate(mixes, axis=0).T.astype(BF)


def attend(first, q, k, v):
    total, width = q.shape
    pairs = width // PAIR
    block = math.gcd(total, 256)
    return pl.pallas_call(
        attend_kernel,
        grid=(pairs, total // block),
        in_specs=[
            pl.BlockSpec((1, block), lambda p, i: (0, i)),
            pl.BlockSpec((block, PAIR), lambda p, i: (i, p)),
            pl.BlockSpec((total, PAIR), lambda p, i: (0, p)),
            pl.BlockSpec((total, PAIR), lambda p, i: (0, p)),
        ],
        out_specs=[
            pl.BlockSpec((block, PAIR), lambda p, i: (i, p)),
            pl.BlockSpec((1, 2, block), lambda p, i: (p, 0, i)),
        ],
        out_shape=[
            jax.ShapeDtypeStruct((total, width), BF),
            jax.ShapeDtypeStruct((pairs, 2, total), F32),
        ],
        scratch_shapes=[pltpu.VMEM((PAIR, total), BF)],
        cost_estimate=pl.CostEstimate(flops=39 * 10**9, bytes_accessed=1, transcendentals=0),
        compiler_params=pltpu.CompilerParams(
            dimension_semantics=("arbitrary", "arbitrary"), vmem_limit_bytes=32 * 2**20
        ),
        name="attend",
    )(first, q, k, v)


def attend_back_kernel(
    first, q_ref, k_ref, v_ref, o_ref, g_ref, log_ref, cosine, ahead, behind,
    out_ref, k_turned, delta, sum_q, sum_k, sum_v,
):
    block, width = k_ref.shape
    pairs = width // PAIR
    at = pl.program_id(0)
    last = pl.num_programs(0)
    scale = HEAD_DIM ** (-0.5)
    k_turned[...] = k_ref[...].astype(F32).T.astype(BF)

    @pl.when(at == 0)
    def _():
        sum_q[...] = jnp.zeros_like(sum_q)

        def fill(number, carry):
            spot = pl.ds(number * block, block)
            both = (g_ref[spot, :].astype(F32) * o_ref[spot, :].astype(F32)).T
            for h in range(2 * pairs):
                delta[h : h + 1, spot] = jnp.sum(
                    both[h * HEAD_DIM : (h + 1) * HEAD_DIM], axis=0, keepdims=True
                )
            return carry

        lax.fori_loop(0, last, fill, 0)

    place = at * block + lax.broadcasted_iota(jnp.int32, (block, block), 0)

    def step(number, carry):
        spot = pl.ds(number * block, block)
        own_place = number * block + lax.broadcasted_iota(jnp.int32, (1, block), 1)
        visible = (place >= first[:, spot]) & (place <= own_place)
        for p in range(pairs):
            pair = slice(p * PAIR, (p + 1) * PAIR)
            q = q_ref[spot, pair] * jnp.asarray(scale, BF)
            g = g_ref[spot, pair]
            k, v = k_ref[:, pair], v_ref[:, pair]
            more_k = more_v = 0.0
            for h in range(2):
                mask = head_mask(h, q.shape)
                q_head = jnp.where(mask, q, jnp.zeros_like(q))
                g_head = jnp.where(mask, g, jnp.zeros_like(g))
                scores = dot(k, q_head, NT)
                probs = jnp.exp(
                    jnp.where(visible, scores - log_ref[p, h : h + 1, spot], neg_large)
                )
                slopes = dot(v, g_head, NT)
                head = 2 * p + h
                low = (probs * (slopes - delta[head : head + 1, spot])).astype(BF)
                more_v = more_v + dot(probs.astype(BF), g_head)
                more_k = more_k + dot(low, q_head)
                span = slice(head * HEAD_DIM, (head + 1) * HEAD_DIM)
                sum_q[span, spot] += dot(k_turned[span, :], low)
            sum_k[:, pair] += more_k
            sum_v[:, pair] += more_v
        return carry

    sum_k[...] = jnp.zeros_like(sum_k)
    sum_v[...] = jnp.zeros_like(sum_v)
    lax.fori_loop(at, last, step, 0)
    mine = pl.ds(at * block, block)
    out_ref[mine, 2 * width :] = sum_v[...].astype(BF)
    for p in range(pairs):
        start = width + p * PAIR
        out_ref[mine, start : start + PAIR] = turn_lanes(
            sum_k[:, p * PAIR : (p + 1) * PAIR],
            cosine[mine, :],
            -ahead[mine, :],
            -behind[mine, :],
        ).astype(BF)

    @pl.when(at == last - 1)
    def _():
        def finish(number, carry):
            spot = pl.ds(number * block, block)
            for p in range(pairs):
                pair = slice(p * PAIR, (p + 1) * PAIR)
                out_ref[spot, pair] = turn_lanes(
                    sum_q[pair, spot].T * scale,
                    cosine[spot, :],
                    -ahead[spot, :],
                    -behind[spot, :],
                ).astype(BF)
            return carry

        lax.fori_loop(0, last, finish, 0)


def attend_back(first, q, k, v, o, g, logs, tables):
    total, width = q.shape
    block = math.gcd(total, 256)

    def whole(*shape):
        return pl.BlockSpec(shape, lambda i: (0,) * len(shape))

    part = pl.BlockSpec((block, width), lambda i: (i, 0))
    return pl.pallas_call(
        attend_back_kernel,
        grid=(total // block,),
        in_specs=[
            whole(1, total),
            whole(total, width),
            part,
            part,
            whole(total, width),
            whole(total, width),
            whole(*logs.shape),
            whole(total, PAIR),
            whole(total, PAIR),
            whole(total, PAIR),
        ],
        out_specs=whole(total, 3 * width),
        out_shape=jax.ShapeDtypeStruct((total, 3 * width), BF),
        scratch_shapes=[
            pltpu.VMEM((width, block), BF),
            pltpu.VMEM((width // HEAD_DIM, total), F32),
            pltpu.VMEM((width, total), F32),
            pltpu.VMEM((block, width), F32),
            pltpu.VMEM((block, width), F32),
        ],
        cost_estimate=pl.CostEstimate(flops=44 * 10**9, bytes_accessed=1, transcendentals=0),
        compiler_params=pltpu.CompilerParams(
            dimension_semantics=("arbitrary",), vmem_limit_bytes=48 * 2**20
        ),
        name="attend_back",
    )(first, q, k, v, o, g, logs, *tables)


def regroup_kernel(x_ref, o_ref):
    count, rows, width = o_ref.shape
    groups = width // HEAD_DIM
    for w in range(count):
        for g in range(0, groups, 2):
            pieces = []
            for j in (g, g + 1):
                at = (j * count + w) * HEAD_DIM
                base = at // PAIR * PAIR
                pair = x_ref[:, base : base + PAIR].astype(F32)
                pieces.append(pair[:, at - base : at - base + HEAD_DIM])
            o_ref[w, :, g * HEAD_DIM : g * HEAD_DIM + PAIR] = jnp.concatenate(
                pieces, axis=1
            ).astype(o_ref.dtype)


def regroup(x, count):
    rows, columns = x.shape
    return pl.pallas_call(
        regroup_kernel,
        out_shape=jax.ShapeDtypeStruct((count, rows, columns // count), x.dtype),
        compiler_params=pltpu.CompilerParams(vmem_limit_bytes=16 * 2**20),
        name="regroup",
    )(x)


def regroup_back_kernel(x_ref, o_ref):
    parts, count, rows, width = x_ref.shape
    for g in range(width // HEAD_DIM):
        base = g * HEAD_DIM // PAIR * PAIR
        shift = g * HEAD_DIM - base
        for w in range(0, count, 2):
            pieces = []
            for j in (w, w + 1):
                total = x_ref[0, j, :, base : base + PAIR].astype(F32)
                for part in range(1, parts):
                    total = total + x_ref[part, j, :, base : base + PAIR].astype(F32)
                pieces.append(total[:, shift : shift + HEAD_DIM])
            at = (g * count + w) * HEAD_DIM
            o_ref[:, at : at + PAIR] = jnp.concatenate(pieces, axis=1)


def regroup_back(x):
    parts, count, rows, width = x.shape
    return pl.pallas_call(
        regroup_back_kernel,
        out_shape=jax.ShapeDtypeStruct((rows, count * width), F32),
        compiler_params=pltpu.CompilerParams(vmem_limit_bytes=16 * 2**20),
        name="regroup_back",
    )(x)


def norm_parts(values):
    centred = values - jnp.mean(values, axis=-1, keepdims=True)
    spread = jnp.mean(centred * centred, axis=-1, keepdims=True)
    rate = lax.rsqrt(spread + epsilon)
    return centred * rate, rate


def norm_back(incoming, unit, rate, gain):
    scaled = incoming * gain
    return rate * (
        scaled
        - jnp.mean(scaled, axis=-1, keepdims=True)
        - unit * jnp.mean(scaled * unit, axis=-1, keepdims=True)
    )


def shards(
    tokens,
    segments,
    w_qkv,
    b_qkv,
    w_out,
    ln1_gain,
    ln1_bias,
    ln2_gain,
    ln2_bias,
    w_gate,
    w_up,
    w_down,
    out_grad,
):
    rows_n, wide_n = lax.axis_size("rows"), lax.axis_size("wide")
    me_row, me = lax.axis_index("rows"), lax.axis_index("wide")
    devices = rows_n * wide_n
    local = tokens.shape[1]
    width = tokens.shape[2]
    row_len = local * wide_n
    per = HEADS // wide_n
    span = per * HEAD_DIM
    slab = width // devices
    bias_slab = 3 * width // devices

    def stage(run, *args):
        shapes = jax.eval_shape(run, *args)

        def blank(*args):
            return jax.tree.map(lambda x: jnp.zeros(x.shape, x.dtype), shapes)

        return lax.cond(segments[0, 0] >= 0, run, blank, *args)

    def sum_rows(x, dim):
        return lax.psum_scatter(x, "rows", scatter_dimension=dim, tiled=True)

    fast_out = slab == HEAD_DIM and per == rows_n
    if fast_out:
        w_out_own = lax.all_gather(w_out, "rows", axis=0, tiled=True)
    else:
        w_out_own = lax.dynamic_index_in_dim(
            lax.all_gather(w_out, ALL, axis=0, tiled=True).reshape(
                per, wide_n, HEAD_DIM, width
            ),
            me,
            1,
            keepdims=False,
        ).reshape(span, width)
    w_qkv_part = lax.all_to_all(
        regroup(w_qkv, wide_n), "wide", 0, 0, tiled=True
    ).reshape(wide_n * slab, 3 * span)
    w_qkv_own = lax.all_gather(w_qkv_part, "rows", axis=0, tiled=True)
    units = w_gate.shape[1]
    enter_slab = lax.all_gather(
        jnp.concatenate([w_gate, w_up], axis=1), "rows", axis=0, tiled=True
    )
    down_slab = lax.all_gather(w_down, "rows", axis=0, tiled=True)

    grad_low = out_grad[0]

    def first_stage(b_qkv, ln1_gain, ln1_bias, ln2_gain, ln2_bias, segs, tokens):
        packed = jnp.concatenate([b_qkv, ln1_gain, ln1_bias, ln2_gain, ln2_bias, segs])
        small = lax.all_gather(lax.all_gather(packed, "rows"), "wide")
        got = gather_first(tokens)
        own, other = gather_last(
            tokens, got, gather_second(tokens, after(got, small) if got else got)
        )
        flat = small.transpose(1, 0, 2)

        def vector(start, size):
            return flat[:, :, start : start + size].reshape(1, devices * size).astype(F32)

        row_segs = lax.dynamic_index_in_dim(small, me_row, 1, keepdims=False)[
            :, bias_slab + 4 * slab :
        ].reshape(row_len)
        own_bias = lax.dynamic_index_in_dim(
            vector(0, bias_slab).reshape(3, per, wide_n, HEAD_DIM), me, 2, keepdims=False
        ).reshape(1, 3 * span)

        doc_first = jnp.sum((row_segs[:, None] < row_segs[None, :]).astype(jnp.int32), axis=0)
        positions = jnp.arange(row_len, dtype=jnp.int32) - doc_first
        freqs = 10000.0 ** (-2.0 * jnp.arange(ROT // 2, dtype=F32) / ROT)
        lane = jnp.arange(PAIR) % HEAD_DIM
        lane_freqs = jnp.where(lane < ROT, jnp.tile(freqs, PAIR // (ROT // 2)), 0.0)
        angles = positions.astype(F32)[:, None] * lane_freqs[None, :]
        sine = jnp.sin(angles)
        half_rot = ROT // 2
        tables = (
            jnp.cos(angles),
            jnp.where(lane < half_rot, -sine, 0.0),
            jnp.where((lane >= half_rot) & (lane < ROT), sine, 0.0),
        )
        gains = tuple(vector(bias_slab + i * slab, slab) for i in range(4))
        return own, other, own_bias, gains, doc_first.reshape(1, row_len), tables

    own, other, own_bias, gains, first, tables = stage(
        first_stage,
        after(b_qkv, w_qkv_part),
        ln1_gain,
        ln1_bias,
        ln2_gain,
        ln2_bias,
        segments[0].astype(BF),
        tokens[0],
    )
    gain_one, shift_one, gain_two, shift_two = gains
    grads_got = gather_first(after(grad_low, own))

    act_one, q, k, v, stats = project(
        after(own, w_out_own), other, gain_one, shift_one, w_qkv_own, own_bias, tables
    )
    grads_passed = gather_second(grad_low, grads_got)
    attn_low, logs = attend(first, after(q, *grads_got), k, v)
    attn_low = after(attn_low, *grads_passed)

    def middle_stage(attn_low, w_out_own, gain_two, shift_two, tokens, grads):
        row_grad = jnp.concatenate(gather_last(*grads))
        attn_halves = to_relative(attn_low)
        total = start_scatter(*[dot(a, w_out_own).astype(BF) for a in attn_halves])
        middle = tokens.astype(F32) + scatter_plane(total)
        unit, rate = norm_parts(middle)
        act_two = (unit * gain_two + shift_two).astype(BF)
        return attn_halves, middle, unit, rate, gather_own(act_two), row_grad

    attn_halves, middle, unit_two, rate_two, act_own, row_grad = middle_stage(
        attn_low,
        w_out_own,
        gain_two,
        shift_two,
        tokens[0],
        (grad_low, grads_got, grads_passed),
    )

    over_first = (((0,), (1,)), ((), ()))
    over_second = (((1,), (0,)), ((), ()))

    def enter_stage(act_own, enter_slab, row_grad):
        act_other = swap(act_own, 1)
        entered = [dot(enter_slab, act, over_first) for act in (act_own, act_other)]
        hidden = [(jax.nn.silu(e[:units]) * e[units:]).astype(BF) for e in entered]
        grad_down = dot(
            row_grad, jnp.concatenate(hidden, axis=1), (((0,), (1,)), ((), ()))
        ).astype(BF)
        return act_other, entered, hidden, grad_down

    act_other, entered, hidden, grad_down = stage(enter_stage, act_own, enter_slab, row_grad)
    act_halves = (act_own, act_other)
    sum_down = sum_rows(grad_down, 0)

    def hidden_stage(act_halves, entered, row_grad, enter_slab, down_slab):
        enter_grads, act_parts = [], []
        for e, grad in zip(entered, jnp.split(row_grad, 2)):
            gate, upper = e[:units], e[units:]
            sig = jax.nn.sigmoid(gate)
            grad_hidden = dot(down_slab, grad, over_first)
            enter_grads.append(
                jnp.concatenate(
                    [
                        (grad_hidden * upper * sig * (1.0 + gate * (1.0 - sig))).astype(BF),
                        (grad_hidden * (gate * sig)).astype(BF),
                    ]
                )
            )
            act_parts.append(dot(enter_grads[-1], enter_slab, over_first).astype(BF))
        grad_enter = dot(
            jnp.concatenate(enter_grads, axis=1), jnp.concatenate(act_halves), over_second
        ).astype(BF)
        return start_scatter(*act_parts), grad_enter

    act_sum, grad_enter = stage(
        hidden_stage, act_halves, entered, row_grad, enter_slab, down_slab
    )
    sum_enter = sum_rows(grad_enter, 1)

    def norm_stage(act_sum, unit, rate, gain, grad_low, hidden, down_slab):
        got = scatter_first(act_sum)
        grad_act_two = scatter_last(act_sum, got, scatter_second(scatter_between(act_sum, got)))
        grad_norm = norm_back(grad_act_two, unit, rate, gain)
        return (
            grad_low.astype(F32) + grad_norm,
            jnp.sum(grad_act_two * unit, axis=0),
            jnp.sum(grad_act_two, axis=0),
            start_scatter(*[dot(h, down_slab, over_first).astype(BF) for h in hidden]),
        )

    grad_middle, grad_gain_two, grad_shift_two, mixed_sum = stage(
        norm_stage, act_sum, unit_two, rate_two, gain_two, grad_low, hidden, down_slab
    )


    def branch_stage(branch, sum_down):
        return gather_own(branch), sum_down.astype(F32)

    branch_own, out_down = stage(branch_stage, grad_middle.astype(BF), sum_down)
    branch_halves = (branch_own, swap(branch_own, 1))
    attn_own_grad = dot(branch_own, w_out_own, NT).astype(BF)
    grad_w_out_own = dot(attn_halves[0], branch_own, TN)

    def back_stage(
        branch_other, own_grad, w_out_own, first, q, k, v, attn_low, logs, tables, act_one, mixed_sum
    ):
        grad_attn = to_absolute(own_grad, dot(branch_other, w_out_own, NT).astype(BF))
        grad_proj = attend_back(first, q, k, v, attn_low, grad_attn, logs, tables)
        return grad_proj, dot(act_one, grad_proj, TN).astype(BF), scatter_first(mixed_sum)

    grad_proj, grad_w_qkv, mixed_got = stage(
        back_stage,
        after(branch_halves[1], grad_w_out_own),
        attn_own_grad,
        w_out_own,
        first,
        q,
        k,
        v,
        attn_low,
        logs,
        tables,
        act_one,
        mixed_sum,
    )
    grad_proj, grad_w_qkv = after((grad_proj, grad_w_qkv), sum_enter)
    sum_qkv = sum_rows(grad_w_qkv, 0)

    branch_other = after(branch_halves[1], grad_w_qkv)
    grad_w_out = (grad_w_out_own + dot(attn_halves[1], branch_other, TN)).astype(BF)
    if fast_out:
        sum_w_out = sum_rows(grad_w_out, 0)
    else:
        spread_out = lax.dynamic_update_index_in_dim(
            jnp.zeros((per, wide_n, HEAD_DIM, width), BF),
            grad_w_out.reshape(per, HEAD_DIM, width),
            me,
            1,
        )
        sum_w_out = lax.psum_scatter(
            spread_out.reshape(width, width), ALL, scatter_dimension=0, tiled=True
        )

    def last_stage(
        grad_proj, w_qkv_own, own, other, stats, gain, grad_middle, grad_gain_two, grad_shift_two,
        mixed_sum, mixed_got, middle,
    ):
        part_other, *sums_other = unproject(grad_proj, other, stats, w_qkv_own, 1)
        part_own, *sums_own = unproject(grad_proj, own, stats, w_qkv_own, 0)
        total = start_scatter(part_own, part_other)
        got = scatter_first(total)
        sums_own, sums_other, got, mixed_got = after((sums_own, sums_other, got, mixed_got))
        passed = scatter_second(scatter_between(total, got))
        total, got = after((total, got), *passed)
        grad_gain, grad_shift, grad_bias = (a + b for a, b in zip(sums_own, sums_other))
        full_bias = lax.dynamic_update_index_in_dim(
            jnp.zeros((3, per, wide_n, HEAD_DIM), F32),
            grad_bias.reshape(3, per, HEAD_DIM),
            me,
            2,
        )
        small = jnp.concatenate(
            [
                full_bias.reshape(devices, bias_slab),
                grad_gain.reshape(devices, slab),
                grad_shift.reshape(devices, slab),
                grad_gain_two.reshape(devices, slab),
                grad_shift_two.reshape(devices, slab),
            ],
            axis=1,
        )
        small = small.reshape(rows_n, wide_n, -1).transpose(1, 0, 2)
        sums = halve(small.reshape(wide_n, -1), "wide").reshape(rows_n, -1)
        rate = stats[:local, 1:2]
        unit = (own[:local].astype(F32) - stats[:local, 0:1]) * rate
        grad_act_one = scatter_last(total, got, passed)
        mixed_passed = scatter_second(scatter_between(mixed_sum, mixed_got))
        if passed:
            mixed_passed = after(mixed_passed, *passed)
        mixed = scatter_last(mixed_sum, mixed_got, mixed_passed)
        return (
            (grad_middle + norm_back(grad_act_one, unit, rate, gain))[None],
            sums,
            (middle + mixed).astype(BF)[None],
        )

    grad_tokens, sums, result = stage(
        last_stage,
        after(grad_proj, grad_w_qkv, grad_w_out),
        w_qkv_own,
        own,
        other,
        stats,
        gain_one,
        grad_middle,
        grad_gain_two,
        grad_shift_two,
        mixed_sum,
        mixed_got,
        middle,
    )
    sum_enter = after(sum_enter, sums)
    out_gate, out_up = sum_enter[:units].T.astype(F32), sum_enter[units:].T.astype(F32)
    out_w_out = sum_w_out.astype(F32)
    part_qkv = lax.all_to_all(
        after(sum_qkv, sums).reshape(wide_n, slab, 3 * span), "wide", 0, 0, tiled=True
    )
    sums = halve(after(sums, sum_qkv), "rows")
    out_qkv = regroup_back(part_qkv[None])
    out_bias = sums[:bias_slab]
    small_outs = [
        sums[bias_slab + i * slab : bias_slab + (i + 1) * slab] for i in range(4)
    ]
    return (
        result,
        grad_tokens,
        out_qkv,
        out_bias,
        out_w_out,
        *small_outs,
        out_gate,
        out_up,
        out_down,
    )


def solution(mesh):
    by_token = P("rows", "wide", None)
    by_both = P(("rows", "wide"), None)
    vector = P(("rows", "wide"))
    by_slab = P("rows", "wide")
    in_specs = (
        by_token, P("rows", "wide"), by_both, vector, by_both, vector, vector, vector, vector,
        by_slab, by_slab, by_slab, by_token,
    )
    out_specs = (
        by_token, by_token, by_both, vector, by_both, vector, vector, vector, vector,
        by_slab, by_slab, by_slab,
    )
    return jax.shard_map(shards, mesh=mesh, in_specs=in_specs, out_specs=out_specs, check_vma=False)
```
